32 devices in a mesh: gx: 4 (over y, core), gy: 8 (over z, x).
Axes of the slice: x: 2, y: 2, z: 4, core: 2. Of those that a mesh axis runs over, the one named last changes fastest.
Arguments:
- elem_volume: float32 [73728], P(('gx', 'gy')), may hold values from 0.5 to 1.5
- elem_velocity: float32 [3, 73728], P(None, ('gx', 'gy')), may hold values from -6 to 6
- elem_energy: float32 [73728], P(('gx', 'gy')), may hold values from 0.3 to 3
- elem_mat: int32 [73728], P(('gx', 'gy')), may hold values from 0 to 7
- elem_dest: int32 [576], P(('gx', 'gy')), may hold values from 0 to 31, as said below
- tile_slot: int32 [4096], P(('gx', 'gy')), may hold values from 0 to 63, as said below
- tile_cell: int32 [4096], P(('gx', 'gy')), may hold values from 0 to 1023
- tile_weight: bfloat16 [4096, 128, 128], P(('gx', 'gy')), may hold values from 0.00390625 to 0.01171875
- tile_count: int32 [32], P(('gx', 'gy')), may hold values from 32 to 128, as said below
- cell_state: float32 [12, 256, 16384], P(None, 'gx', 'gy'), may hold values from -4 to 4, as said below
- mat_props: float32 [2, 8], replicated, may hold values from 0.5 to 4
Outputs:
- remapped: float32 [12, 256, 16384], P(None, 'gx', 'gy')
- elem_pressure: bfloat16 [73728], P(('gx', 'gy'))
The draws below stay inside these ranges and needn't reach their ends.
Inputs may be any that keep to these rules, and one draw needn't show every extreme that they name: `elem_dest`: each device sends exactly 2 of its blocks to each of the nine devices at offsets -1, 0, +1 along gx and along gy, wrapping at the ends, itself included. `tile_slot`: A value is source * 2 + rank of a block that was sent to this device; every block sent to a device is named by some tile below its count. `tile_count`: some device has all 128 tiles counted. `cell_state`: the volume and energy rows lie between 0.1 and 1; the three momentum rows are signed.
All inputs are finite; a program needn't handle non-finite values.
Results may differ from the reference program's by a relative error of at most 0.0024.
Values may be sent and summed in bfloat16 or wider, within the bound.
No kernel may reach another device: no remote copies, remote signals or barrier semaphores. Data moves between devices by JAX's collectives and lax.ppermute only.
A program may use at most 192 MiB of HBM per device.

```python
import math
import jax
import jax.numpy as jnp
from jax import lax

MAT = 8
P_SIZE = 12
NZ = 64
BLK = 128
NXD = 64
NYD = 32
CAP = 2
TCAP = 128
GRID_X = 4
GRID_Y = 8
EB_DEV = 18
EBLOCKS = 576
ELEMS = 73728
NX = 256
NY = 256
CB_DEV = 1024
TILES = 4096
LOW = 32


def neighbour_index(pos_x, pos_y, which, sign):
    step_x = which // 3 - 1
    step_y = which % 3 - 1
    return (pos_x + sign * step_x) % GRID_X * GRID_Y + (pos_y + sign * step_y) % GRID_Y


def draw_elem_dest(key, part):
    nodes = GRID_X * GRID_Y
    keys = jax.random.split(key, nodes)

    def single(sub, device):
        order = jax.random.permutation(sub, EB_DEV)
        return neighbour_index(device // GRID_Y, device % GRID_Y, order // CAP, 1)
    return jax.vmap(single)(keys, jnp.arange(nodes, dtype=jnp.int32)).reshape(-1).astype(jnp.int32)


def draw_tile_slot(key, part):
    nodes = GRID_X * GRID_Y
    keys = jax.random.split(key, nodes)

    def single(sub, device):
        first, second, third = jax.random.split(sub, 3)
        places = jnp.arange(TCAP, dtype=jnp.int32)
        extra_which = jax.random.randint(first, (TCAP,), 0, 9)
        extra_rank = jax.random.randint(second, (TCAP,), 0, CAP)
        which = jnp.where(places < 9 * CAP, places // CAP, extra_which)
        rank = jnp.where(places < 9 * CAP, places % CAP, extra_rank)
        source = neighbour_index(device // GRID_Y, device % GRID_Y, which, -1)
        slots = source * CAP + rank
        head = jax.random.permutation(third, slots[:LOW])
        return jnp.concatenate([head, slots[LOW:]])
    return jax.vmap(single)(keys, jnp.arange(nodes, dtype=jnp.int32)).reshape(-1).astype(jnp.int32)


def draw_tile_count(key, part):
    nodes = GRID_X * GRID_Y
    first, second = jax.random.split(key)
    counts = jax.random.randint(first, (nodes,), LOW, TCAP + 1)
    busiest = jax.random.randint(second, (), 0, nodes)
    return jnp.where(jnp.arange(nodes) == busiest, TCAP, counts).astype(jnp.int32)


def draw_cell_state(key, part):
    count = MAT + 4
    fresh_key = jax.random.fold_in(key, 17)
    unit = jax.random.uniform(fresh_key, (count, NX, NY * NZ), jnp.float32)
    quantity = jnp.arange(count, dtype=jnp.int32)
    moving = (quantity >= MAT) & (quantity < MAT + 3)
    level = 0.1 + 0.9 * unit
    drift = -4.0 + 8.0 * unit
    return jnp.where(moving[:, None, None], drift, level).astype(jnp.float32)


def plant(values, rng, low, largest):
    longest = values.shape.index(max(values.shape))
    spots = []
    for shift in (0, 1):
        where = [jax.random.randint(jax.random.fold_in(rng, axis), (), 0, length) for axis, length in enumerate(values.shape)]
        where[longest] = (where[longest] + shift) % values.shape[longest]
        spots.append(tuple(where))
    return values.at[spots[0]].set(low).at[spots[1]].set(largest)


def shard_levels(rng, dims, cuts, least, top_value):
    level = 1.0
    for dim, shards_of in cuts:
        draws = jax.random.uniform(jax.random.fold_in(jax.random.fold_in(rng, 6), dim), (shards_of,), jnp.float32, least / len(cuts), top_value / len(cuts))
        level = level * jnp.repeat(jnp.exp(draws), dims[dim] // shards_of).reshape((-1,) + (1,) * (len(dims) - 1 - dim))
    return level


def noise(rng, shape, scale, bound, cuts=(), held_as=jnp.bfloat16):
    array = jax.random.normal(rng, shape, jnp.float32) * scale
    if len(cuts) > 0:
        array = shard_levels(rng, shape, cuts, -0.22, 0.18) * array
    return jnp.clip(array, min=-bound, max=bound).astype(held_as)


def setup_inputs(seed: int = 0) -> dict:
    seeds = jax.random.split(jax.random.key(seed), 12)
    return {
        "elem_volume": jnp.clip(0.5 + 1.0 * jax.random.uniform(seeds[0], (ELEMS,), jnp.float32) ** shard_levels(seeds[0], (ELEMS,), ((0, 32),), -0.2, 0.2), 0.5, 1.5),
        "elem_velocity": noise(seeds[1], (3, ELEMS), 1.5, 6.0, ((1, 32),), jnp.float32),
        "elem_energy": jnp.clip(jnp.exp(math.log(3.0) - 2.3025851 * jax.random.uniform(seeds[2], (ELEMS,), jnp.float32) ** shard_levels(seeds[2], (ELEMS,), ((0, 32),), -0.2, 0.2)), 0.3, 3.0),
        "elem_mat": plant(jax.random.randint(seeds[3], (ELEMS,), 0, MAT), jax.random.fold_in(seeds[3], 1), 0, MAT - 1).astype(jnp.int32),
        "elem_dest": draw_elem_dest(jax.random.fold_in(seeds[11], 71), 0),
        "tile_slot": draw_tile_slot(jax.random.fold_in(seeds[11], 71), 0),
        "tile_cell": plant(jax.random.randint(seeds[6], (TILES,), 0, CB_DEV), jax.random.fold_in(seeds[6], 1), 0, CB_DEV - 1).astype(jnp.int32),
        "tile_weight": jnp.clip(0.00390625 + 0.0078125 * jax.random.uniform(seeds[7], (TILES, BLK, BLK), jnp.float32) ** shard_levels(seeds[7], (TILES, BLK, BLK), ((0, 32),), -0.2, 0.2), 0.00390625, 0.01171875).astype(jnp.bfloat16),
        "tile_count": draw_tile_count(jax.random.fold_in(seeds[11], 71), 0),
        "cell_state": draw_cell_state(jax.random.fold_in(seeds[11], 71), 0),
        "mat_props": jnp.clip(jnp.exp(jax.random.uniform(seeds[10], (2, MAT), jnp.float32, math.log(0.5), math.log(4.0))), 0.5, 4.0),
    }


time_step = 0.8


def face_flux(q_lo, q_hi, u_lo, u_hi):
    speed = 0.5 * (u_lo + u_hi)
    return 0.5 * (speed * (q_lo + q_hi) - jnp.abs(speed) * (q_hi - q_lo))


def reference(elem_volume, elem_velocity, elem_energy, elem_mat, elem_dest, tile_slot, tile_cell, tile_weight, tile_count, cell_state, mat_props):
    nodes = GRID_X * GRID_Y
    density = mat_props[0]
    modulus = mat_props[1]
    onehot = (elem_mat[None, :] == jnp.arange(MAT, dtype=jnp.int32)[:, None]).astype(jnp.float32)
    mass_e = elem_volume * jnp.sum(onehot * density[:, None], axis=0)
    rows = jnp.concatenate([onehot * elem_volume[None, :], mass_e[None, :] * elem_velocity, (mass_e * elem_energy)[None, :]], axis=0).astype(jnp.bfloat16)
    payload = rows.reshape(P_SIZE, EBLOCKS, BLK).transpose(1, 0, 2)

    dest_two = elem_dest.reshape(nodes, EB_DEV)
    index = jnp.arange(EB_DEV, dtype=jnp.int32)
    earlier = index[:, None] > index[None, :]
    same = dest_two[:, :, None] == dest_two[:, None, :]
    rank = jnp.sum((same & earlier[None]).astype(jnp.int32), axis=2)
    block_key = dest_two * (nodes * CAP) + jnp.arange(nodes, dtype=jnp.int32)[:, None] * CAP + rank
    block_key = block_key.reshape(-1)
    order = jnp.argsort(block_key).astype(jnp.int32)
    sorted_key = block_key[order]
    tile_key = jnp.repeat(jnp.arange(nodes, dtype=jnp.int32), TCAP) * (nodes * CAP) + tile_slot
    tile_block = order[jnp.searchsorted(sorted_key, tile_key)].astype(jnp.int32)

    valid = (jnp.arange(TCAP, dtype=jnp.int32)[None, :] < tile_count[:, None]).astype(jnp.float32)
    block_two = tile_block.reshape(nodes, TCAP)
    cell_two = tile_cell.reshape(nodes, TCAP)
    weight_two = tile_weight.reshape(nodes, TCAP, BLK, BLK)

    def deposit(item):
        blocks, cells, weights, flags = item
        picked = payload[blocks].astype(jnp.float32)
        contrib = jnp.einsum('trb,tbc->trc', picked, weights.astype(jnp.float32)) * flags[:, None, None]
        return jax.ops.segment_sum(contrib, cells, num_segments=CB_DEV)

    dep_all = lax.map(deposit, (block_two, cell_two, weight_two, valid))
    dep = dep_all.reshape(GRID_X, GRID_Y, CB_DEV, P_SIZE, BLK).transpose(3, 0, 1, 2, 4)
    dep = dep.reshape(P_SIZE, GRID_X, GRID_Y, NXD, NYD, NZ).transpose(0, 1, 3, 2, 4, 5).reshape(P_SIZE, NX, NY, NZ)

    q = cell_state.reshape(P_SIZE, NX, NY, NZ) + dep
    mass = 1.0 + jnp.sum(density[:, None, None, None] * q[:MAT], axis=0)
    u_x = q[MAT] / mass
    u_y = q[MAT + 1] / mass
    qx = jnp.pad(q, ((0, 0), (1, 1), (0, 0), (0, 0)))
    vx = jnp.pad(u_x, ((1, 1), (0, 0), (0, 0)))[None]
    flux_x = face_flux(qx[:, :-1], qx[:, 1:], vx[:, :-1], vx[:, 1:])
    qy = jnp.pad(q, ((0, 0), (0, 0), (1, 1), (0, 0)))
    vy = jnp.pad(u_y, ((0, 0), (1, 1), (0, 0)))[None]
    flux_y = face_flux(qy[:, :, :-1], qy[:, :, 1:], vy[:, :, :-1], vy[:, :, 1:])
    fresh = q - time_step * (flux_x[:, 1:] - flux_x[:, :-1] + flux_y[:, :, 1:] - flux_y[:, :, :-1])
    remapped = fresh.reshape(P_SIZE, NX, NY * NZ)

    volumes = fresh[:MAT]
    pressure = jnp.sum(modulus[:, None, None, None] * volumes * (1.0 + 0.5 * volumes), axis=0) + 0.4 * fresh[P_SIZE - 1]
    pressure = pressure.astype(jnp.bfloat16)
    press_dev = pressure.reshape(GRID_X, NXD, GRID_Y, NYD, NZ).transpose(0, 2, 1, 3, 4).reshape(nodes, CB_DEV, BLK)

    def sample(item):
        cells, weights, flags, press = item
        local = press[cells].astype(jnp.float32)
        wide = weights.astype(jnp.float32)
        numer = jnp.einsum('tec,tc->te', wide, local) * flags[:, None]
        denom = jnp.sum(wide, axis=2) * flags[:, None]
        return numer, denom

    numer, denom = lax.map(sample, (cell_two, weight_two, valid, press_dev))
    numer = jax.ops.segment_sum(numer.reshape(-1, BLK), tile_block, num_segments=EBLOCKS)
    denom = jax.ops.segment_sum(denom.reshape(-1, BLK), tile_block, num_segments=EBLOCKS)
    elem_pressure = (numer / jnp.maximum(denom, 1.0)).astype(jnp.bfloat16).reshape(ELEMS)
    return remapped, elem_pressure
```

```python
import functools

import jax
import jax.numpy as jnp
from jax import lax
from jax.experimental import pallas as pl
from jax.experimental.pallas import tpu as pltpu
from jax.sharding import PartitionSpec as P

MAT = 8
NZ = 64
BLK = 128
CAP = 2
HALF = BLK // 2
PAD = 8
ROWS = 16
UNROLL = 8
MIB = 2**20

time_step = 0.8
F32 = jnp.float32
BF16 = jnp.bfloat16

SMEM = pl.BlockSpec(memory_space=pltpu.SMEM)
VMEM = pl.BlockSpec(memory_space=pltpu.VMEM)
ANY = pl.BlockSpec(memory_space=pl.ANY)


def partner(index, size, which):
    if which == 1:
        return index ^ 1
    return (index + 1 if index % 2 else index - 1) % size


def swap(value, axis, which, wrap=True):
    size = lax.axis_size(axis)
    pairs = [(i, partner(i, size, which)) for i in range(size)]
    if not wrap:
        pairs = [(i, j) for i, j in pairs if abs(i - j) == 1]
    return lax.ppermute(value, axis, pairs)


def code_of(index, mine):
    return jnp.where(index == mine, 0, jnp.where(index == (mine ^ 1), 1, 2))


def split_device(device, size):
    if size & (size - 1) == 0:
        return device >> (size.bit_length() - 1), device & (size - 1)
    return lax.div(device, size), lax.rem(device, size)


def payload_kernel(dest, props, volume, velocity, energy, mat, own, first, second, place, seen, packed, *, size_y):
    pos_x, pos_y = lax.axis_index("gx"), lax.axis_index("gy")
    n_blocks = volume.shape[0]
    kinds = mat[...]
    density = jnp.zeros(kinds.shape, F32)
    for m in range(MAT):
        density = jnp.where(kinds == m, props[0, m], density)
    mass = volume[...] * density
    heat = mass * energy[...]
    level = lax.broadcasted_iota(jnp.int32, (MAT, BLK), 0)
    for k in range(9):
        seen[k] = 0
    for b in range(n_blocks):
        at_x, at_y = split_device(dest[b], size_y)
        near = code_of(at_x, pos_x) * 3 + code_of(at_y, pos_y)
        rank = seen[near]
        seen[near] = rank + 1
        slot = near * CAP + rank
        place[b] = slot
        volumes = jnp.where(kinds[b : b + 1] == level, volume[b : b + 1, :], 0.0)
        momentum = mass[b : b + 1] * velocity[:, b * BLK : (b + 1) * BLK]
        rows = jnp.concatenate([volumes, momentum, heat[b : b + 1], jnp.zeros((4, BLK), F32)], axis=0)
        packed[slot] = rows.astype(BF16)
    for k, out in enumerate((own, first, second)):
        for s in range(3 * CAP):
            out[s] = packed[k * 3 * CAP + s]


def payload(dest, props, volume, velocity, energy, mat, size_y):
    n_blocks = volume.shape[0]
    parcel = pltpu.VMEM((3 * CAP, ROWS, BLK), BF16)
    return pl.pallas_call(
        functools.partial(payload_kernel, size_y=size_y),
        name="payload",
        out_shape=(parcel, parcel, parcel, jax.ShapeDtypeStruct((n_blocks,), jnp.int32)),
        in_specs=[SMEM, SMEM, VMEM, VMEM, VMEM, VMEM],
        out_specs=(VMEM, VMEM, VMEM, SMEM),
        scratch_shapes=[pltpu.SMEM((9,), jnp.int32), pltpu.VMEM((9 * CAP, ROWS, BLK), BF16)],
        compiler_params=pltpu.CompilerParams(vmem_limit_bytes=4 * MIB),
    )(dest, props, volume, velocity, energy, mat)


def stage_kernel(cell, state, sem):
    columns = state.shape[0] - 2
    width = state.shape[2] - 2 * PAD
    copies = [
        pltpu.make_async_copy(
            cell.at[:, :, pl.ds(j * BLK, BLK)], state.at[j + 1, :, pl.ds(PAD, width)], sem.at[j]
        )
        for j in range(columns)
    ]
    for copy in copies:
        copy.start()
    for copy in copies:
        copy.wait()


def stage(cell):
    count, width, lanes = cell.shape
    columns = lanes // BLK
    return pl.pallas_call(
        stage_kernel,
        name="stage",
        out_shape=pltpu.VMEM((columns + 2, count, width + 2 * PAD, BLK), F32),
        in_specs=[ANY],
        out_specs=VMEM,
        scratch_shapes=[pltpu.SemaphoreType.DMA((columns,))],
        compiler_params=pltpu.CompilerParams(vmem_limit_bytes=2 * MIB),
        cost_estimate=pl.CostEstimate(flops=0, bytes_accessed=2 * cell.size * 4, transcendentals=0),
    )(cell)


def local_slot(slot, pos_x, pos_y, size_y):
    at_x, at_y = split_device(slot >> 1, size_y)
    return code_of(at_y, pos_y) * (3 * CAP) + code_of(at_x, pos_x) * CAP + (slot & 1)


def low_lanes():
    return lax.broadcasted_iota(jnp.int32, (1, BLK), 1) < HALF


def turn(value):
    return pltpu.roll(value, HALF, value.ndim - 1)


def deposit_kernel(
    tile_slot, tile_cell, tile_count, own, first, second, north, south, weight, state_in,
    state, edge_x1, edge_x2, edge_y1, edge_y2, rows, *, size_y
):
    pos_x, pos_y = lax.axis_index("gx"), lax.axis_index("gy")
    n_tiles = weight.shape[0]
    columns, count, tall = state.shape[0] - 2, state.shape[1], state.shape[2]
    flat = state.reshape(columns + 2, count * tall, BLK)
    for k, part in enumerate((own, first, second)):
        for r in range(CAP):
            rows[k * CAP + r] = part[r]
    for k, part in enumerate((north, south)):
        for r in range(3 * CAP):
            rows[(k + 1) * 3 * CAP + r] = part[r]
    counted = tile_count[0]

    def add_tiles(step, carry):
        for k in range(UNROLL):
            t = step * UNROLL + k
            slot = local_slot(tile_slot[t], pos_x, pos_y, size_y)
            contrib = jnp.dot(rows[slot], weight[t], preferred_element_type=F32)[:count]
            contrib = jnp.where(t < counted, contrib, 0.0)
            x, j = split_device(tile_cell[t], columns)
            at = pl.ds(x + PAD, count, stride=tall)
            flat[j + 1, at, :] = flat[j + 1, at, :] + contrib
        return carry

    lax.fori_loop(0, n_tiles // UNROLL, add_tiles, 0)

    even_x, even_y = (pos_x & 1) == 0, (pos_y & 1) == 0
    top, bottom = tall - PAD - 1, PAD
    line = state.reshape((columns + 2) * count * tall, BLK)
    for edge, row in (
        (edge_x1, jnp.where(even_x, top, bottom)),
        (edge_x2, jnp.where(even_x, bottom, top)),
    ):
        for q in range(count):
            at = pl.ds(count * tall + q * tall + row, columns, stride=count * tall)
            edge[q * columns : (q + 1) * columns, :] = line[at, :].astype(BF16)
    low = low_lanes()
    width = tall - 2 * PAD
    for edge, upper in ((edge_y1, even_y), (edge_y2, jnp.logical_not(even_y))):
        column = jnp.where(upper, columns, 1)
        for q in range(count // 2):
            for i in range(width // ROWS):
                here = slice(PAD + i * ROWS, PAD + (i + 1) * ROWS)
                a = state[column, q, here, :]
                b = state[column, q + count // 2, here, :]
                both = jnp.where(low, jnp.where(upper, turn(a), a), jnp.where(upper, b, turn(b)))
                edge[q * width + i * ROWS : q * width + (i + 1) * ROWS, :] = both.astype(BF16)


def deposit(tile_slot, tile_cell, tile_count, parts, weight, state, size_y):
    columns, count, tall = state.shape[0] - 2, state.shape[1], state.shape[2]
    edge_x = pltpu.VMEM((count * columns, BLK), BF16)
    edge_y = pltpu.VMEM((count // 2 * (tall - 2 * PAD), BLK), BF16)
    return pl.pallas_call(
        functools.partial(deposit_kernel, size_y=size_y),
        name="deposit",
        out_shape=(pltpu.VMEM(state.shape, F32), edge_x, edge_x, edge_y, edge_y),
        in_specs=[SMEM] * 3 + [VMEM] * 7,
        out_specs=(VMEM,) * 5,
        input_output_aliases={9: 0},
        scratch_shapes=[pltpu.VMEM((9 * CAP, ROWS, BLK), BF16)],
        compiler_params=pltpu.CompilerParams(vmem_limit_bytes=4 * MIB),
    )(tile_slot, tile_cell, tile_count, *parts, weight, state)


def speeds_at(props, state, speed, j, here, parts):
    mass = 1.0 + props[0, 0] * state[j, 0, here, :]
    for m in range(1, MAT):
        mass = mass + props[0, m] * state[j, m, here, :]
    share = 1.0 / mass
    for k in parts:
        speed[j, k, here, :] = state[j, MAT + k, here, :] * share


def remap_at(props, state, speed, press, fresh, j, first_row):
    count = state.shape[1]
    low = low_lanes()
    here = slice(first_row, first_row + 8)
    before = slice(first_row - 1, first_row + 7)
    after = slice(first_row + 1, first_row + 9)
    inside = slice(first_row - PAD, first_row - PAD + 8)
    scale = 0.5 * time_step
    ux = speed[j, 0, here, :]
    lower = scale * (speed[j, 0, before, :] + ux)
    upper = scale * (ux + speed[j, 0, after, :])
    uy = speed[j, 1, here, :]
    left = scale * (turn(jnp.where(low, uy, speed[j - 1, 1, here, :])) + uy)
    right = scale * (uy + turn(jnp.where(low, speed[j + 1, 1, here, :], uy)))
    keep = 1.0 - (
        jnp.maximum(upper, 0.0) + jnp.maximum(-lower, 0.0) + jnp.maximum(right, 0.0) + jnp.maximum(-left, 0.0)
    )
    take_before = jnp.maximum(lower, 0.0)
    take_after = jnp.maximum(-upper, 0.0)
    take_left = turn(jnp.maximum(left, 0.0))
    take_right = turn(jnp.maximum(-right, 0.0))
    same = jnp.where(low, take_left, take_right)
    other = jnp.where(low, take_right, take_left)
    total = None
    for q in range(count):
        mid = state[j, q, here, :]
        beside = jnp.where(low, state[j + 1, q, here, :], state[j - 1, q, here, :])
        value = keep * mid + take_before * state[j, q, before, :]
        value = value + take_after * state[j, q, after, :]
        value = value + turn(same * mid + other * beside)
        fresh[j - 1, q, inside, :] = value
        if q < MAT:
            term = value * (props[1, q] + (0.5 * props[1, q]) * value)
            total = term if total is None else total + term
        elif q == count - 1:
            total = total + 0.4 * value
    press[j - 1, inside, :] = total


def inner_kernel(props, state, remapped, press, speed, fresh, sem):
    columns, tall = state.shape[0] - 2, state.shape[2]
    tiles = (tall - 2 * PAD) // 8

    def speeds(j, carry):
        for i in range(tiles):
            speeds_at(props, state, speed, j, slice(PAD + 8 * i, PAD + 8 * i + 8), (0, 1))
        return carry

    lax.fori_loop(1, columns + 1, speeds, 0)

    def write(j):
        rows = pl.ds(8, 8 * (tiles - 2))
        lanes = pl.ds(pl.multiple_of((j - 1) * BLK, BLK), BLK)
        return pltpu.make_async_copy(fresh.at[j - 1, :, rows], remapped.at[:, rows, lanes], sem.at[j - 1])

    def remap(j, carry):
        for i in range(1, tiles - 1):
            remap_at(props, state, speed, press, fresh, j, PAD + 8 * i)
        write(j).start()
        return carry

    lax.fori_loop(2, columns, remap, 0)

    def finish(j, carry):
        write(j).wait()
        return carry

    lax.fori_loop(2, columns, finish, 0)


def inner(props, state, width):
    columns, count, tall = state.shape[0] - 2, state.shape[1], state.shape[2]
    return pl.pallas_call(
        inner_kernel,
        name="inner",
        out_shape=(
            jax.ShapeDtypeStruct((count, width, columns * BLK), F32),
            pltpu.VMEM((columns, width, BLK), F32),
            pltpu.VMEM((columns + 2, 2, tall, BLK), F32),
        ),
        in_specs=[SMEM, VMEM],
        out_specs=(ANY, VMEM, VMEM),
        scratch_shapes=[pltpu.VMEM((columns, count, width, BLK), F32), pltpu.SemaphoreType.DMA((columns,))],
        compiler_params=pltpu.CompilerParams(vmem_limit_bytes=10 * MIB),
        cost_estimate=pl.CostEstimate(flops=20 * state.size, bytes_accessed=2 * state.size * 4, transcendentals=0),
    )(props, state)


def outer_kernel(
    props, tile_slot, tile_cell, tile_count, edge_x1, edge_x2, edge_y1, edge_y2, weight, state_in, speed_in, press_in,
    remapped_in, remapped, state, speed, press, own, first, second, fresh, sums, sem, *, size_y
):
    pos_x, pos_y = lax.axis_index("gx"), lax.axis_index("gy")
    n_tiles = weight.shape[0]
    columns, count, tall = state.shape[0] - 2, state.shape[1], state.shape[2]
    width = tall - 2 * PAD
    tiles = width // 8
    even_x, even_y = (pos_x & 1) == 0, (pos_y & 1) == 0
    line = state.reshape((columns + 2) * count * tall, BLK)
    above, below = tall - PAD, PAD - 1
    for edge, row in (
        (edge_x1, jnp.where(even_x, above, below)),
        (edge_x2, jnp.where(even_x, below, above)),
    ):
        for q in range(count):
            at = pl.ds(count * tall + q * tall + row, columns, stride=count * tall)
            line[at, :] = edge[q * columns : (q + 1) * columns, :].astype(F32)
    low = low_lanes()
    for edge, column in (
        (edge_y1, jnp.where(even_y, columns + 1, 0)),
        (edge_y2, jnp.where(even_y, 0, columns + 1)),
    ):
        for q in range(count // 2):
            for i in range(width // ROWS):
                here = slice(PAD + i * ROWS, PAD + (i + 1) * ROWS)
                both = edge[q * width + i * ROWS : q * width + (i + 1) * ROWS, :].astype(F32)
                turned = turn(both)
                state[column, q, here, :] = jnp.where(low, both, turned)
                state[column, q + count // 2, here, :] = jnp.where(low, turned, both)

    def side_speeds(j, carry):
        speeds_at(props, state, speed, j, slice(0, PAD), (0,))
        speeds_at(props, state, speed, j, slice(tall - PAD, tall), (0,))
        return carry

    lax.fori_loop(1, columns + 1, side_speeds, 0)
    for j in (0, columns + 1):
        for i in range(tiles):
            speeds_at(props, state, speed, j, slice(PAD + 8 * i, PAD + 8 * i + 8), (1,))

    def write(j, first_row, rows, which):
        rows = pl.ds(first_row, rows)
        lanes = pl.ds(pl.multiple_of((j - 1) * BLK, BLK), BLK)
        return pltpu.make_async_copy(fresh.at[j - 1, :, rows], remapped.at[:, rows, lanes], sem.at[which, j - 1])

    def sides(j, carry):
        for which, i in enumerate((0, tiles - 1)):
            remap_at(props, state, speed, press, fresh, j, PAD + 8 * i)
            write(j, 8 * i, 8, which).start()
        return carry

    lax.fori_loop(1, columns + 1, sides, 0)
    for j in (1, columns):
        for i in range(1, tiles - 1):
            remap_at(props, state, speed, press, fresh, j, PAD + 8 * i)
        write(j, 8, 8 * (tiles - 2), 2).start()

    sums[...] = jnp.zeros(sums.shape, F32)
    counted = tile_count[0]
    head = lax.broadcasted_iota(jnp.int32, (ROWS, BLK), 0) == 0

    def sample(step, carry):
        for k in range(UNROLL):
            t = step * UNROLL + k
            slot = local_slot(tile_slot[t], pos_x, pos_y, size_y)
            x, j = split_device(tile_cell[t], columns)
            probe = jnp.where(head, press[j, pl.ds(x, 1), :], 1.0).astype(BF16)
            both = lax.dot_general(probe, weight[t], (((1,), (1,)), ((), ())), preferred_element_type=F32)[:8]
            sums[slot] = sums[slot] + jnp.where(t < counted, both, 0.0)
        return carry

    lax.fori_loop(0, n_tiles // UNROLL, sample, 0)
    table = sums.reshape(sums.shape[0] * 8, BLK)
    for k, out in enumerate((own, first, second)):
        top = table[pl.ds(k * 3 * CAP * 8, 3 * CAP, stride=8), :]
        under = table[pl.ds(k * 3 * CAP * 8 + 1, 3 * CAP, stride=8), :]
        out[...] = top / jnp.maximum(under, 1.0)

    def finish(j, carry):
        write(j, 0, 8, 0).wait()
        write(j, 8 * (tiles - 1), 8, 1).wait()
        return carry

    lax.fori_loop(1, columns + 1, finish, 0)
    for j in (1, columns):
        write(j, 8, 8 * (tiles - 2), 2).wait()


def outer(props, tile_slot, tile_cell, tile_count, edges, weight, state, speed, press, remapped, size_y):
    columns, count = state.shape[0] - 2, state.shape[1]
    answer = pltpu.VMEM((3 * CAP, BLK), F32)
    outs = pl.pallas_call(
        functools.partial(outer_kernel, size_y=size_y),
        name="outer",
        out_shape=(
            jax.ShapeDtypeStruct(remapped.shape, F32),
            pltpu.VMEM(state.shape, F32),
            pltpu.VMEM(speed.shape, F32),
            pltpu.VMEM(press.shape, F32),
            answer,
            answer,
            answer,
        ),
        in_specs=[SMEM] * 4 + [VMEM] * 8 + [ANY],
        out_specs=(ANY,) + (VMEM,) * 6,
        input_output_aliases={12: 0, 9: 1, 10: 2, 11: 3},
        scratch_shapes=[
            pltpu.VMEM((columns, count, remapped.shape[1], BLK), F32),
            pltpu.VMEM((9 * CAP, 8, BLK), F32),
            pltpu.SemaphoreType.DMA((3, columns)),
        ],
        compiler_params=pltpu.CompilerParams(vmem_limit_bytes=10 * MIB),
    )(props, tile_slot, tile_cell, tile_count, *edges, weight, state, speed, press, remapped)
    return outs[0], outs[4], outs[5], outs[6]


def pick_kernel(place, own, first, second, out, table):
    for k, part in enumerate((own, first, second)):
        table[k * 3 * CAP : (k + 1) * 3 * CAP, :] = part[...]
    for b in range(out.shape[0]):
        out[b : b + 1, :] = table[pl.ds(place[b], 1), :]


def pick(place, own, first, second):
    return pl.pallas_call(
        pick_kernel,
        name="pick",
        out_shape=pltpu.VMEM((place.shape[0], BLK), F32),
        in_specs=[SMEM, VMEM, VMEM, VMEM],
        out_specs=VMEM,
        scratch_shapes=[pltpu.VMEM((9 * CAP, BLK), F32)],
        compiler_params=pltpu.CompilerParams(vmem_limit_bytes=2 * MIB),
    )(place, own, first, second)


def per_device(
    elem_volume,
    elem_velocity,
    elem_energy,
    elem_mat,
    elem_dest,
    tile_slot,
    tile_cell,
    tile_weight,
    tile_count,
    cell_state,
    mat_props,
):
    size_y = lax.axis_size("gy")
    n_blocks = elem_dest.shape[0]
    shape = (n_blocks, BLK)
    own, first, second, place = payload(
        elem_dest,
        mat_props,
        elem_volume.reshape(shape),
        elem_velocity,
        elem_energy.reshape(shape),
        elem_mat.reshape(shape),
        size_y,
    )
    state = stage(cell_state)
    weight = pltpu.with_memory_space_constraint(tile_weight, pltpu.VMEM)

    first = swap(first, "gx", 1)
    second = swap(second, "gx", 2)

    def along_y(which):
        rows = slice(which * CAP, (which + 1) * CAP)
        return jnp.concatenate([own[rows], first[rows], second[rows]], axis=0)

    north = swap(along_y(1), "gy", 1)
    south = swap(along_y(2), "gy", 2)
    state, *edges = deposit(
        tile_slot, tile_cell, tile_count, (own, first, second, north, south), weight, state, size_y
    )
    edges = (
        swap(edges[0], "gx", 1, wrap=False),
        swap(edges[1], "gx", 2, wrap=False),
        swap(edges[2], "gy", 1, wrap=False),
        swap(edges[3], "gy", 2, wrap=False),
    )
    remapped, press, speed = inner(mat_props, state, cell_state.shape[1])
    remapped, own, first, second = outer(
        mat_props, tile_slot, tile_cell, tile_count, edges, weight, state, speed, press, remapped, size_y
    )
    first = swap(first, "gy", 1)
    second = swap(second, "gy", 2)

    def along_x(which):
        rows = slice(which * CAP, (which + 1) * CAP)
        return jnp.concatenate([own[rows], first[rows], second[rows]], axis=0)

    back = pick(place, along_x(0), swap(along_x(1), "gx", 1), swap(along_x(2), "gx", 2))
    return remapped, back.astype(BF16).reshape(n_blocks * BLK)


def solution(mesh):
    placed = (
        P(("gx", "gy")),
        P(None, ("gx", "gy")),
        P(("gx", "gy")),
        P(("gx", "gy")),
        P(("gx", "gy")),
        P(("gx", "gy")),
        P(("gx", "gy")),
        P(("gx", "gy"), None, None),
        P(("gx", "gy")),
        P(None, "gx", "gy"),
        P(),
    )
    return jax.shard_map(
        per_device,
        mesh=mesh,
        in_specs=placed,
        out_specs=(P(None, "gx", "gy"), P(("gx", "gy"))),
        check_vma=False,
    )
```

```python
import functools

import jax
import jax.numpy as jnp
from jax import lax
from jax.experimental import pallas as pl
from jax.experimental.pallas import tpu as pltpu
from jax.sharding import PartitionSpec as P

MAT = 8
NZ = 64
BLK = 128
CAP = 2
HALF = BLK // 2
PAD = 8
ROWS = 16
UNROLL = 32
MIB = 2**20

time_step = 0.8
F32 = jnp.float32
BF16 = jnp.bfloat16

SMEM = pl.BlockSpec(memory_space=pltpu.SMEM)
VMEM = pl.BlockSpec(memory_space=pltpu.VMEM)
ANY = pl.BlockSpec(memory_space=pl.ANY)


def partner(index, size, which):
    if which == 1:
        return index ^ 1
    return (index + 1 if index % 2 else index - 1) % size


def swap(value, axis, which, wrap=True):
    size = lax.axis_size(axis)
    pairs = [(i, partner(i, size, which)) for i in range(size)]
    if not wrap:
        pairs = [(i, j) for i, j in pairs if abs(i - j) == 1]
    return lax.ppermute(value, axis, pairs)


def code_of(index, mine):
    return jnp.where(index == mine, 0, jnp.where(index == (mine ^ 1), 1, 2))


def split_device(device, size):
    if size & (size - 1) == 0:
        return device >> (size.bit_length() - 1), device & (size - 1)
    return lax.div(device, size), lax.rem(device, size)


def in_hbm(value):
    return pltpu.with_memory_space_constraint(value, pltpu.HBM)


def payload_kernel(
    dest_hbm, props_hbm, volume_hbm, velocity_hbm, energy_hbm, mat_hbm, own, first, second, place,
    dest, props, volume, velocity, energy, mat, seen, packed, sem, *, size_y
):
    moves = (
        (dest_hbm, dest), (props_hbm, props), (mat_hbm, mat),
        (volume_hbm, volume), (velocity_hbm, velocity), (energy_hbm, energy),
    )
    copies = [pltpu.make_async_copy(src, dst, sem.at[k]) for k, (src, dst) in enumerate(moves)]
    for copy in copies:
        copy.start()
    for copy in copies:
        copy.wait()
    pos_x, pos_y = lax.axis_index("gx"), lax.axis_index("gy")
    n_blocks = volume.shape[0]
    kinds = mat[...]
    density = jnp.zeros(kinds.shape, F32)
    for m in range(MAT):
        density = jnp.where(kinds == m, props[0, m], density)
    mass = volume[...] * density
    heat = mass * energy[...]
    level = lax.broadcasted_iota(jnp.int32, (MAT, BLK), 0)
    for k in range(9):
        seen[k] = 0
    for b in range(n_blocks):
        at_x, at_y = split_device(dest[b], size_y)
        near = code_of(at_x, pos_x) * 3 + code_of(at_y, pos_y)
        rank = seen[near]
        seen[near] = rank + 1
        slot = near * CAP + rank
        place[b] = slot
        volumes = jnp.where(kinds[b : b + 1] == level, volume[b : b + 1, :], 0.0)
        momentum = mass[b : b + 1] * velocity[:, b * BLK : (b + 1) * BLK]
        rows = jnp.concatenate([volumes, momentum, heat[b : b + 1], jnp.zeros((4, BLK), F32)], axis=0)
        packed[slot] = rows.astype(BF16)
    for k, out in enumerate((own, first, second)):
        for s in range(3 * CAP):
            out[s] = packed[k * 3 * CAP + s]


def payload(dest, props, volume, velocity, energy, mat, size_y):
    n_blocks = volume.shape[0]
    parcel = pltpu.VMEM((3 * CAP, ROWS, BLK), BF16)
    return pl.pallas_call(
        functools.partial(payload_kernel, size_y=size_y),
        name="payload",
        out_shape=(parcel, parcel, parcel, jax.ShapeDtypeStruct((n_blocks,), jnp.int32)),
        in_specs=[ANY] * 6,
        out_specs=(VMEM, VMEM, VMEM, SMEM),
        scratch_shapes=[
            pltpu.SMEM(dest.shape, jnp.int32),
            pltpu.SMEM(props.shape, F32),
            pltpu.VMEM(volume.shape, F32),
            pltpu.VMEM(velocity.shape, F32),
            pltpu.VMEM(energy.shape, F32),
            pltpu.VMEM(mat.shape, jnp.int32),
            pltpu.SMEM((9,), jnp.int32),
            pltpu.VMEM((9 * CAP, ROWS, BLK), BF16),
            pltpu.SemaphoreType.DMA((6,)),
        ],
        compiler_params=pltpu.CompilerParams(vmem_limit_bytes=4 * MIB),
    )(*(in_hbm(value) for value in (dest, props, volume, velocity, energy, mat)))


def stage_kernel(cell, state, sem):
    columns = state.shape[0] - 2
    width = state.shape[2] - 2 * PAD
    copies = [
        pltpu.make_async_copy(
            cell.at[:, :, pl.ds(j * BLK, BLK)], state.at[j + 1, :, pl.ds(PAD, width)], sem.at[j]
        )
        for j in range(columns)
    ]
    for copy in copies:
        copy.start()
    for copy in copies:
        copy.wait()


def stage(cell):
    count, width, lanes = cell.shape
    columns = lanes // BLK
    return pl.pallas_call(
        stage_kernel,
        name="stage",
        out_shape=pltpu.VMEM((columns + 2, count, width + 2 * PAD, BLK), F32),
        in_specs=[ANY],
        out_specs=VMEM,
        scratch_shapes=[pltpu.SemaphoreType.DMA((columns,))],
        compiler_params=pltpu.CompilerParams(vmem_limit_bytes=2 * MIB),
        cost_estimate=pl.CostEstimate(flops=0, bytes_accessed=2 * cell.size * 4, transcendentals=0),
    )(in_hbm(cell))


def fetch_kernel(source, target, sem):
    copy = pltpu.make_async_copy(source, target, sem)
    copy.start()
    copy.wait()


def fetch(value):
    return pl.pallas_call(
        fetch_kernel,
        name="fetch",
        out_shape=pltpu.VMEM(value.shape, value.dtype),
        in_specs=[ANY],
        out_specs=VMEM,
        scratch_shapes=[pltpu.SemaphoreType.DMA],
        compiler_params=pltpu.CompilerParams(vmem_limit_bytes=2 * MIB),
        cost_estimate=pl.CostEstimate(flops=0, bytes_accessed=2 * value.size * 2, transcendentals=0),
    )(in_hbm(value))


def local_slot(slot, pos_x, pos_y, size_y):
    at_x, at_y = split_device(slot >> 1, size_y)
    return code_of(at_y, pos_y) * (3 * CAP) + code_of(at_x, pos_x) * CAP + (slot & 1)


def low_lanes():
    return lax.broadcasted_iota(jnp.int32, (1, BLK), 1) < HALF


def turn(value):
    return pltpu.roll(value, HALF, value.ndim - 1)


def deposit_kernel(
    tile_slot, tile_cell, tile_count, own, first, second, north, south, weight, state_in,
    state, edge_x1, edge_x2, edge_y1, edge_y2, rows, *, size_y
):
    pos_x, pos_y = lax.axis_index("gx"), lax.axis_index("gy")
    n_tiles = weight.shape[0]
    columns, count, tall = state.shape[0] - 2, state.shape[1], state.shape[2]
    flat = state.reshape(columns + 2, count * tall, BLK)
    for k, part in enumerate((own, first, second)):
        for r in range(CAP):
            rows[k * CAP + r] = part[r]
    for k, part in enumerate((north, south)):
        for r in range(3 * CAP):
            rows[(k + 1) * 3 * CAP + r] = part[r]
    counted = tile_count[0]

    def add_tiles(step, carry):
        for k in range(UNROLL):
            t = step * UNROLL + k
            slot = local_slot(tile_slot[t], pos_x, pos_y, size_y)
            contrib = jnp.dot(rows[slot], weight[t], preferred_element_type=F32)[:count]
            contrib = jnp.where(t < counted, contrib, 0.0)
            x, j = split_device(tile_cell[t], columns)
            at = pl.ds(x + PAD, count, stride=tall)
            flat[j + 1, at, :] = flat[j + 1, at, :] + contrib
        return carry

    lax.fori_loop(0, n_tiles // UNROLL, add_tiles, 0)

    even_x, even_y = (pos_x & 1) == 0, (pos_y & 1) == 0
    top, bottom = tall - PAD - 1, PAD
    line = state.reshape((columns + 2) * count * tall, BLK)
    for edge, row in (
        (edge_x1, jnp.where(even_x, top, bottom)),
        (edge_x2, jnp.where(even_x, bottom, top)),
    ):
        for q in range(count):
            at = pl.ds(count * tall + q * tall + row, columns, stride=count * tall)
            edge[q * columns : (q + 1) * columns, :] = line[at, :].astype(BF16)
    low = low_lanes()
    width = tall - 2 * PAD
    for edge, upper in ((edge_y1, even_y), (edge_y2, jnp.logical_not(even_y))):
        column = jnp.where(upper, columns, 1)
        for q in range(count // 2):
            for i in range(width // ROWS):
                here = slice(PAD + i * ROWS, PAD + (i + 1) * ROWS)
                a = state[column, q, here, :]
                b = state[column, q + count // 2, here, :]
                both = jnp.where(low, jnp.where(upper, turn(a), a), jnp.where(upper, b, turn(b)))
                edge[q * width + i * ROWS : q * width + (i + 1) * ROWS, :] = both.astype(BF16)


def deposit(tile_slot, tile_cell, tile_count, parts, weight, state, size_y):
    columns, count, tall = state.shape[0] - 2, state.shape[1], state.shape[2]
    edge_x = pltpu.VMEM((count * columns, BLK), BF16)
    edge_y = pltpu.VMEM((count // 2 * (tall - 2 * PAD), BLK), BF16)
    return pl.pallas_call(
        functools.partial(deposit_kernel, size_y=size_y),
        name="deposit",
        out_shape=(pltpu.VMEM(state.shape, F32), edge_x, edge_x, edge_y, edge_y),
        in_specs=[SMEM] * 3 + [VMEM] * 7,
        out_specs=(VMEM,) * 5,
        input_output_aliases={9: 0},
        scratch_shapes=[pltpu.VMEM((9 * CAP, ROWS, BLK), BF16)],
        compiler_params=pltpu.CompilerParams(vmem_limit_bytes=4 * MIB),
    )(tile_slot, tile_cell, tile_count, *parts, weight, state)


def speeds_at(props, state, j, here, parts):
    terms = [props[0, m] * state[j, m, here, :] for m in range(MAT)]
    while len(terms) > 1:
        terms = [a + b for a, b in zip(terms[::2], terms[1::2], strict=True)]
    share = 1.0 / (1.0 + terms[0])
    found = []
    if 0 in parts:
        found.append((0, state[j, MAT, here, :] * share))
    if 1 in parts:
        along = state[j, MAT + 1, here, :] * share
        found += [(1, along), (2, turn(along))]
    return found


def store_speeds(props, state, speed, j, first_rows, parts):
    rows = [slice(first, first + 8) for first in first_rows]
    found = [speeds_at(props, state, j, here, parts) for here in rows]
    for here, planes in zip(rows, found, strict=True):
        for plane, value in planes:
            speed[j, plane, here, :] = value


def weights_at(speed, j, first_row):
    low = low_lanes()
    here = slice(first_row, first_row + 8)
    scale = 0.5 * time_step
    ux = speed[j, 0, here, :]
    lower = scale * (speed[j, 0, slice(first_row - 1, first_row + 7), :] + ux)
    upper = scale * (ux + speed[j, 0, slice(first_row + 1, first_row + 9), :])
    uy, before, after = (speed[k, 1, here, :] for k in (j, j - 1, j + 1))
    turned, turned_before, turned_after = (speed[k, 2, here, :] for k in (j, j - 1, j + 1))
    left = scale * (jnp.where(low, turned_before, turned) + uy)
    right = scale * (uy + jnp.where(low, turned, turned_after))
    keep = 1.0 - (
        (jnp.maximum(upper, 0.0) + jnp.maximum(-lower, 0.0)) + (jnp.maximum(right, 0.0) + jnp.maximum(-left, 0.0))
    )
    take_left = jnp.maximum(scale * (jnp.where(low, uy, before) + turned), 0.0)
    take_right = jnp.maximum(-scale * (turned + jnp.where(low, after, uy)), 0.0)
    same = jnp.where(low, take_left, take_right)
    other = jnp.where(low, take_right, take_left)
    return keep, jnp.maximum(lower, 0.0), jnp.maximum(-upper, 0.0), same, other


def remap_at(props, state, weights, j, first_row):
    count = state.shape[1]
    low = low_lanes()
    here = slice(first_row, first_row + 8)
    before = slice(first_row - 1, first_row + 7)
    after = slice(first_row + 1, first_row + 9)
    keep, take_before, take_after, same, other = weights
    values = []
    total = None
    for q in range(count):
        mid = state[j, q, here, :]
        beside = jnp.where(low, state[j + 1, q, here, :], state[j - 1, q, here, :])
        value = (keep * mid + take_before * state[j, q, before, :]) + take_after * state[j, q, after, :]
        value = value + turn(same * mid + other * beside)
        values.append(value)
        if q < MAT:
            term = value * (props[1, q] + (0.5 * props[1, q]) * value)
            total = term if total is None else total + term
        elif q == count - 1:
            total = total + 0.4 * value
    return values, total


def remap_tiles(props, state, speed, press, fresh, j, first_rows):
    def store(first_row, values, total):
        inside = slice(first_row - PAD, first_row - PAD + 8)
        for q, value in enumerate(values):
            fresh[j - 1, q, inside, :] = value
        press[j - 1, inside, :] = total

    waiting = None
    for first_row in first_rows:
        found = (first_row, *remap_at(props, state, weights_at(speed, j, first_row), j, first_row))
        if waiting is not None:
            store(*waiting)
        waiting = found
    store(*waiting)


def inner_kernel(props, state, remapped, press, speed, fresh, sem):
    columns, tall = state.shape[0] - 2, state.shape[2]
    tiles = (tall - 2 * PAD) // 8

    def speeds(j, carry):
        store_speeds(props, state, speed, j, range(PAD, tall - PAD, 8), (0, 1))
        return carry

    lax.fori_loop(1, columns + 1, speeds, 0)

    def write(j):
        rows = pl.ds(8, 8 * (tiles - 2))
        lanes = pl.ds(pl.multiple_of((j - 1) * BLK, BLK), BLK)
        return pltpu.make_async_copy(fresh.at[j - 1, :, rows], remapped.at[:, rows, lanes], sem.at[j - 1])

    def remap(j, carry):
        remap_tiles(props, state, speed, press, fresh, j, range(PAD + 8, tall - PAD - 8, 8))
        write(j).start()
        return carry

    lax.fori_loop(2, columns, remap, 0)

    def finish(j, carry):
        write(j).wait()
        return carry

    lax.fori_loop(2, columns, finish, 0)


def inner(props, state, width):
    columns, count, tall = state.shape[0] - 2, state.shape[1], state.shape[2]
    return pl.pallas_call(
        inner_kernel,
        name="inner",
        out_shape=(
            jax.ShapeDtypeStruct((count, width, columns * BLK), F32),
            pltpu.VMEM((columns, width, BLK), F32),
            pltpu.VMEM((columns + 2, 3, tall, BLK), F32),
        ),
        in_specs=[SMEM, VMEM],
        out_specs=(ANY, VMEM, VMEM),
        scratch_shapes=[pltpu.VMEM((columns, count, width, BLK), F32), pltpu.SemaphoreType.DMA((columns,))],
        compiler_params=pltpu.CompilerParams(vmem_limit_bytes=10 * MIB),
        cost_estimate=pl.CostEstimate(flops=20 * state.size, bytes_accessed=2 * state.size * 4, transcendentals=0),
    )(props, state)


def outer_kernel(
    props, tile_slot, tile_cell, tile_count, edge_x1, edge_x2, edge_y1, edge_y2, weight, state_in, speed_in, press_in,
    remapped_in, remapped, state, speed, press, own, first, second, fresh, sums, sem, *, size_y
):
    pos_x, pos_y = lax.axis_index("gx"), lax.axis_index("gy")
    n_tiles = weight.shape[0]
    columns, count, tall = state.shape[0] - 2, state.shape[1], state.shape[2]
    width = tall - 2 * PAD
    tiles = width // 8
    even_x, even_y = (pos_x & 1) == 0, (pos_y & 1) == 0
    line = state.reshape((columns + 2) * count * tall, BLK)
    above, below = tall - PAD, PAD - 1
    for edge, row in (
        (edge_x1, jnp.where(even_x, above, below)),
        (edge_x2, jnp.where(even_x, below, above)),
    ):
        for q in range(count):
            at = pl.ds(count * tall + q * tall + row, columns, stride=count * tall)
            line[at, :] = edge[q * columns : (q + 1) * columns, :].astype(F32)
    low = low_lanes()
    for edge, column in (
        (edge_y1, jnp.where(even_y, columns + 1, 0)),
        (edge_y2, jnp.where(even_y, 0, columns + 1)),
    ):
        for q in range(count // 2):
            for i in range(width // ROWS):
                here = slice(PAD + i * ROWS, PAD + (i + 1) * ROWS)
                both = edge[q * width + i * ROWS : q * width + (i + 1) * ROWS, :].astype(F32)
                turned = turn(both)
                state[column, q, here, :] = jnp.where(low, both, turned)
                state[column, q + count // 2, here, :] = jnp.where(low, turned, both)

    def side_speeds(j, carry):
        store_speeds(props, state, speed, j, (0, tall - PAD), (0,))
        return carry

    lax.fori_loop(1, columns + 1, side_speeds, 0)
    for j in (0, columns + 1):
        store_speeds(props, state, speed, j, range(PAD, tall - PAD, 8), (1,))

    def write(j, first_row, rows, which):
        rows = pl.ds(first_row, rows)
        lanes = pl.ds(pl.multiple_of((j - 1) * BLK, BLK), BLK)
        return pltpu.make_async_copy(fresh.at[j - 1, :, rows], remapped.at[:, rows, lanes], sem.at[which, j - 1])

    def sides(j, carry):
        remap_tiles(props, state, speed, press, fresh, j, (PAD, tall - PAD - 8))
        for which, i in enumerate((0, tiles - 1)):
            write(j, 8 * i, 8, which).start()
        return carry

    lax.fori_loop(1, columns + 1, sides, 0)
    for j in (1, columns):
        remap_tiles(props, state, speed, press, fresh, j, range(PAD + 8, tall - PAD - 8, 8))
        write(j, 8, 8 * (tiles - 2), 2).start()

    sums[...] = jnp.zeros(sums.shape, F32)
    counted = tile_count[0]
    head = lax.broadcasted_iota(jnp.int32, (ROWS, BLK), 0) == 0

    def sample(step, carry):
        for k in range(UNROLL):
            t = step * UNROLL + k
            slot = local_slot(tile_slot[t], pos_x, pos_y, size_y)
            x, j = split_device(tile_cell[t], columns)
            probe = jnp.where(head, press[j, pl.ds(x, 1), :], 1.0).astype(BF16)
            both = lax.dot_general(probe, weight[t], (((1,), (1,)), ((), ())), preferred_element_type=F32)[:8]
            sums[slot] = sums[slot] + jnp.where(t < counted, both, 0.0)
        return carry

    lax.fori_loop(0, n_tiles // UNROLL, sample, 0)
    table = sums.reshape(sums.shape[0] * 8, BLK)
    for k, out in enumerate((own, first, second)):
        top = table[pl.ds(k * 3 * CAP * 8, 3 * CAP, stride=8), :]
        under = table[pl.ds(k * 3 * CAP * 8 + 1, 3 * CAP, stride=8), :]
        out[...] = top / jnp.maximum(under, 1.0)

    def finish(j, carry):
        write(j, 0, 8, 0).wait()
        write(j, 8 * (tiles - 1), 8, 1).wait()
        return carry

    lax.fori_loop(1, columns + 1, finish, 0)
    for j in (1, columns):
        write(j, 8, 8 * (tiles - 2), 2).wait()


def outer(props, tile_slot, tile_cell, tile_count, edges, weight, state, speed, press, remapped, size_y):
    columns, count = state.shape[0] - 2, state.shape[1]
    answer = pltpu.VMEM((3 * CAP, BLK), F32)
    outs = pl.pallas_call(
        functools.partial(outer_kernel, size_y=size_y),
        name="outer",
        out_shape=(
            jax.ShapeDtypeStruct(remapped.shape, F32),
            pltpu.VMEM(state.shape, F32),
            pltpu.VMEM(speed.shape, F32),
            pltpu.VMEM(press.shape, F32),
            answer,
            answer,
            answer,
        ),
        in_specs=[SMEM] * 4 + [VMEM] * 8 + [ANY],
        out_specs=(ANY,) + (VMEM,) * 6,
        input_output_aliases={12: 0, 9: 1, 10: 2, 11: 3},
        scratch_shapes=[
            pltpu.VMEM((columns, count, remapped.shape[1], BLK), F32),
            pltpu.VMEM((9 * CAP, 8, BLK), F32),
            pltpu.SemaphoreType.DMA((3, columns)),
        ],
        compiler_params=pltpu.CompilerParams(vmem_limit_bytes=10 * MIB),
    )(props, tile_slot, tile_cell, tile_count, *edges, weight, state, speed, press, remapped)
    return outs[0], outs[4], outs[5], outs[6]


def pick_kernel(place, own, first, second, out, table):
    for k, part in enumerate((own, first, second)):
        table[k * 3 * CAP : (k + 1) * 3 * CAP, :] = part[...]
    for b in range(out.shape[0]):
        out[b : b + 1, :] = table[pl.ds(place[b], 1), :]


def pick(place, own, first, second):
    return pl.pallas_call(
        pick_kernel,
        name="pick",
        out_shape=pltpu.VMEM((place.shape[0], BLK), F32),
        in_specs=[SMEM, VMEM, VMEM, VMEM],
        out_specs=VMEM,
        scratch_shapes=[pltpu.VMEM((9 * CAP, BLK), F32)],
        compiler_params=pltpu.CompilerParams(vmem_limit_bytes=2 * MIB),
    )(place, own, first, second)


def per_device(
    elem_volume,
    elem_velocity,
    elem_energy,
    elem_mat,
    elem_dest,
    tile_slot,
    tile_cell,
    tile_weight,
    tile_count,
    cell_state,
    mat_props,
):
    size_y = lax.axis_size("gy")
    n_blocks = elem_dest.shape[0]
    shape = (n_blocks, BLK)
    own, first, second, place = payload(
        elem_dest,
        mat_props,
        elem_volume.reshape(shape),
        elem_velocity,
        elem_energy.reshape(shape),
        elem_mat.reshape(shape),
        size_y,
    )
    state = stage(cell_state)
    weight = fetch(tile_weight)

    second = swap(second, "gx", 2)
    first = swap(first, "gx", 1)

    def along_y(which):
        rows = slice(which * CAP, (which + 1) * CAP)
        return jnp.concatenate([own[rows], first[rows], second[rows]], axis=0)

    south = swap(along_y(2), "gy", 2)
    north = swap(along_y(1), "gy", 1)
    state, *edges = deposit(
        tile_slot, tile_cell, tile_count, (own, first, second, north, south), weight, state, size_y
    )
    edges = (
        swap(edges[0], "gx", 1, wrap=False),
        swap(edges[1], "gx", 2, wrap=False),
        swap(edges[2], "gy", 1, wrap=False),
        swap(edges[3], "gy", 2, wrap=False),
    )
    remapped, press, speed = inner(mat_props, state, cell_state.shape[1])
    remapped, own, first, second = outer(
        mat_props, tile_slot, tile_cell, tile_count, edges, weight, state, speed, press, remapped, size_y
    )
    second = swap(second, "gy", 2)
    first = swap(first, "gy", 1)

    def along_x(which):
        rows = slice(which * CAP, (which + 1) * CAP)
        return jnp.concatenate([own[rows], first[rows], second[rows]], axis=0)

    back = pick(place, along_x(0), swap(along_x(1), "gx", 1), swap(along_x(2), "gx", 2))
    return remapped, back.astype(BF16).reshape(n_blocks * BLK)


def solution(mesh):
    placed = (
        P(("gx", "gy")),
        P(None, ("gx", "gy")),
        P(("gx", "gy")),
        P(("gx", "gy")),
        P(("gx", "gy")),
        P(("gx", "gy")),
        P(("gx", "gy")),
        P(("gx", "gy"), None, None),
        P(("gx", "gy")),
        P(None, "gx", "gy"),
        P(),
    )
    return jax.shard_map(
        per_device,
        mesh=mesh,
        in_specs=placed,
        out_specs=(P(None, "gx", "gy"), P(("gx", "gy"))),
        check_vma=False,
    )
```

```python
import functools

import jax
import jax.numpy as jnp
from jax import lax
from jax.experimental import pallas as pl
from jax.experimental.pallas import tpu as pltpu
from jax.sharding import PartitionSpec as P

MAT = 8
NZ = 64
BLK = 128
CAP = 2
HALF = BLK // 2
PAD = 8
ROWS = 16
UNROLL = 128
PAIR = 2
GROUP = 8
DELAY = 4
MIB = 2**20

time_step = 0.8
F32 = jnp.float32
BF16 = jnp.bfloat16

SMEM = pl.BlockSpec(memory_space=pltpu.SMEM)
VMEM = pl.BlockSpec(memory_space=pltpu.VMEM)
ANY = pl.BlockSpec(memory_space=pl.ANY)


def partner(index, size, which):
    if which == 2:
        return index ^ 1
    return (index + 1 if index % 2 else index - 1) % size


def swap(value, axis, which, wrap=True):
    size = lax.axis_size(axis)
    pairs = [(i, partner(i, size, which)) for i in range(size)]
    if not wrap:
        pairs = [(i, j) for i, j in pairs if abs(i - j) == 1]
    return lax.ppermute(value, axis, pairs)


def code_of(index, mine):
    return jnp.where(index == mine, 0, jnp.where(index == (mine ^ 1), 2, 1))


def split_device(device, size):
    if size & (size - 1) == 0:
        return device >> (size.bit_length() - 1), device & (size - 1)
    return lax.div(device, size), lax.rem(device, size)


def in_hbm(value):
    return pltpu.with_memory_space_constraint(value, pltpu.HBM)


def payload_kernel(
    dest_hbm, props_hbm, volume_hbm, velocity_hbm, energy_hbm, mat_hbm, own, first, second, place,
    dest, props, volume, velocity, energy, mat, seen, packed, sem, *, size_y
):
    moves = (
        (dest_hbm, dest), (props_hbm, props), (mat_hbm, mat),
        (volume_hbm, volume), (velocity_hbm, velocity), (energy_hbm, energy),
    )
    copies = [pltpu.make_async_copy(src, dst, sem.at[k]) for k, (src, dst) in enumerate(moves)]
    for copy in copies:
        copy.start()
    for copy in copies:
        copy.wait()
    pos_x, pos_y = lax.axis_index("gx"), lax.axis_index("gy")
    n_blocks = volume.shape[0]
    kinds = mat[...]
    density = jnp.zeros(kinds.shape, F32)
    for m in range(MAT):
        density = jnp.where(kinds == m, props[0, m], density)
    mass = volume[...] * density
    heat = mass * energy[...]
    level = lax.broadcasted_iota(jnp.int32, (MAT, BLK), 0)
    for k in range(9):
        seen[k] = 0
    for b in range(n_blocks):
        at_x, at_y = split_device(dest[b], size_y)
        near = code_of(at_x, pos_x) * 3 + code_of(at_y, pos_y)
        rank = seen[near]
        seen[near] = rank + 1
        slot = near * CAP + rank
        place[b] = slot
        volumes = jnp.where(kinds[b : b + 1] == level, volume[b : b + 1, :], 0.0)
        momentum = mass[b : b + 1] * velocity[:, b * BLK : (b + 1) * BLK]
        rows = jnp.concatenate([volumes, momentum, heat[b : b + 1], jnp.zeros((4, BLK), F32)], axis=0)
        packed[slot] = rows.astype(BF16)
    for k, out in enumerate((own, first, second)):
        for s in range(3 * CAP):
            out[s] = packed[k * 3 * CAP + s]


def payload(dest, props, volume, velocity, energy, mat, size_y):
    n_blocks = volume.shape[0]
    parcel = pltpu.VMEM((3 * CAP, ROWS, BLK), BF16)
    return pl.pallas_call(
        functools.partial(payload_kernel, size_y=size_y),
        name="payload",
        out_shape=(parcel, parcel, parcel, jax.ShapeDtypeStruct((n_blocks,), jnp.int32)),
        in_specs=[ANY] * 6,
        out_specs=(VMEM, VMEM, VMEM, SMEM),
        scratch_shapes=[
            pltpu.SMEM(dest.shape, jnp.int32),
            pltpu.SMEM(props.shape, F32),
            pltpu.VMEM(volume.shape, F32),
            pltpu.VMEM(velocity.shape, F32),
            pltpu.VMEM(energy.shape, F32),
            pltpu.VMEM(mat.shape, jnp.int32),
            pltpu.SMEM((9,), jnp.int32),
            pltpu.VMEM((9 * CAP, ROWS, BLK), BF16),
            pltpu.SemaphoreType.DMA((6,)),
        ],
        compiler_params=pltpu.CompilerParams(vmem_limit_bytes=4 * MIB),
    )(*(in_hbm(value) for value in (dest, props, volume, velocity, energy, mat)))


def stage_kernel(cell, state, sem):
    columns = state.shape[0] - 2
    width = state.shape[2] - 2 * PAD
    copies = [
        pltpu.make_async_copy(
            cell.at[:, :, pl.ds(j * BLK, BLK)], state.at[j + 1, :, pl.ds(PAD, width)], sem.at[j]
        )
        for j in range(columns)
    ]
    for copy in copies:
        copy.start()
    for copy in copies:
        copy.wait()


def stage(cell):
    count, width, lanes = cell.shape
    columns = lanes // BLK
    return pl.pallas_call(
        stage_kernel,
        name="stage",
        out_shape=pltpu.VMEM((columns + 2, count, width + 2 * PAD, BLK), F32),
        in_specs=[ANY],
        out_specs=VMEM,
        scratch_shapes=[pltpu.SemaphoreType.DMA((columns,))],
        compiler_params=pltpu.CompilerParams(vmem_limit_bytes=2 * MIB),
        cost_estimate=pl.CostEstimate(flops=0, bytes_accessed=2 * cell.size * 4, transcendentals=0),
    )(in_hbm(cell))


def fetch_kernel(source, target, sem):
    copy = pltpu.make_async_copy(source, target, sem)
    copy.start()
    copy.wait()


def fetch(value):
    return pl.pallas_call(
        fetch_kernel,
        name="fetch",
        out_shape=pltpu.VMEM(value.shape, value.dtype),
        in_specs=[ANY],
        out_specs=VMEM,
        scratch_shapes=[pltpu.SemaphoreType.DMA],
        compiler_params=pltpu.CompilerParams(vmem_limit_bytes=2 * MIB),
        cost_estimate=pl.CostEstimate(flops=0, bytes_accessed=2 * value.size * 2, transcendentals=0),
    )(in_hbm(value))


def local_slot(slot, pos_x, pos_y, size_y):
    at_x, at_y = split_device(slot >> 1, size_y)
    return code_of(at_y, pos_y) * (3 * CAP) + code_of(at_x, pos_x) * CAP + (slot & 1)


def low_lanes():
    return lax.broadcasted_iota(jnp.int32, (1, BLK), 1) < HALF


def turn(value):
    return pltpu.roll(value, HALF, value.ndim - 1)


def deposit_kernel(
    tile_slot, tile_cell, tile_count, own, first, second, south, north, weight, state_in,
    state, edge_x1, edge_x2, edge_y1, edge_y2, rows, *, size_y
):
    pos_x, pos_y = lax.axis_index("gx"), lax.axis_index("gy")
    n_tiles = weight.shape[0]
    columns, count, tall = state.shape[0] - 2, state.shape[1], state.shape[2]
    flat = state.reshape(columns + 2, count * tall, BLK)
    for k, part in enumerate((own, first, second)):
        for r in range(CAP):
            rows[k * CAP + r] = part[r]
    for k, part in enumerate((south, north)):
        for r in range(3 * CAP):
            rows[(k + 1) * 3 * CAP + r] = part[r]
    counted = tile_count[0]

    def add_tiles(step, carry):
        for k in range(UNROLL):
            t = step * UNROLL + k
            slot = local_slot(tile_slot[t], pos_x, pos_y, size_y)
            contrib = jnp.dot(rows[slot], weight[t], preferred_element_type=F32)[:count]
            contrib = jnp.where(t < counted, contrib, 0.0)
            x, j = split_device(tile_cell[t], columns)
            at = pl.ds(x + PAD, count, stride=tall)
            flat[j + 1, at, :] = flat[j + 1, at, :] + contrib
        return carry

    lax.fori_loop(0, n_tiles // UNROLL, add_tiles, 0)

    even_x, even_y = (pos_x & 1) == 0, (pos_y & 1) == 0
    top, bottom = tall - PAD - 1, PAD
    line = state.reshape((columns + 2) * count * tall, BLK)
    for edge, row in (
        (edge_x1, jnp.where(even_x, bottom, top)),
        (edge_x2, jnp.where(even_x, top, bottom)),
    ):
        for q in range(count):
            at = pl.ds(count * tall + q * tall + row, columns, stride=count * tall)
            edge[q * columns : (q + 1) * columns, :] = line[at, :].astype(BF16)
    low = low_lanes()
    width = tall - 2 * PAD
    for edge, upper in ((edge_y1, jnp.logical_not(even_y)), (edge_y2, even_y)):
        column = jnp.where(upper, columns, 1)
        for q in range(count // 2):
            for i in range(width // ROWS):
                here = slice(PAD + i * ROWS, PAD + (i + 1) * ROWS)
                a = state[column, q, here, :]
                b = state[column, q + count // 2, here, :]
                both = jnp.where(low, jnp.where(upper, turn(a), a), jnp.where(upper, b, turn(b)))
                edge[q * width + i * ROWS : q * width + (i + 1) * ROWS, :] = both.astype(BF16)


def deposit(tile_slot, tile_cell, tile_count, parts, weight, state, size_y):
    columns, count, tall = state.shape[0] - 2, state.shape[1], state.shape[2]
    edge_x = pltpu.VMEM((count * columns, BLK), BF16)
    edge_y = pltpu.VMEM((count // 2 * (tall - 2 * PAD), BLK), BF16)
    return pl.pallas_call(
        functools.partial(deposit_kernel, size_y=size_y),
        name="deposit",
        out_shape=(pltpu.VMEM(state.shape, F32), edge_x, edge_x, edge_y, edge_y),
        in_specs=[SMEM] * 3 + [VMEM] * 7,
        out_specs=(VMEM,) * 5,
        input_output_aliases={9: 0},
        scratch_shapes=[pltpu.VMEM((9 * CAP, ROWS, BLK), BF16)],
        compiler_params=pltpu.CompilerParams(vmem_limit_bytes=4 * MIB),
    )(tile_slot, tile_cell, tile_count, *parts, weight, state)


def total(terms):
    while len(terms) > 1:
        terms = [a + b for a, b in zip(terms[::2], terms[1::2], strict=True)]
    return terms[0]


def speeds_at(props, state, j, here, parts):
    share = 1.0 / (1.0 + total([props[0, m] * state[j, m, here, :] for m in range(MAT)]))
    found = []
    if 0 in parts:
        found.append((0, state[j, MAT, here, :] * share))
    if 1 in parts:
        along = state[j, MAT + 1, here, :] * share
        found += [(1, along), (2, turn(along))]
    return found


def store_speeds(props, state, speed, places, parts):
    waiting = []
    for step in range(len(places) + DELAY):
        if step < len(places):
            j, first_row = places[step]
            waiting.append(speeds_at(props, state, j, slice(first_row, first_row + 8), parts))
        if step >= DELAY:
            j, first_row = places[step - DELAY]
            for plane, value in waiting.pop(0):
                speed[j, plane, first_row : first_row + 8, :] = value


def weights_at(speed, j, first_row):
    low = low_lanes()
    here = slice(first_row, first_row + 8)
    scale = 0.5 * time_step
    ux = speed[j, 0, here, :]
    lower = scale * (speed[j, 0, slice(first_row - 1, first_row + 7), :] + ux)
    upper = scale * (ux + speed[j, 0, slice(first_row + 1, first_row + 9), :])
    uy, before, after = (speed[k, 1, here, :] for k in (j, j - 1, j + 1))
    turned, turned_before, turned_after = (speed[k, 2, here, :] for k in (j, j - 1, j + 1))
    left = scale * (jnp.where(low, turned_before, turned) + uy)
    right = scale * (uy + jnp.where(low, turned, turned_after))
    keep = 1.0 - (
        (jnp.maximum(upper, 0.0) + jnp.maximum(-lower, 0.0)) + (jnp.maximum(right, 0.0) + jnp.maximum(-left, 0.0))
    )
    take_left = jnp.maximum(scale * (jnp.where(low, uy, before) + turned), 0.0)
    take_right = jnp.maximum(-scale * (turned + jnp.where(low, after, uy)), 0.0)
    same = jnp.where(low, take_left, take_right)
    other = jnp.where(low, take_right, take_left)
    return keep, jnp.maximum(lower, 0.0), jnp.maximum(-upper, 0.0), same, other


def values_at(state, weights, j, first_row):
    low = low_lanes()
    here = slice(first_row, first_row + 8)
    before = slice(first_row - 1, first_row + 7)
    after = slice(first_row + 1, first_row + 9)
    keep, take_before, take_after, same, other = weights
    values = []
    for q in range(state.shape[1]):
        mid = state[j, q, here, :]
        beside = jnp.where(low, state[j + 1, q, here, :], state[j - 1, q, here, :])
        value = (keep * mid + take_before * state[j, q, before, :]) + take_after * state[j, q, after, :]
        values.append(value + turn(same * mid + other * beside))
    return values


def pressure_of(props, values):
    terms = [value * (props[1, m] + (0.5 * props[1, m]) * value) for m, value in enumerate(values[:MAT])]
    return total(terms) + 0.4 * values[-1]


def remap_tiles(props, state, speed, press, fresh, places):
    weights, values = {}, {}
    for step in range(len(places) + 2):
        if step < len(places):
            weights[step] = weights_at(speed, *places[step])
        k = step - 1
        if 0 <= k < len(places):
            values[k] = values_at(state, weights.pop(k), *places[k])
        k = step - 2
        if k >= 0:
            found = values.pop(k)
            j, first_row = places[k]
            inside = slice(first_row - PAD, first_row - PAD + 8)
            lanes = column_lanes(j)
            for q, value in enumerate(found):
                fresh[q, inside, lanes] = value
            press[j - 1, inside, :] = pressure_of(props, found)


def column_lanes(j):
    if isinstance(j, int):
        return slice((j - 1) * BLK, j * BLK)
    return pl.ds(pl.multiple_of((j - 1) * BLK, BLK), BLK)


def inner_kernel(props, state, fresh, press, speed):
    columns, tall = state.shape[0] - 2, state.shape[2]

    def speeds(step, carry):
        rows = range(PAD, tall - PAD, 8)
        places = [(1 + step * GROUP + k, row) for k in range(GROUP) for row in rows]
        store_speeds(props, state, speed, places, (0, 1))
        return carry

    lax.fori_loop(0, columns // GROUP, speeds, 0)

    def remap(step, carry):
        rows = range(PAD + 8, tall - PAD - 8, 8)
        places = [(2 + step * PAIR + k, row) for k in range(PAIR) for row in rows]
        remap_tiles(props, state, speed, press, fresh, places)
        return carry

    lax.fori_loop(0, (columns - 2) // PAIR, remap, 0)


def inner(props, state, width):
    columns, count, tall = state.shape[0] - 2, state.shape[1], state.shape[2]
    return pl.pallas_call(
        inner_kernel,
        name="inner",
        out_shape=(
            pltpu.VMEM((count, width, columns * BLK), F32),
            pltpu.VMEM((columns, width, BLK), F32),
            pltpu.VMEM((columns + 2, 3, tall, BLK), F32),
        ),
        in_specs=[SMEM, VMEM],
        out_specs=(VMEM, VMEM, VMEM),
        compiler_params=pltpu.CompilerParams(vmem_limit_bytes=4 * MIB),
        cost_estimate=pl.CostEstimate(flops=20 * state.size, bytes_accessed=2 * state.size * 4, transcendentals=0),
    )(props, state)


def outer_kernel(
    props, tile_slot, tile_cell, tile_count, edge_x1, edge_x2, edge_y1, edge_y2, weight, state_in, speed_in, press_in,
    fresh_in, remapped, state, speed, press, fresh, own, first, second, sums, sem, *, size_y
):
    pos_x, pos_y = lax.axis_index("gx"), lax.axis_index("gy")
    n_tiles = weight.shape[0]
    columns, count, tall = state.shape[0] - 2, state.shape[1], state.shape[2]
    width = tall - 2 * PAD
    middle = pl.ds(8, width - 16)
    areas = (
        (middle, pl.ds(BLK, (columns - 2) * BLK)),
        (pl.ds(0, 8), pl.ds(0, columns * BLK)),
        (pl.ds(width - 8, 8), pl.ds(0, columns * BLK)),
        (middle, pl.ds(0, BLK)),
        (middle, pl.ds((columns - 1) * BLK, BLK)),
    )
    copies = [
        pltpu.make_async_copy(fresh.at[:, rows, lanes], remapped.at[:, rows, lanes], sem.at[k])
        for k, (rows, lanes) in enumerate(areas)
    ]
    copies[0].start()
    even_x, even_y = (pos_x & 1) == 0, (pos_y & 1) == 0
    line = state.reshape((columns + 2) * count * tall, BLK)
    above, below = tall - PAD, PAD - 1
    for edge, row in (
        (edge_x1, jnp.where(even_x, below, above)),
        (edge_x2, jnp.where(even_x, above, below)),
    ):
        for q in range(count):
            at = pl.ds(count * tall + q * tall + row, columns, stride=count * tall)
            line[at, :] = edge[q * columns : (q + 1) * columns, :].astype(F32)
    low = low_lanes()
    for edge, column in (
        (edge_y1, jnp.where(even_y, 0, columns + 1)),
        (edge_y2, jnp.where(even_y, columns + 1, 0)),
    ):
        for q in range(count // 2):
            for i in range(width // ROWS):
                here = slice(PAD + i * ROWS, PAD + (i + 1) * ROWS)
                both = edge[q * width + i * ROWS : q * width + (i + 1) * ROWS, :].astype(F32)
                turned = turn(both)
                state[column, q, here, :] = jnp.where(low, both, turned)
                state[column, q + count // 2, here, :] = jnp.where(low, turned, both)

    places = [(j, row) for j in range(1, columns + 1) for row in (0, tall - PAD)]
    store_speeds(props, state, speed, places, (0,))
    places = [(j, row) for j in (0, columns + 1) for row in range(PAD, tall - PAD, 8)]
    store_speeds(props, state, speed, places, (1,))

    def sides(step, carry):
        places = [(1 + step * 2 * PAIR + k, row) for k in range(2 * PAIR) for row in (PAD, tall - PAD - 8)]
        remap_tiles(props, state, speed, press, fresh, places)
        return carry

    lax.fori_loop(0, columns // (2 * PAIR), sides, 0)
    copies[1].start()
    copies[2].start()
    places = [(j, row) for j in (1, columns) for row in range(PAD + 8, tall - PAD - 8, 8)]
    remap_tiles(props, state, speed, press, fresh, places)
    copies[3].start()
    copies[4].start()

    sums[...] = jnp.zeros(sums.shape, F32)
    counted = tile_count[0]
    head = lax.broadcasted_iota(jnp.int32, (ROWS, BLK), 0) == 0

    def sample(step, carry):
        for k in range(UNROLL):
            t = step * UNROLL + k
            slot = local_slot(tile_slot[t], pos_x, pos_y, size_y)
            x, j = split_device(tile_cell[t], columns)
            probe = jnp.where(head, press[j, pl.ds(x, 1), :], 1.0).astype(BF16)
            both = lax.dot_general(probe, weight[t], (((1,), (1,)), ((), ())), preferred_element_type=F32)[:8]
            sums[slot] = sums[slot] + jnp.where(t < counted, both, 0.0)
        return carry

    lax.fori_loop(0, n_tiles // UNROLL, sample, 0)
    table = sums.reshape(sums.shape[0] * 8, BLK)
    for k, out in enumerate((own, first, second)):
        top = table[pl.ds(k * 3 * CAP * 8, 3 * CAP, stride=8), :]
        under = table[pl.ds(k * 3 * CAP * 8 + 1, 3 * CAP, stride=8), :]
        out[...] = top / jnp.maximum(under, 1.0)

    for copy in copies:
        copy.wait()


def outer(props, tile_slot, tile_cell, tile_count, edges, weight, state, speed, press, fresh, size_y):
    answer = pltpu.VMEM((3 * CAP, BLK), F32)
    outs = pl.pallas_call(
        functools.partial(outer_kernel, size_y=size_y),
        name="outer",
        out_shape=(
            jax.ShapeDtypeStruct(fresh.shape, F32),
            pltpu.VMEM(state.shape, F32),
            pltpu.VMEM(speed.shape, F32),
            pltpu.VMEM(press.shape, F32),
            pltpu.VMEM(fresh.shape, F32),
            answer,
            answer,
            answer,
        ),
        in_specs=[SMEM] * 4 + [VMEM] * 9,
        out_specs=(ANY,) + (VMEM,) * 7,
        input_output_aliases={9: 1, 10: 2, 11: 3, 12: 4},
        scratch_shapes=[pltpu.VMEM((9 * CAP, 8, BLK), F32), pltpu.SemaphoreType.DMA((5,))],
        compiler_params=pltpu.CompilerParams(vmem_limit_bytes=4 * MIB),
    )(props, tile_slot, tile_cell, tile_count, *edges, weight, state, speed, press, fresh)
    return outs[0], outs[5], outs[6], outs[7]


def pick_kernel(place, own, first, second, out, table):
    for k, part in enumerate((own, first, second)):
        table[k * 3 * CAP : (k + 1) * 3 * CAP, :] = part[...]
    for b in range(out.shape[0]):
        out[b : b + 1, :] = table[pl.ds(place[b], 1), :]


def pick(place, own, first, second):
    return pl.pallas_call(
        pick_kernel,
        name="pick",
        out_shape=pltpu.VMEM((place.shape[0], BLK), F32),
        in_specs=[SMEM, VMEM, VMEM, VMEM],
        out_specs=VMEM,
        scratch_shapes=[pltpu.VMEM((9 * CAP, BLK), F32)],
        compiler_params=pltpu.CompilerParams(vmem_limit_bytes=2 * MIB),
    )(place, own, first, second)


def per_device(
    elem_volume,
    elem_velocity,
    elem_energy,
    elem_mat,
    elem_dest,
    tile_slot,
    tile_cell,
    tile_weight,
    tile_count,
    cell_state,
    mat_props,
):
    size_y = lax.axis_size("gy")
    n_blocks = elem_dest.shape[0]
    shape = (n_blocks, BLK)
    own, first, second, place = payload(
        elem_dest,
        mat_props,
        elem_volume.reshape(shape),
        elem_velocity,
        elem_energy.reshape(shape),
        elem_mat.reshape(shape),
        size_y,
    )
    state = stage(cell_state)
    weight = fetch(tile_weight)

    first = swap(first, "gx", 1)
    second = swap(second, "gx", 2)
    weight, own = lax.optimization_barrier((weight, own))

    def along_y(which):
        rows = slice(which * CAP, (which + 1) * CAP)
        return jnp.concatenate([own[rows], first[rows], second[rows]], axis=0)

    south = swap(along_y(1), "gy", 1)
    north = swap(along_y(2), "gy", 2)
    state, *edges = deposit(
        tile_slot, tile_cell, tile_count, (own, first, second, south, north), weight, state, size_y
    )
    edges = (
        swap(edges[0], "gx", 1, wrap=False),
        swap(edges[1], "gx", 2, wrap=False),
        swap(edges[2], "gy", 1, wrap=False),
        swap(edges[3], "gy", 2, wrap=False),
    )
    fresh, press, speed = inner(mat_props, state, cell_state.shape[1])
    remapped, own, first, second = outer(
        mat_props, tile_slot, tile_cell, tile_count, edges, weight, state, speed, press, fresh, size_y
    )
    first = swap(first, "gy", 1)
    second = swap(second, "gy", 2)

    def along_x(which):
        rows = slice(which * CAP, (which + 1) * CAP)
        return jnp.concatenate([own[rows], first[rows], second[rows]], axis=0)

    back = pick(place, along_x(0), swap(along_x(1), "gx", 1), swap(along_x(2), "gx", 2))
    return remapped, back.astype(BF16).reshape(n_blocks * BLK)


def solution(mesh):
    placed = (
        P(("gx", "gy")),
        P(None, ("gx", "gy")),
        P(("gx", "gy")),
        P(("gx", "gy")),
        P(("gx", "gy")),
        P(("gx", "gy")),
        P(("gx", "gy")),
        P(("gx", "gy"), None, None),
        P(("gx", "gy")),
        P(None, "gx", "gy"),
        P(),
    )
    return jax.shard_map(
        per_device,
        mesh=mesh,
        in_specs=placed,
        out_specs=(P(None, "gx", "gy"), P(("gx", "gy"))),
        check_vma=False,
    )
```

```python
import functools

import jax
import jax.numpy as jnp
from jax import lax
from jax.experimental import pallas as pl
from jax.experimental.pallas import tpu as pltpu
from jax.sharding import PartitionSpec as P

MAT = 8
NZ = 64
BLK = 128
CAP = 2
HALF = BLK // 2
PAD = 8
ROWS = 16
UNROLL = 128
PAIR = 2
TURN = 16
GROUP = 8
DELAY = 4
MIB = 2**20

time_step = 0.8
F32 = jnp.float32
BF16 = jnp.bfloat16

SMEM = pl.BlockSpec(memory_space=pltpu.SMEM)
VMEM = pl.BlockSpec(memory_space=pltpu.VMEM)
ANY = pl.BlockSpec(memory_space=pl.ANY)


def partner(index, size, which):
    if which == 2:
        return index ^ 1
    return (index + 1 if index % 2 else index - 1) % size


def swap(value, axis, which, wrap=True):
    size = lax.axis_size(axis)
    pairs = [(i, partner(i, size, which)) for i in range(size)]
    if not wrap:
        pairs = [(i, j if abs(i - j) == 1 else i) for i, j in pairs]
    return lax.ppermute(value, axis, pairs)


def has_far(index, size):
    return (index > 0) & (index < size - 1)


def code_of(index, mine):
    return jnp.where(index == mine, 0, jnp.where(index == (mine ^ 1), 2, 1))


def split_device(device, size):
    if size & (size - 1) == 0:
        return device >> (size.bit_length() - 1), device & (size - 1)
    return lax.div(device, size), lax.rem(device, size)


def in_hbm(value):
    return pltpu.with_memory_space_constraint(value, pltpu.HBM)


def payload_kernel(
    dest_hbm, props_hbm, volume_hbm, velocity_hbm, energy_hbm, mat_hbm, own, first, second, place,
    dest, props, volume, velocity, energy, mat, seen, packed, sem, *, size_y
):
    moves = (
        (dest_hbm, dest), (props_hbm, props), (mat_hbm, mat),
        (volume_hbm, volume), (velocity_hbm, velocity), (energy_hbm, energy),
    )
    copies = [pltpu.make_async_copy(src, dst, sem.at[k]) for k, (src, dst) in enumerate(moves)]
    for copy in copies:
        copy.start()
    for copy in copies:
        copy.wait()
    pos_x, pos_y = lax.axis_index("gx"), lax.axis_index("gy")
    n_blocks = volume.shape[0]
    kinds = mat[...]
    density = jnp.zeros(kinds.shape, F32)
    for m in range(MAT):
        density = jnp.where(kinds == m, props[0, m], density)
    mass = volume[...] * density
    heat = mass * energy[...]
    level = lax.broadcasted_iota(jnp.int32, (MAT, BLK), 0)
    for k in range(9):
        seen[k] = 0
    for b in range(n_blocks):
        at_x, at_y = split_device(dest[b], size_y)
        near = code_of(at_x, pos_x) * 3 + code_of(at_y, pos_y)
        rank = seen[near]
        seen[near] = rank + 1
        slot = near * CAP + rank
        place[b] = slot
        volumes = jnp.where(kinds[b : b + 1] == level, volume[b : b + 1, :], 0.0)
        momentum = mass[b : b + 1] * velocity[:, b * BLK : (b + 1) * BLK]
        rows = jnp.concatenate([volumes, momentum, heat[b : b + 1], jnp.zeros((4, BLK), F32)], axis=0)
        packed[slot] = rows.astype(BF16)
    for k, out in enumerate((own, first, second)):
        for s in range(3 * CAP):
            out[s] = packed[k * 3 * CAP + s]


def payload(dest, props, volume, velocity, energy, mat, size_y):
    n_blocks = volume.shape[0]
    parcel = pltpu.VMEM((3 * CAP, ROWS, BLK), BF16)
    return pl.pallas_call(
        functools.partial(payload_kernel, size_y=size_y),
        name="payload",
        out_shape=(parcel, parcel, parcel, jax.ShapeDtypeStruct((n_blocks,), jnp.int32)),
        in_specs=[ANY] * 6,
        out_specs=(VMEM, VMEM, VMEM, SMEM),
        scratch_shapes=[
            pltpu.SMEM(dest.shape, jnp.int32),
            pltpu.SMEM(props.shape, F32),
            pltpu.VMEM(volume.shape, F32),
            pltpu.VMEM(velocity.shape, F32),
            pltpu.VMEM(energy.shape, F32),
            pltpu.VMEM(mat.shape, jnp.int32),
            pltpu.SMEM((9,), jnp.int32),
            pltpu.VMEM((9 * CAP, ROWS, BLK), BF16),
            pltpu.SemaphoreType.DMA((6,)),
        ],
        compiler_params=pltpu.CompilerParams(vmem_limit_bytes=4 * MIB),
    )(*(in_hbm(value) for value in (dest, props, volume, velocity, energy, mat)))


def stage_kernel(cell, weight, state, turned, sem):
    columns = state.shape[0] - 2
    width = state.shape[2] - 2 * PAD
    copies = [
        pltpu.make_async_copy(
            cell.at[:, :, pl.ds(j * BLK, BLK)], state.at[j + 1, :, pl.ds(PAD, width)], sem.at[j]
        )
        for j in range(columns)
    ]
    for copy in copies:
        copy.start()

    def transpose(step, carry):
        for k in range(TURN):
            turned[step * TURN + k] = weight[step * TURN + k].T
        return carry

    lax.fori_loop(0, weight.shape[0] // TURN, transpose, 0)
    for copy in copies:
        copy.wait()


def stage(cell, weight):
    count, width, lanes = cell.shape
    columns = lanes // BLK
    return pl.pallas_call(
        stage_kernel,
        name="stage",
        out_shape=(
            pltpu.VMEM((columns + 2, count, width + 2 * PAD, BLK), F32),
            pltpu.VMEM(weight.shape, weight.dtype),
        ),
        in_specs=[ANY, VMEM],
        out_specs=(VMEM, VMEM),
        scratch_shapes=[pltpu.SemaphoreType.DMA((columns,))],
        compiler_params=pltpu.CompilerParams(vmem_limit_bytes=2 * MIB),
        cost_estimate=pl.CostEstimate(flops=0, bytes_accessed=2 * cell.size * 4, transcendentals=0),
    )(in_hbm(cell), weight)


def fetch_kernel(source, target, sem):
    copy = pltpu.make_async_copy(source, target, sem)
    copy.start()
    copy.wait()


def fetch(value):
    return pl.pallas_call(
        fetch_kernel,
        name="fetch",
        out_shape=pltpu.VMEM(value.shape, value.dtype),
        in_specs=[ANY],
        out_specs=VMEM,
        scratch_shapes=[pltpu.SemaphoreType.DMA],
        compiler_params=pltpu.CompilerParams(vmem_limit_bytes=2 * MIB),
        cost_estimate=pl.CostEstimate(flops=0, bytes_accessed=2 * value.size * 2, transcendentals=0),
    )(in_hbm(value))


def local_slot(slot, pos_x, pos_y, size_y):
    at_x, at_y = split_device(slot >> 1, size_y)
    return code_of(at_y, pos_y) * (3 * CAP) + code_of(at_x, pos_x) * CAP + (slot & 1)


def low_lanes():
    return lax.broadcasted_iota(jnp.int32, (1, BLK), 1) < HALF


def turn(value):
    return pltpu.roll(value, HALF, value.ndim - 1)


def deposit_kernel(
    tile_slot, tile_cell, tile_count, own, first, second, south, north, weight, state_in,
    state, edge_x1, edge_x2, edge_y1, edge_y2, rows, *, size_y
):
    pos_x, pos_y = lax.axis_index("gx"), lax.axis_index("gy")
    n_tiles = weight.shape[0]
    columns, count, tall = state.shape[0] - 2, state.shape[1], state.shape[2]
    flat = state.reshape(columns + 2, count * tall, BLK)
    for k, part in enumerate((own, first, second)):
        for r in range(CAP):
            rows[k * CAP + r] = part[r]
    for k, part in enumerate((south, north)):
        for r in range(3 * CAP):
            rows[(k + 1) * 3 * CAP + r] = part[r]
    counted = tile_count[0]

    def add_tiles(step, carry):
        for k in range(UNROLL):
            t = step * UNROLL + k
            slot = local_slot(tile_slot[t], pos_x, pos_y, size_y)
            contrib = jnp.dot(rows[slot], weight[t], preferred_element_type=F32)[:count]
            contrib = jnp.where(t < counted, contrib, 0.0)
            x, j = split_device(tile_cell[t], columns)
            at = pl.ds(x + PAD, count, stride=tall)
            flat[j + 1, at, :] = flat[j + 1, at, :] + contrib
        return carry

    lax.fori_loop(0, n_tiles // UNROLL, add_tiles, 0)

    even_x, even_y = (pos_x & 1) == 0, (pos_y & 1) == 0
    top, bottom = tall - PAD - 1, PAD
    line = state.reshape((columns + 2) * count * tall, BLK)
    for edge, row in (
        (edge_x1, jnp.where(even_x, bottom, top)),
        (edge_x2, jnp.where(even_x, top, bottom)),
    ):
        for q in range(count):
            at = pl.ds(count * tall + q * tall + row, columns, stride=count * tall)
            edge[q * columns : (q + 1) * columns, :] = line[at, :].astype(BF16)
    low = low_lanes()
    width = tall - 2 * PAD
    for edge, upper in ((edge_y1, jnp.logical_not(even_y)), (edge_y2, even_y)):
        column = jnp.where(upper, columns, 1)
        for q in range(count // 2):
            for i in range(width // ROWS):
                here = slice(PAD + i * ROWS, PAD + (i + 1) * ROWS)
                a = state[column, q, here, :]
                b = state[column, q + count // 2, here, :]
                both = jnp.where(low, jnp.where(upper, turn(a), a), jnp.where(upper, b, turn(b)))
                edge[q * width + i * ROWS : q * width + (i + 1) * ROWS, :] = both.astype(BF16)


def deposit(tile_slot, tile_cell, tile_count, parts, weight, state, size_y):
    columns, count, tall = state.shape[0] - 2, state.shape[1], state.shape[2]
    edge_x = pltpu.VMEM((count * columns, BLK), BF16)
    edge_y = pltpu.VMEM((count // 2 * (tall - 2 * PAD), BLK), BF16)
    return pl.pallas_call(
        functools.partial(deposit_kernel, size_y=size_y),
        name="deposit",
        out_shape=(pltpu.VMEM(state.shape, F32), edge_x, edge_x, edge_y, edge_y),
        in_specs=[SMEM] * 3 + [VMEM] * 7,
        out_specs=(VMEM,) * 5,
        input_output_aliases={9: 0},
        scratch_shapes=[pltpu.VMEM((9 * CAP, ROWS, BLK), BF16)],
        compiler_params=pltpu.CompilerParams(vmem_limit_bytes=4 * MIB),
    )(tile_slot, tile_cell, tile_count, *parts, weight, state)


def total(terms):
    while len(terms) > 1:
        terms = [a + b for a, b in zip(terms[::2], terms[1::2], strict=True)]
    return terms[0]


def speeds_at(props, state, j, here, parts):
    share = 1.0 / (1.0 + total([props[0, m] * state[j, m, here, :] for m in range(MAT)]))
    found = []
    if 0 in parts:
        found.append((0, state[j, MAT, here, :] * share))
    if 1 in parts:
        along = state[j, MAT + 1, here, :] * share
        found += [(1, along), (2, turn(along))]
    return found


def store_speeds(props, state, speed, places, parts):
    waiting = []
    for step in range(len(places) + DELAY):
        if step < len(places):
            j, first_row = places[step]
            waiting.append(speeds_at(props, state, j, slice(first_row, first_row + 8), parts))
        if step >= DELAY:
            j, first_row = places[step - DELAY]
            for plane, value in waiting.pop(0):
                speed[j, plane, first_row : first_row + 8, :] = value


def weights_at(speed, j, first_row):
    low = low_lanes()
    here = slice(first_row, first_row + 8)
    scale = 0.5 * time_step
    ux = speed[j, 0, here, :]
    lower = scale * (speed[j, 0, slice(first_row - 1, first_row + 7), :] + ux)
    upper = scale * (ux + speed[j, 0, slice(first_row + 1, first_row + 9), :])
    uy, before, after = (speed[k, 1, here, :] for k in (j, j - 1, j + 1))
    turned, turned_before, turned_after = (speed[k, 2, here, :] for k in (j, j - 1, j + 1))
    left = scale * (jnp.where(low, turned_before, turned) + uy)
    right = scale * (uy + jnp.where(low, turned, turned_after))
    keep = 1.0 - (
        (jnp.maximum(upper, 0.0) + jnp.maximum(-lower, 0.0)) + (jnp.maximum(right, 0.0) + jnp.maximum(-left, 0.0))
    )
    take_left = jnp.maximum(scale * (jnp.where(low, uy, before) + turned), 0.0)
    take_right = jnp.maximum(-scale * (turned + jnp.where(low, after, uy)), 0.0)
    same = jnp.where(low, take_left, take_right)
    other = jnp.where(low, take_right, take_left)
    return keep, jnp.maximum(lower, 0.0), jnp.maximum(-upper, 0.0), same, other


def values_at(state, weights, j, first_row, wanted):
    low = low_lanes()
    here = slice(first_row, first_row + 8)
    before = slice(first_row - 1, first_row + 7)
    after = slice(first_row + 1, first_row + 9)
    keep, take_before, take_after, same, other = weights
    values = []
    for q in wanted:
        mid = state[j, q, here, :]
        beside = jnp.where(low, state[j + 1, q, here, :], state[j - 1, q, here, :])
        value = (keep * mid + take_before * state[j, q, before, :]) + take_after * state[j, q, after, :]
        values.append(value + turn(same * mid + other * beside))
    return values


def pressure_of(props, values):
    terms = [value * (props[1, m] + (0.5 * props[1, m]) * value) for m, value in enumerate(values[:MAT])]
    return total(terms) + 0.4 * values[-1]


def remap_tiles(props, state, speed, press, fresh, places, wanted):
    weights, values = {}, {}
    for step in range(len(places) + 2):
        if step < len(places):
            weights[step] = weights_at(speed, *places[step])
        k = step - 1
        if 0 <= k < len(places):
            values[k] = values_at(state, weights.pop(k), *places[k], wanted)
        k = step - 2
        if k >= 0:
            found = values.pop(k)
            j, first_row = places[k]
            inside = slice(first_row - PAD, first_row - PAD + 8)
            lanes = column_lanes(j)
            for q, value in zip(wanted, found, strict=True):
                fresh[q, inside, lanes] = value
            if press is not None:
                press[j - 1, inside, :] = pressure_of(props, found)


def scalars(count):
    return [*range(MAT), count - 1]


def column_lanes(j):
    if isinstance(j, int):
        return slice((j - 1) * BLK, j * BLK)
    return pl.ds(pl.multiple_of((j - 1) * BLK, BLK), BLK)


def inner_kernel(props, state, fresh, press, speed):
    columns, tall = state.shape[0] - 2, state.shape[2]

    def speeds(step, carry):
        rows = range(PAD, tall - PAD, 8)
        places = [(1 + step * GROUP + k, row) for k in range(GROUP) for row in rows]
        store_speeds(props, state, speed, places, (0, 1))
        return carry

    lax.fori_loop(0, columns // GROUP, speeds, 0)

    def remap(step, carry):
        rows = range(PAD + 8, tall - PAD - 8, 8)
        places = [(2 + step * PAIR + k, row) for k in range(PAIR) for row in rows]
        remap_tiles(props, state, speed, press, fresh, places, scalars(state.shape[1]))
        return carry

    lax.fori_loop(0, (columns - 2) // PAIR, remap, 0)


def inner(props, state, width):
    columns, count, tall = state.shape[0] - 2, state.shape[1], state.shape[2]
    return pl.pallas_call(
        inner_kernel,
        name="inner",
        out_shape=(
            pltpu.VMEM((count, width, columns * BLK), F32),
            pltpu.VMEM((columns, width, BLK), F32),
            pltpu.VMEM((columns + 2, 3, tall, BLK), F32),
        ),
        in_specs=[SMEM, VMEM],
        out_specs=(VMEM, VMEM, VMEM),
        compiler_params=pltpu.CompilerParams(vmem_limit_bytes=4 * MIB),
        cost_estimate=pl.CostEstimate(flops=20 * state.size, bytes_accessed=2 * state.size * 4, transcendentals=0),
    )(props, state)


def outer_kernel(
    props, tile_slot, tile_cell, tile_count, edge_x1, edge_x2, edge_y1, edge_y2, weight, state_in, speed_in, press_in,
    fresh_in, state, speed, press, fresh, own, first, second, sums, *, size_x, size_y
):
    pos_x, pos_y = lax.axis_index("gx"), lax.axis_index("gy")
    n_tiles = weight.shape[0]
    columns, count, tall = state.shape[0] - 2, state.shape[1], state.shape[2]
    width = tall - 2 * PAD
    even_x, even_y = (pos_x & 1) == 0, (pos_y & 1) == 0
    line = state.reshape((columns + 2) * count * tall, BLK)
    above, below = tall - PAD, PAD - 1
    for edge, row, there in (
        (edge_x1, jnp.where(even_x, below, above), has_far(pos_x, size_x)),
        (edge_x2, jnp.where(even_x, above, below), True),
    ):
        for q in range(count):
            at = pl.ds(count * tall + q * tall + row, columns, stride=count * tall)
            line[at, :] = jnp.where(there, edge[q * columns : (q + 1) * columns, :].astype(F32), 0.0)
    low = low_lanes()
    for edge, column, there in (
        (edge_y1, jnp.where(even_y, 0, columns + 1), has_far(pos_y, size_y)),
        (edge_y2, jnp.where(even_y, columns + 1, 0), True),
    ):
        for q in range(count // 2):
            for i in range(width // ROWS):
                here = slice(PAD + i * ROWS, PAD + (i + 1) * ROWS)
                both = edge[q * width + i * ROWS : q * width + (i + 1) * ROWS, :].astype(F32)
                both = jnp.where(there, both, 0.0)
                turned = turn(both)
                state[column, q, here, :] = jnp.where(low, both, turned)
                state[column, q + count // 2, here, :] = jnp.where(low, turned, both)

    places = [(j, row) for j in range(1, columns + 1) for row in (0, tall - PAD)]
    store_speeds(props, state, speed, places, (0,))
    places = [(j, row) for j in (0, columns + 1) for row in range(PAD, tall - PAD, 8)]
    store_speeds(props, state, speed, places, (1,))

    def sides(step, carry):
        places = [(1 + step * 2 * PAIR + k, row) for k in range(2 * PAIR) for row in (PAD, tall - PAD - 8)]
        remap_tiles(props, state, speed, press, fresh, places, scalars(state.shape[1]))
        return carry

    lax.fori_loop(0, columns // (2 * PAIR), sides, 0)
    places = [(j, row) for j in (1, columns) for row in range(PAD + 8, tall - PAD - 8, 8)]
    remap_tiles(props, state, speed, press, fresh, places, scalars(state.shape[1]))

    sums[...] = jnp.zeros(sums.shape, F32)
    counted = tile_count[0]
    head = lax.broadcasted_iota(jnp.int32, (ROWS, BLK), 0) == 0

    def sample(step, carry):
        for k in range(UNROLL):
            t = step * UNROLL + k
            slot = local_slot(tile_slot[t], pos_x, pos_y, size_y)
            x, j = split_device(tile_cell[t], columns)
            probe = jnp.where(head, press[j, pl.ds(x, 1), :], 1.0).astype(BF16)
            both = jnp.dot(probe, weight[t], preferred_element_type=F32)[:8]
            sums[slot] = sums[slot] + jnp.where(t < counted, both, 0.0)
        return carry

    lax.fori_loop(0, n_tiles // UNROLL, sample, 0)
    table = sums.reshape(sums.shape[0] * 8, BLK)
    for k, out in enumerate((own, first, second)):
        top = table[pl.ds(k * 3 * CAP * 8, 3 * CAP, stride=8), :]
        under = table[pl.ds(k * 3 * CAP * 8 + 1, 3 * CAP, stride=8), :]
        out[...] = top / jnp.maximum(under, 1.0)


def outer(props, tile_slot, tile_cell, tile_count, edges, weight, state, speed, press, fresh, size_x, size_y):
    answer = pltpu.VMEM((3 * CAP, BLK), F32)
    outs = pl.pallas_call(
        functools.partial(outer_kernel, size_x=size_x, size_y=size_y),
        name="outer",
        out_shape=(
            pltpu.VMEM(state.shape, F32),
            pltpu.VMEM(speed.shape, F32),
            pltpu.VMEM(press.shape, F32),
            pltpu.VMEM(fresh.shape, F32),
            answer,
            answer,
            answer,
        ),
        in_specs=[SMEM] * 4 + [VMEM] * 9,
        out_specs=(VMEM,) * 7,
        input_output_aliases={9: 0, 10: 1, 11: 2, 12: 3},
        scratch_shapes=[pltpu.VMEM((9 * CAP, 8, BLK), F32)],
        compiler_params=pltpu.CompilerParams(vmem_limit_bytes=4 * MIB),
    )(props, tile_slot, tile_cell, tile_count, *edges, weight, state, speed, press, fresh)
    return outs[0], outs[1], outs[3], outs[4], outs[5], outs[6]


def late_kernel(state, speed, fresh_in, remapped, fresh, sem):
    columns, count, tall = state.shape[0] - 2, state.shape[1], state.shape[2]
    moving = range(MAT, count - 1)
    copies = [
        pltpu.make_async_copy(fresh.at[rows], remapped.at[rows], sem.at[k])
        for k, rows in enumerate((pl.ds(0, MAT), pl.ds(count - 1, 1), pl.ds(MAT, count - 1 - MAT)))
    ]
    copies[0].start()
    copies[1].start()

    def remap(step, carry):
        rows = range(PAD, tall - PAD, 8)
        places = [(1 + step * PAIR + k, row) for k in range(PAIR) for row in rows]
        remap_tiles(None, state, speed, None, fresh, places, moving)
        return carry

    lax.fori_loop(0, columns // PAIR, remap, 0)
    copies[2].start()
    for copy in copies:
        copy.wait()


def late(state, speed, fresh):
    return pl.pallas_call(
        late_kernel,
        name="late",
        out_shape=(jax.ShapeDtypeStruct(fresh.shape, F32), pltpu.VMEM(fresh.shape, F32)),
        in_specs=[VMEM] * 3,
        out_specs=(ANY, VMEM),
        input_output_aliases={2: 1},
        scratch_shapes=[pltpu.SemaphoreType.DMA((3,))],
        compiler_params=pltpu.CompilerParams(vmem_limit_bytes=4 * MIB),
        cost_estimate=pl.CostEstimate(flops=5 * state.size, bytes_accessed=2 * state.size * 4, transcendentals=0),
    )(state, speed, fresh)[0]


def pick_kernel(place, own, first, second, out, table, lines):
    for k, part in enumerate((own, first, second)):
        table[k * 3 * CAP : (k + 1) * 3 * CAP, :] = part[...]
    for b in range(out.shape[0]):
        lines[b : b + 1, :] = table[pl.ds(place[b], 1), :]
    out[...] = lines[...].astype(BF16)


def pick(place, own, first, second):
    n_blocks = place.shape[0]
    return pl.pallas_call(
        pick_kernel,
        name="pick",
        out_shape=jax.ShapeDtypeStruct((n_blocks, BLK), BF16),
        in_specs=[SMEM, VMEM, VMEM, VMEM],
        out_specs=VMEM,
        scratch_shapes=[pltpu.VMEM((9 * CAP, BLK), F32), pltpu.VMEM((n_blocks, BLK), F32)],
        compiler_params=pltpu.CompilerParams(vmem_limit_bytes=2 * MIB),
    )(place, own, first, second)


def per_device(
    elem_volume,
    elem_velocity,
    elem_energy,
    elem_mat,
    elem_dest,
    tile_slot,
    tile_cell,
    tile_weight,
    tile_count,
    cell_state,
    mat_props,
):
    size_x, size_y = lax.axis_size("gx"), lax.axis_size("gy")
    n_blocks = elem_dest.shape[0]
    shape = (n_blocks, BLK)
    own, first, second, place = payload(
        elem_dest,
        mat_props,
        elem_volume.reshape(shape),
        elem_velocity,
        elem_energy.reshape(shape),
        elem_mat.reshape(shape),
        size_y,
    )
    weight = fetch(tile_weight)

    first = swap(first, "gx", 1)
    second = swap(second, "gx", 2)
    weight, own = lax.optimization_barrier((weight, own))
    state, turned = stage(cell_state, weight)

    def along_y(which):
        rows = slice(which * CAP, (which + 1) * CAP)
        return jnp.concatenate([own[rows], first[rows], second[rows]], axis=0)

    south = swap(along_y(1), "gy", 1)
    north = swap(along_y(2), "gy", 2)
    state, *edges = deposit(
        tile_slot, tile_cell, tile_count, (own, first, second, south, north), weight, state, size_y
    )
    edges = (
        swap(edges[0], "gx", 1),
        swap(edges[1], "gx", 2),
        swap(edges[2], "gy", 1, wrap=False),
        swap(edges[3], "gy", 2),
    )
    fresh, press, speed = inner(mat_props, state, cell_state.shape[1])
    state, speed, fresh, own, first, second = outer(
        mat_props, tile_slot, tile_cell, tile_count, edges, turned, state, speed, press, fresh, size_x, size_y
    )
    remapped = late(state, speed, fresh)
    first = swap(first, "gy", 1)
    second = swap(second, "gy", 2)

    def along_x(which):
        rows = slice(which * CAP, (which + 1) * CAP)
        return jnp.concatenate([own[rows], first[rows], second[rows]], axis=0)

    back = pick(place, along_x(0), swap(along_x(1), "gx", 1), swap(along_x(2), "gx", 2))
    return remapped, back.reshape(n_blocks * BLK)


def solution(mesh):
    placed = (
        P(("gx", "gy")),
        P(None, ("gx", "gy")),
        P(("gx", "gy")),
        P(("gx", "gy")),
        P(("gx", "gy")),
        P(("gx", "gy")),
        P(("gx", "gy")),
        P(("gx", "gy"), None, None),
        P(("gx", "gy")),
        P(None, "gx", "gy"),
        P(),
    )
    return jax.shard_map(
        per_device,
        mesh=mesh,
        in_specs=placed,
        out_specs=(P(None, "gx", "gy"), P(("gx", "gy"))),
        check_vma=False,
    )
```

```python
import functools

import jax
import jax.numpy as jnp
from jax import lax
from jax.experimental import pallas as pl
from jax.experimental.pallas import tpu as pltpu
from jax.sharding import PartitionSpec as P

MAT = 8
NZ = 64
BLK = 128
CAP = 2
HALF = BLK // 2
PAD = 8
ROWS = 16
UNROLL = 128
PAIR = 2
TURN = 16
GROUP = 8
DELAY = 4
MIB = 2**20

time_step = 0.8
F32 = jnp.float32
BF16 = jnp.bfloat16

SMEM = pl.BlockSpec(memory_space=pltpu.SMEM)
VMEM = pl.BlockSpec(memory_space=pltpu.VMEM)
ANY = pl.BlockSpec(memory_space=pl.ANY)


def partner(index, size, which):
    if which == 2:
        return index ^ 1
    return (index + 1 if index % 2 else index - 1) % size


def swap(value, axis, which):
    size = lax.axis_size(axis)
    return lax.ppermute(value, axis, [(i, partner(i, size, which)) for i in range(size)])


def has_far(index, size):
    return (index > 0) & (index < size - 1)


def code_of(index, mine):
    return jnp.where(index == mine, 0, jnp.where(index == (mine ^ 1), 2, 1))


def split_device(device, size):
    if size & (size - 1) == 0:
        return device >> (size.bit_length() - 1), device & (size - 1)
    return lax.div(device, size), lax.rem(device, size)


def in_hbm(value):
    return pltpu.with_memory_space_constraint(value, pltpu.HBM)


def payload_kernel(
    dest_hbm, props_hbm, volume_hbm, velocity_hbm, energy_hbm, mat_hbm, weight_hbm, own, first, second, place, weight,
    dest, props, volume, velocity, energy, mat, seen, packed, sem, *, size_y
):
    moves = (
        (dest_hbm, dest), (props_hbm, props), (mat_hbm, mat),
        (volume_hbm, volume), (velocity_hbm, velocity), (energy_hbm, energy),
    )
    copies = [pltpu.make_async_copy(src, dst, sem.at[k]) for k, (src, dst) in enumerate(moves)]
    some = pl.ds(0, early_tiles(weight.shape[0]))
    ahead = pltpu.make_async_copy(weight_hbm.at[some], weight.at[some], sem.at[len(moves)])
    for copy in copies:
        copy.start()
    ahead.start()
    for copy in copies:
        copy.wait()
    pos_x, pos_y = lax.axis_index("gx"), lax.axis_index("gy")
    n_blocks = volume.shape[0]
    kinds = mat[...]
    density = jnp.zeros(kinds.shape, F32)
    for m in range(MAT):
        density = jnp.where(kinds == m, props[0, m], density)
    mass = volume[...] * density
    heat = mass * energy[...]
    level = lax.broadcasted_iota(jnp.int32, (MAT, BLK), 0)
    for k in range(9):
        seen[k] = 0
    for b in range(n_blocks):
        at_x, at_y = split_device(dest[b], size_y)
        near = code_of(at_x, pos_x) * 3 + code_of(at_y, pos_y)
        rank = seen[near]
        seen[near] = rank + 1
        slot = near * CAP + rank
        place[b] = slot
        volumes = jnp.where(kinds[b : b + 1] == level, volume[b : b + 1, :], 0.0)
        momentum = mass[b : b + 1] * velocity[:, b * BLK : (b + 1) * BLK]
        rows = jnp.concatenate([volumes, momentum, heat[b : b + 1], jnp.zeros((4, BLK), F32)], axis=0)
        packed[slot] = rows.astype(BF16)
    for k, out in enumerate((own, first, second)):
        for s in range(3 * CAP):
            out[s] = packed[k * 3 * CAP + s]
    ahead.wait()


def early_tiles(n_tiles):
    return n_tiles * 3 // 8


def payload(dest, props, volume, velocity, energy, mat, weight, size_y):
    n_blocks = volume.shape[0]
    parcel = pltpu.VMEM((3 * CAP, ROWS, BLK), BF16)
    return pl.pallas_call(
        functools.partial(payload_kernel, size_y=size_y),
        name="payload",
        out_shape=(
            parcel,
            parcel,
            parcel,
            jax.ShapeDtypeStruct((n_blocks,), jnp.int32),
            pltpu.VMEM(weight.shape, weight.dtype),
        ),
        in_specs=[ANY] * 7,
        out_specs=(VMEM, VMEM, VMEM, SMEM, VMEM),
        scratch_shapes=[
            pltpu.SMEM(dest.shape, jnp.int32),
            pltpu.SMEM(props.shape, F32),
            pltpu.VMEM(volume.shape, F32),
            pltpu.VMEM(velocity.shape, F32),
            pltpu.VMEM(energy.shape, F32),
            pltpu.VMEM(mat.shape, jnp.int32),
            pltpu.SMEM((9,), jnp.int32),
            pltpu.VMEM((9 * CAP, ROWS, BLK), BF16),
            pltpu.SemaphoreType.DMA((7,)),
        ],
        compiler_params=pltpu.CompilerParams(vmem_limit_bytes=4 * MIB),
    )(*(in_hbm(value) for value in (dest, props, volume, velocity, energy, mat, weight)))


def stage_kernel(cell, weight, state, turned, sem):
    columns = state.shape[0] - 2
    width = state.shape[2] - 2 * PAD
    copies = [
        pltpu.make_async_copy(
            cell.at[:, :, pl.ds(j * BLK, BLK)], state.at[j + 1, :, pl.ds(PAD, width)], sem.at[j]
        )
        for j in range(columns)
    ]
    for copy in copies:
        copy.start()

    def transpose(step, carry):
        for k in range(TURN):
            turned[step * TURN + k] = weight[step * TURN + k].T
        return carry

    lax.fori_loop(0, weight.shape[0] // TURN, transpose, 0)
    for copy in copies:
        copy.wait()


def stage(cell, weight):
    count, width, lanes = cell.shape
    columns = lanes // BLK
    return pl.pallas_call(
        stage_kernel,
        name="stage",
        out_shape=(
            pltpu.VMEM((columns + 2, count, width + 2 * PAD, BLK), F32),
            pltpu.VMEM(weight.shape, weight.dtype),
        ),
        in_specs=[ANY, VMEM],
        out_specs=(VMEM, VMEM),
        scratch_shapes=[pltpu.SemaphoreType.DMA((columns,))],
        compiler_params=pltpu.CompilerParams(vmem_limit_bytes=2 * MIB),
        cost_estimate=pl.CostEstimate(flops=0, bytes_accessed=2 * cell.size * 4, transcendentals=0),
    )(in_hbm(cell), weight)


def fetch_kernel(source, target_in, target, sem):
    n_tiles = target.shape[0]
    rest = pl.ds(early_tiles(n_tiles), n_tiles - early_tiles(n_tiles))
    copy = pltpu.make_async_copy(source.at[rest], target.at[rest], sem)
    copy.start()
    copy.wait()


def fetch(value, target):
    return pl.pallas_call(
        fetch_kernel,
        name="fetch",
        out_shape=pltpu.VMEM(value.shape, value.dtype),
        in_specs=[ANY, VMEM],
        out_specs=VMEM,
        input_output_aliases={1: 0},
        scratch_shapes=[pltpu.SemaphoreType.DMA],
        compiler_params=pltpu.CompilerParams(vmem_limit_bytes=2 * MIB),
        cost_estimate=pl.CostEstimate(flops=0, bytes_accessed=2 * value.size * 2, transcendentals=0),
    )(in_hbm(value), target)


def local_slot(slot, pos_x, pos_y, size_y):
    at_x, at_y = split_device(slot >> 1, size_y)
    return code_of(at_y, pos_y) * (3 * CAP) + code_of(at_x, pos_x) * CAP + (slot & 1)


def low_lanes():
    return lax.broadcasted_iota(jnp.int32, (1, BLK), 1) < HALF


def turn(value):
    return pltpu.roll(value, HALF, value.ndim - 1)


def deposit_kernel(
    tile_slot, tile_cell, tile_count, own, first, second, south, north, weight, state_in,
    state, edge_x1, edge_x2, edge_y1, edge_y2, rows, *, size_y
):
    pos_x, pos_y = lax.axis_index("gx"), lax.axis_index("gy")
    n_tiles = weight.shape[0]
    columns, count, tall = state.shape[0] - 2, state.shape[1], state.shape[2]
    flat = state.reshape(columns + 2, count * tall, BLK)
    for k, part in enumerate((own, first, second)):
        for r in range(CAP):
            rows[k * CAP + r] = part[r]
    for k, part in enumerate((south, north)):
        for r in range(3 * CAP):
            rows[(k + 1) * 3 * CAP + r] = part[r]
    counted = tile_count[0]

    def add_tiles(step, carry):
        for k in range(UNROLL):
            t = step * UNROLL + k
            slot = local_slot(tile_slot[t], pos_x, pos_y, size_y)
            contrib = jnp.dot(rows[slot], weight[t], preferred_element_type=F32)[:count]
            contrib = jnp.where(t < counted, contrib, 0.0)
            x, j = split_device(tile_cell[t], columns)
            at = pl.ds(x + PAD, count, stride=tall)
            flat[j + 1, at, :] = flat[j + 1, at, :] + contrib
        return carry

    lax.fori_loop(0, n_tiles // UNROLL, add_tiles, 0)

    even_x, even_y = (pos_x & 1) == 0, (pos_y & 1) == 0
    top, bottom = tall - PAD - 1, PAD
    line = state.reshape((columns + 2) * count * tall, BLK)
    for edge, row in (
        (edge_x1, jnp.where(even_x, bottom, top)),
        (edge_x2, jnp.where(even_x, top, bottom)),
    ):
        for q in range(count):
            at = pl.ds(count * tall + q * tall + row, columns, stride=count * tall)
            edge[q * columns : (q + 1) * columns, :] = line[at, :].astype(BF16)
    low = low_lanes()
    width = tall - 2 * PAD
    for edge, upper in ((edge_y1, jnp.logical_not(even_y)), (edge_y2, even_y)):
        column = jnp.where(upper, columns, 1)
        for q in range(count // 2):
            for i in range(width // ROWS):
                here = slice(PAD + i * ROWS, PAD + (i + 1) * ROWS)
                a = state[column, q, here, :]
                b = state[column, q + count // 2, here, :]
                both = jnp.where(low, jnp.where(upper, turn(a), a), jnp.where(upper, b, turn(b)))
                edge[q * width + i * ROWS : q * width + (i + 1) * ROWS, :] = both.astype(BF16)


def deposit(tile_slot, tile_cell, tile_count, parts, weight, state, size_y):
    columns, count, tall = state.shape[0] - 2, state.shape[1], state.shape[2]
    edge_x = pltpu.VMEM((count * columns, BLK), BF16)
    edge_y = pltpu.VMEM((count // 2 * (tall - 2 * PAD), BLK), BF16)
    return pl.pallas_call(
        functools.partial(deposit_kernel, size_y=size_y),
        name="deposit",
        out_shape=(pltpu.VMEM(state.shape, F32), edge_x, edge_x, edge_y, edge_y),
        in_specs=[SMEM] * 3 + [VMEM] * 7,
        out_specs=(VMEM,) * 5,
        input_output_aliases={9: 0},
        scratch_shapes=[pltpu.VMEM((9 * CAP, ROWS, BLK), BF16)],
        compiler_params=pltpu.CompilerParams(vmem_limit_bytes=4 * MIB),
    )(tile_slot, tile_cell, tile_count, *parts, weight, state)


def total(terms):
    while len(terms) > 1:
        terms = [a + b for a, b in zip(terms[::2], terms[1::2], strict=True)]
    return terms[0]


def speeds_at(props, state, j, here, parts):
    share = 1.0 / (1.0 + total([props[0, m] * state[j, m, here, :] for m in range(MAT)]))
    found = []
    if 0 in parts:
        found.append((0, state[j, MAT, here, :] * share))
    if 1 in parts:
        along = state[j, MAT + 1, here, :] * share
        found += [(1, along), (2, turn(along))]
    return found


def store_speeds(props, state, speed, places, parts):
    waiting = []
    for step in range(len(places) + DELAY):
        if step < len(places):
            j, first_row = places[step]
            waiting.append(speeds_at(props, state, j, slice(first_row, first_row + 8), parts))
        if step >= DELAY:
            j, first_row = places[step - DELAY]
            for plane, value in waiting.pop(0):
                speed[j, plane, first_row : first_row + 8, :] = value


def weights_at(speed, j, first_row):
    low = low_lanes()
    here = slice(first_row, first_row + 8)
    scale = 0.5 * time_step
    ux = speed[j, 0, here, :]
    lower = scale * (speed[j, 0, slice(first_row - 1, first_row + 7), :] + ux)
    upper = scale * (ux + speed[j, 0, slice(first_row + 1, first_row + 9), :])
    uy, before, after = (speed[k, 1, here, :] for k in (j, j - 1, j + 1))
    turned, turned_before, turned_after = (speed[k, 2, here, :] for k in (j, j - 1, j + 1))
    left = scale * (jnp.where(low, turned_before, turned) + uy)
    right = scale * (uy + jnp.where(low, turned, turned_after))
    keep = 1.0 - (
        (jnp.maximum(upper, 0.0) + jnp.maximum(-lower, 0.0)) + (jnp.maximum(right, 0.0) + jnp.maximum(-left, 0.0))
    )
    take_left = jnp.maximum(scale * (jnp.where(low, uy, before) + turned), 0.0)
    take_right = jnp.maximum(-scale * (turned + jnp.where(low, after, uy)), 0.0)
    same = jnp.where(low, take_left, take_right)
    other = jnp.where(low, take_right, take_left)
    return keep, jnp.maximum(lower, 0.0), jnp.maximum(-upper, 0.0), same, other


def values_at(state, weights, j, first_row, wanted):
    low = low_lanes()
    here = slice(first_row, first_row + 8)
    before = slice(first_row - 1, first_row + 7)
    after = slice(first_row + 1, first_row + 9)
    keep, take_before, take_after, same, other = weights
    values = []
    for q in wanted:
        mid = state[j, q, here, :]
        beside = jnp.where(low, state[j + 1, q, here, :], state[j - 1, q, here, :])
        value = (keep * mid + take_before * state[j, q, before, :]) + take_after * state[j, q, after, :]
        values.append(value + turn(same * mid + other * beside))
    return values


def pressure_of(props, values):
    terms = [value * (props[1, m] + (0.5 * props[1, m]) * value) for m, value in enumerate(values[:MAT])]
    return total(terms) + 0.4 * values[-1]


def remap_tiles(props, state, speed, press, fresh, places, wanted):
    weights, values = {}, {}
    for step in range(len(places) + 2):
        if step < len(places):
            weights[step] = weights_at(speed, *places[step])
        k = step - 1
        if 0 <= k < len(places):
            values[k] = values_at(state, weights.pop(k), *places[k], wanted)
        k = step - 2
        if k >= 0:
            found = values.pop(k)
            j, first_row = places[k]
            inside = slice(first_row - PAD, first_row - PAD + 8)
            lanes = column_lanes(j)
            for q, value in zip(wanted, found, strict=True):
                fresh[q, inside, lanes] = value
            if press is not None:
                press[j - 1, inside, :] = pressure_of(props, found)


def scalars(count):
    return [*range(MAT), count - 1]


def column_lanes(j):
    if isinstance(j, int):
        return slice((j - 1) * BLK, j * BLK)
    return pl.ds(pl.multiple_of((j - 1) * BLK, BLK), BLK)


def inner_kernel(props, state, fresh, press, speed):
    columns, tall = state.shape[0] - 2, state.shape[2]

    def speeds(step, carry):
        rows = range(PAD, tall - PAD, 8)
        places = [(1 + step * GROUP + k, row) for k in range(GROUP) for row in rows]
        store_speeds(props, state, speed, places, (0, 1))
        return carry

    lax.fori_loop(0, columns // GROUP, speeds, 0)

    def remap(step, carry):
        rows = range(PAD + 8, tall - PAD - 8, 8)
        places = [(2 + step * PAIR + k, row) for k in range(PAIR) for row in rows]
        remap_tiles(props, state, speed, press, fresh, places, scalars(state.shape[1]))
        return carry

    lax.fori_loop(0, (columns - 2) // PAIR, remap, 0)


def inner(props, state, width):
    columns, count, tall = state.shape[0] - 2, state.shape[1], state.shape[2]
    return pl.pallas_call(
        inner_kernel,
        name="inner",
        out_shape=(
            pltpu.VMEM((count, width, columns * BLK), F32),
            pltpu.VMEM((columns, width, BLK), F32),
            pltpu.VMEM((columns + 2, 3, tall, BLK), F32),
        ),
        in_specs=[SMEM, VMEM],
        out_specs=(VMEM, VMEM, VMEM),
        compiler_params=pltpu.CompilerParams(vmem_limit_bytes=4 * MIB),
        cost_estimate=pl.CostEstimate(flops=20 * state.size, bytes_accessed=2 * state.size * 4, transcendentals=0),
    )(props, state)


def outer_kernel(
    props, tile_slot, tile_cell, tile_count, edge_x1, edge_x2, edge_y1, edge_y2, weight, state_in, speed_in, press_in,
    fresh_in, state, speed, press, fresh, own, first, second, sums, *, size_x, size_y
):
    pos_x, pos_y = lax.axis_index("gx"), lax.axis_index("gy")
    n_tiles = weight.shape[0]
    columns, count, tall = state.shape[0] - 2, state.shape[1], state.shape[2]
    width = tall - 2 * PAD
    even_x, even_y = (pos_x & 1) == 0, (pos_y & 1) == 0
    line = state.reshape((columns + 2) * count * tall, BLK)
    above, below = tall - PAD, PAD - 1
    for edge, row, there in (
        (edge_x1, jnp.where(even_x, below, above), has_far(pos_x, size_x)),
        (edge_x2, jnp.where(even_x, above, below), True),
    ):
        for q in range(count):
            at = pl.ds(count * tall + q * tall + row, columns, stride=count * tall)
            line[at, :] = jnp.where(there, edge[q * columns : (q + 1) * columns, :].astype(F32), 0.0)
    low = low_lanes()
    for edge, column, there in (
        (edge_y1, jnp.where(even_y, 0, columns + 1), has_far(pos_y, size_y)),
        (edge_y2, jnp.where(even_y, columns + 1, 0), True),
    ):
        for q in range(count // 2):
            for i in range(width // ROWS):
                here = slice(PAD + i * ROWS, PAD + (i + 1) * ROWS)
                both = edge[q * width + i * ROWS : q * width + (i + 1) * ROWS, :].astype(F32)
                both = jnp.where(there, both, 0.0)
                turned = turn(both)
                state[column, q, here, :] = jnp.where(low, both, turned)
                state[column, q + count // 2, here, :] = jnp.where(low, turned, both)

    places = [(j, row) for j in range(1, columns + 1) for row in (0, tall - PAD)]
    store_speeds(props, state, speed, places, (0,))
    places = [(j, row) for j in (0, columns + 1) for row in range(PAD, tall - PAD, 8)]
    store_speeds(props, state, speed, places, (1,))

    def sides(step, carry):
        places = [(1 + step * 2 * PAIR + k, row) for k in range(2 * PAIR) for row in (PAD, tall - PAD - 8)]
        remap_tiles(props, state, speed, press, fresh, places, scalars(state.shape[1]))
        return carry

    lax.fori_loop(0, columns // (2 * PAIR), sides, 0)
    places = [(j, row) for j in (1, columns) for row in range(PAD + 8, tall - PAD - 8, 8)]
    remap_tiles(props, state, speed, press, fresh, places, scalars(state.shape[1]))

    sums[...] = jnp.zeros(sums.shape, F32)
    counted = tile_count[0]
    head = lax.broadcasted_iota(jnp.int32, (ROWS, BLK), 0) == 0

    def sample(step, carry):
        for k in range(UNROLL):
            t = step * UNROLL + k
            slot = local_slot(tile_slot[t], pos_x, pos_y, size_y)
            x, j = split_device(tile_cell[t], columns)
            probe = jnp.where(head, press[j, pl.ds(x, 1), :], 1.0).astype(BF16)
            both = jnp.dot(probe, weight[t], preferred_element_type=F32)[:8]
            sums[slot] = sums[slot] + jnp.where(t < counted, both, 0.0)
        return carry

    lax.fori_loop(0, n_tiles // UNROLL, sample, 0)
    table = sums.reshape(sums.shape[0] * 8, BLK)
    for k, out in enumerate((own, first, second)):
        top = table[pl.ds(k * 3 * CAP * 8, 3 * CAP, stride=8), :]
        under = table[pl.ds(k * 3 * CAP * 8 + 1, 3 * CAP, stride=8), :]
        out[...] = top / jnp.maximum(under, 1.0)


def outer(props, tile_slot, tile_cell, tile_count, edges, weight, state, speed, press, fresh, size_x, size_y):
    answer = pltpu.VMEM((3 * CAP, BLK), F32)
    outs = pl.pallas_call(
        functools.partial(outer_kernel, size_x=size_x, size_y=size_y),
        name="outer",
        out_shape=(
            pltpu.VMEM(state.shape, F32),
            pltpu.VMEM(speed.shape, F32),
            pltpu.VMEM(press.shape, F32),
            pltpu.VMEM(fresh.shape, F32),
            answer,
            answer,
            answer,
        ),
        in_specs=[SMEM] * 4 + [VMEM] * 9,
        out_specs=(VMEM,) * 7,
        input_output_aliases={9: 0, 10: 1, 11: 2, 12: 3},
        scratch_shapes=[pltpu.VMEM((9 * CAP, 8, BLK), F32)],
        compiler_params=pltpu.CompilerParams(vmem_limit_bytes=4 * MIB),
    )(props, tile_slot, tile_cell, tile_count, *edges, weight, state, speed, press, fresh)
    return outs[0], outs[1], outs[3], outs[4], outs[5], outs[6]


def late_kernel(state, speed, fresh_in, remapped, fresh, sem):
    columns, count, tall = state.shape[0] - 2, state.shape[1], state.shape[2]
    moving = range(MAT, count - 1)
    copies = [
        pltpu.make_async_copy(fresh.at[rows], remapped.at[rows], sem.at[k])
        for k, rows in enumerate((pl.ds(0, MAT), pl.ds(count - 1, 1), pl.ds(MAT, count - 1 - MAT)))
    ]
    copies[0].start()
    copies[1].start()

    def remap(step, carry):
        rows = range(PAD, tall - PAD, 8)
        places = [(1 + step * PAIR + k, row) for k in range(PAIR) for row in rows]
        remap_tiles(None, state, speed, None, fresh, places, moving)
        return carry

    lax.fori_loop(0, columns // PAIR, remap, 0)
    copies[2].start()
    for copy in copies:
        copy.wait()


def late(state, speed, fresh):
    return pl.pallas_call(
        late_kernel,
        name="late",
        out_shape=(jax.ShapeDtypeStruct(fresh.shape, F32), pltpu.VMEM(fresh.shape, F32)),
        in_specs=[VMEM] * 3,
        out_specs=(ANY, VMEM),
        input_output_aliases={2: 1},
        scratch_shapes=[pltpu.SemaphoreType.DMA((3,))],
        compiler_params=pltpu.CompilerParams(vmem_limit_bytes=4 * MIB),
        cost_estimate=pl.CostEstimate(flops=5 * state.size, bytes_accessed=2 * state.size * 4, transcendentals=0),
    )(state, speed, fresh)[0]


def pick_kernel(place, own, first, second, out, table, lines):
    for k, part in enumerate((own, first, second)):
        table[k * 3 * CAP : (k + 1) * 3 * CAP, :] = part[...]
    for b in range(out.shape[0]):
        lines[b : b + 1, :] = table[pl.ds(place[b], 1), :]
    out[...] = lines[...].astype(BF16)


def pick(place, own, first, second):
    n_blocks = place.shape[0]
    return pl.pallas_call(
        pick_kernel,
        name="pick",
        out_shape=jax.ShapeDtypeStruct((n_blocks, BLK), BF16),
        in_specs=[SMEM, VMEM, VMEM, VMEM],
        out_specs=VMEM,
        scratch_shapes=[pltpu.VMEM((9 * CAP, BLK), F32), pltpu.VMEM((n_blocks, BLK), F32)],
        compiler_params=pltpu.CompilerParams(vmem_limit_bytes=2 * MIB),
    )(place, own, first, second)


def per_device(
    elem_volume,
    elem_velocity,
    elem_energy,
    elem_mat,
    elem_dest,
    tile_slot,
    tile_cell,
    tile_weight,
    tile_count,
    cell_state,
    mat_props,
):
    size_x, size_y = lax.axis_size("gx"), lax.axis_size("gy")
    n_blocks = elem_dest.shape[0]
    shape = (n_blocks, BLK)
    own, first, second, place, weight = payload(
        elem_dest,
        mat_props,
        elem_volume.reshape(shape),
        elem_velocity,
        elem_energy.reshape(shape),
        elem_mat.reshape(shape),
        tile_weight,
        size_y,
    )
    weight = fetch(tile_weight, weight)

    first = swap(first, "gx", 1)
    second = swap(second, "gx", 2)
    weight, own = lax.optimization_barrier((weight, own))
    state, turned = stage(cell_state, weight)

    def along_y(which):
        rows = slice(which * CAP, (which + 1) * CAP)
        return jnp.concatenate([own[rows], first[rows], second[rows]], axis=0)

    south = swap(along_y(1), "gy", 1)
    north = swap(along_y(2), "gy", 2)
    state, *edges = deposit(
        tile_slot, tile_cell, tile_count, (own, first, second, south, north), weight, state, size_y
    )
    edges = (
        swap(edges[0], "gx", 1),
        swap(edges[1], "gx", 2),
        swap(edges[2], "gy", 1),
        swap(edges[3], "gy", 2),
    )
    fresh, press, speed = inner(mat_props, state, cell_state.shape[1])
    state, speed, fresh, own, first, second = outer(
        mat_props, tile_slot, tile_cell, tile_count, edges, turned, state, speed, press, fresh, size_x, size_y
    )
    remapped = late(state, speed, fresh)
    first = swap(first, "gy", 1)
    second = swap(second, "gy", 2)

    def along_x(which):
        rows = slice(which * CAP, (which + 1) * CAP)
        return jnp.concatenate([own[rows], first[rows], second[rows]], axis=0)

    back = pick(place, along_x(0), swap(along_x(1), "gx", 1), swap(along_x(2), "gx", 2))
    return remapped, back.reshape(n_blocks * BLK)


def solution(mesh):
    placed = (
        P(("gx", "gy")),
        P(None, ("gx", "gy")),
        P(("gx", "gy")),
        P(("gx", "gy")),
        P(("gx", "gy")),
        P(("gx", "gy")),
        P(("gx", "gy")),
        P(("gx", "gy"), None, None),
        P(("gx", "gy")),
        P(None, "gx", "gy"),
        P(),
    )
    return jax.shard_map(
        per_device,
        mesh=mesh,
        in_specs=placed,
        out_specs=(P(None, "gx", "gy"), P(("gx", "gy"))),
        check_vma=False,
    )
```

```python
import functools

import jax
import jax.numpy as jnp
from jax import lax
from jax.experimental import pallas as pl
from jax.experimental.pallas import tpu as pltpu
from jax.sharding import PartitionSpec as P

MAT = 8
NZ = 64
BLK = 128
CAP = 2
HALF = BLK // 2
PAD = 8
ROWS = 16
UNROLL = 128
PAIR = 2
TURN = 16
GROUP = 8
DELAY = 4
MIB = 2**20

time_step = 0.8
F32 = jnp.float32
BF16 = jnp.bfloat16

SMEM = pl.BlockSpec(memory_space=pltpu.SMEM)
VMEM = pl.BlockSpec(memory_space=pltpu.VMEM)
ANY = pl.BlockSpec(memory_space=pl.ANY)


def partner(index, size, which):
    if which == 2:
        return index ^ 1
    return (index + 1 if index % 2 else index - 1) % size


def swap(value, axis, which, wrap=True):
    size = lax.axis_size(axis)
    pairs = [(i, partner(i, size, which)) for i in range(size)]
    if not wrap:
        pairs = [(i, j if abs(i - j) == 1 else i) for i, j in pairs]
    return lax.ppermute(value, axis, pairs)


def has_far(index, size):
    return (index > 0) & (index < size - 1)


def code_of(index, mine):
    return jnp.where(index == mine, 0, jnp.where(index == (mine ^ 1), 2, 1))


def split_device(device, size):
    if size & (size - 1) == 0:
        return device >> (size.bit_length() - 1), device & (size - 1)
    return lax.div(device, size), lax.rem(device, size)


def in_hbm(value):
    return pltpu.with_memory_space_constraint(value, pltpu.HBM)


def payload_kernel(
    dest_hbm, props_hbm, volume_hbm, velocity_hbm, energy_hbm, mat_hbm, slot_hbm, cell_hbm,
    own, first, second, place, props, slot_out, cell_out, dest, volume, velocity, energy, mat, seen, packed, sem, *, size_y
):
    moves = (
        (dest_hbm, dest), (props_hbm, props), (mat_hbm, mat),
        (volume_hbm, volume), (velocity_hbm, velocity), (energy_hbm, energy),
        (slot_hbm, slot_out), (cell_hbm, cell_out),
    )
    copies = [pltpu.make_async_copy(src, dst, sem.at[k]) for k, (src, dst) in enumerate(moves)]
    for copy in copies:
        copy.start()
    for copy in copies:
        copy.wait()
    pos_x, pos_y = lax.axis_index("gx"), lax.axis_index("gy")
    n_blocks = volume.shape[0]
    kinds = mat[...]
    density = jnp.zeros(kinds.shape, F32)
    for m in range(MAT):
        density = jnp.where(kinds == m, props[0, m], density)
    mass = volume[...] * density
    heat = mass * energy[...]
    level = lax.broadcasted_iota(jnp.int32, (MAT, BLK), 0)
    for k in range(9):
        seen[k] = 0
    for b in range(n_blocks):
        at_x, at_y = split_device(dest[b], size_y)
        near = code_of(at_x, pos_x) * 3 + code_of(at_y, pos_y)
        rank = seen[near]
        seen[near] = rank + 1
        slot = near * CAP + rank
        place[b] = slot
        volumes = jnp.where(kinds[b : b + 1] == level, volume[b : b + 1, :], 0.0)
        momentum = mass[b : b + 1] * velocity[:, b * BLK : (b + 1) * BLK]
        rows = jnp.concatenate([volumes, momentum, heat[b : b + 1], jnp.zeros((4, BLK), F32)], axis=0)
        packed[slot] = rows.astype(BF16)
    for k, out in enumerate((own, first, second)):
        for s in range(3 * CAP):
            out[s] = packed[k * 3 * CAP + s]


def payload(dest, props, volume, velocity, energy, mat, tile_slot, tile_cell, size_y):
    n_blocks = volume.shape[0]
    parcel = pltpu.VMEM((3 * CAP, ROWS, BLK), BF16)
    return pl.pallas_call(
        functools.partial(payload_kernel, size_y=size_y),
        name="payload",
        out_shape=(
            parcel,
            parcel,
            parcel,
            pltpu.SMEM((n_blocks,), jnp.int32),
            pltpu.SMEM(props.shape, F32),
            pltpu.SMEM(tile_slot.shape, jnp.int32),
            pltpu.SMEM(tile_cell.shape, jnp.int32),
        ),
        in_specs=[ANY] * 8,
        out_specs=(VMEM, VMEM, VMEM, SMEM, SMEM, SMEM, SMEM),
        scratch_shapes=[
            pltpu.SMEM(dest.shape, jnp.int32),
            pltpu.VMEM(volume.shape, F32),
            pltpu.VMEM(velocity.shape, F32),
            pltpu.VMEM(energy.shape, F32),
            pltpu.VMEM(mat.shape, jnp.int32),
            pltpu.SMEM((9,), jnp.int32),
            pltpu.VMEM((9 * CAP, ROWS, BLK), BF16),
            pltpu.SemaphoreType.DMA((8,)),
        ],
        compiler_params=pltpu.CompilerParams(vmem_limit_bytes=4 * MIB),
    )(*(in_hbm(value) for value in (dest, props, volume, velocity, energy, mat, tile_slot, tile_cell)))


def stage_kernel(cell, weight, state, turned, sem):
    columns = state.shape[0] - 2
    width = state.shape[2] - 2 * PAD
    copies = [
        pltpu.make_async_copy(
            cell.at[:, :, pl.ds(j * BLK, BLK)], state.at[j + 1, :, pl.ds(PAD, width)], sem.at[j]
        )
        for j in range(columns)
    ]
    for copy in copies:
        copy.start()

    def transpose(step, carry):
        for k in range(TURN):
            turned[step * TURN + k] = weight[step * TURN + k].T
        return carry

    lax.fori_loop(0, weight.shape[0] // TURN, transpose, 0)
    for copy in copies:
        copy.wait()


def stage(cell, weight):
    count, width, lanes = cell.shape
    columns = lanes // BLK
    return pl.pallas_call(
        stage_kernel,
        name="stage",
        out_shape=(
            pltpu.VMEM((columns + 2, count, width + 2 * PAD, BLK), F32),
            pltpu.VMEM(weight.shape, weight.dtype),
        ),
        in_specs=[ANY, VMEM],
        out_specs=(VMEM, VMEM),
        scratch_shapes=[pltpu.SemaphoreType.DMA((columns,))],
        compiler_params=pltpu.CompilerParams(vmem_limit_bytes=2 * MIB),
        cost_estimate=pl.CostEstimate(flops=0, bytes_accessed=2 * cell.size * 4, transcendentals=0),
    )(in_hbm(cell), weight)


def fetch_kernel(source, target, sem):
    copy = pltpu.make_async_copy(source, target, sem)
    copy.start()
    copy.wait()


def fetch(value):
    return pl.pallas_call(
        fetch_kernel,
        name="fetch",
        out_shape=pltpu.VMEM(value.shape, value.dtype),
        in_specs=[ANY],
        out_specs=VMEM,
        scratch_shapes=[pltpu.SemaphoreType.DMA],
        compiler_params=pltpu.CompilerParams(vmem_limit_bytes=2 * MIB),
        cost_estimate=pl.CostEstimate(flops=0, bytes_accessed=2 * value.size * 2, transcendentals=0),
    )(in_hbm(value))


def local_slot(slot, pos_x, pos_y, size_y):
    at_x, at_y = split_device(slot >> 1, size_y)
    return code_of(at_y, pos_y) * (3 * CAP) + code_of(at_x, pos_x) * CAP + (slot & 1)


def low_lanes():
    return lax.broadcasted_iota(jnp.int32, (1, BLK), 1) < HALF


def turn(value):
    return pltpu.roll(value, HALF, value.ndim - 1)


def deposit_kernel(
    tile_slot, tile_cell, tile_count, own, first, second, south, north, weight, state_in,
    state, edge_x1, edge_x2, edge_y1, edge_y2, rows, *, size_y
):
    pos_x, pos_y = lax.axis_index("gx"), lax.axis_index("gy")
    n_tiles = weight.shape[0]
    columns, count, tall = state.shape[0] - 2, state.shape[1], state.shape[2]
    flat = state.reshape(columns + 2, count * tall, BLK)
    for k, part in enumerate((own, first, second)):
        for r in range(CAP):
            rows[k * CAP + r] = part[r]
    for k, part in enumerate((south, north)):
        for r in range(3 * CAP):
            rows[(k + 1) * 3 * CAP + r] = part[r]
    counted = tile_count[0]

    def add_tiles(step, carry):
        for k in range(UNROLL):
            t = step * UNROLL + k
            slot = local_slot(tile_slot[t], pos_x, pos_y, size_y)
            contrib = jnp.dot(rows[slot], weight[t], preferred_element_type=F32)[:count]
            contrib = jnp.where(t < counted, contrib, 0.0)
            x, j = split_device(tile_cell[t], columns)
            at = pl.ds(x + PAD, count, stride=tall)
            flat[j + 1, at, :] = flat[j + 1, at, :] + contrib
        return carry

    lax.fori_loop(0, n_tiles // UNROLL, add_tiles, 0)

    even_x, even_y = (pos_x & 1) == 0, (pos_y & 1) == 0
    top, bottom = tall - PAD - 1, PAD
    line = state.reshape((columns + 2) * count * tall, BLK)
    for edge, row in (
        (edge_x1, jnp.where(even_x, bottom, top)),
        (edge_x2, jnp.where(even_x, top, bottom)),
    ):
        for q in range(count):
            at = pl.ds(count * tall + q * tall + row, columns, stride=count * tall)
            edge[q * columns : (q + 1) * columns, :] = line[at, :].astype(BF16)
    low = low_lanes()
    width = tall - 2 * PAD
    for edge, upper in ((edge_y1, jnp.logical_not(even_y)), (edge_y2, even_y)):
        column = jnp.where(upper, columns, 1)
        for q in range(count // 2):
            for i in range(width // ROWS):
                here = slice(PAD + i * ROWS, PAD + (i + 1) * ROWS)
                a = state[column, q, here, :]
                b = state[column, q + count // 2, here, :]
                both = jnp.where(low, jnp.where(upper, turn(a), a), jnp.where(upper, b, turn(b)))
                edge[q * width + i * ROWS : q * width + (i + 1) * ROWS, :] = both.astype(BF16)


def deposit(tile_slot, tile_cell, tile_count, parts, weight, state, size_y):
    columns, count, tall = state.shape[0] - 2, state.shape[1], state.shape[2]
    edge_x = pltpu.VMEM((count * columns, BLK), BF16)
    edge_y = pltpu.VMEM((count // 2 * (tall - 2 * PAD), BLK), BF16)
    return pl.pallas_call(
        functools.partial(deposit_kernel, size_y=size_y),
        name="deposit",
        out_shape=(pltpu.VMEM(state.shape, F32), edge_x, edge_x, edge_y, edge_y),
        in_specs=[SMEM] * 3 + [VMEM] * 7,
        out_specs=(VMEM,) * 5,
        input_output_aliases={9: 0},
        scratch_shapes=[pltpu.VMEM((9 * CAP, ROWS, BLK), BF16)],
        compiler_params=pltpu.CompilerParams(vmem_limit_bytes=4 * MIB),
    )(tile_slot, tile_cell, tile_count, *parts, weight, state)


def total(terms):
    while len(terms) > 1:
        terms = [a + b for a, b in zip(terms[::2], terms[1::2], strict=True)]
    return terms[0]


def speeds_at(props, state, j, here, parts):
    share = 1.0 / (1.0 + total([props[0, m] * state[j, m, here, :] for m in range(MAT)]))
    found = []
    if 0 in parts:
        found.append((0, state[j, MAT, here, :] * share))
    if 1 in parts:
        along = state[j, MAT + 1, here, :] * share
        found += [(1, along), (2, turn(along))]
    return found


def store_speeds(props, state, speed, places, parts):
    waiting = []
    for step in range(len(places) + DELAY):
        if step < len(places):
            j, first_row = places[step]
            waiting.append(speeds_at(props, state, j, slice(first_row, first_row + 8), parts))
        if step >= DELAY:
            j, first_row = places[step - DELAY]
            for plane, value in waiting.pop(0):
                speed[j, plane, first_row : first_row + 8, :] = value


def weights_at(speed, j, first_row):
    low = low_lanes()
    here = slice(first_row, first_row + 8)
    scale = 0.5 * time_step
    ux = speed[j, 0, here, :]
    lower = scale * (speed[j, 0, slice(first_row - 1, first_row + 7), :] + ux)
    upper = scale * (ux + speed[j, 0, slice(first_row + 1, first_row + 9), :])
    uy, before, after = (speed[k, 1, here, :] for k in (j, j - 1, j + 1))
    turned, turned_before, turned_after = (speed[k, 2, here, :] for k in (j, j - 1, j + 1))
    left = scale * (jnp.where(low, turned_before, turned) + uy)
    right = scale * (uy + jnp.where(low, turned, turned_after))
    keep = 1.0 - (
        (jnp.maximum(upper, 0.0) + jnp.maximum(-lower, 0.0)) + (jnp.maximum(right, 0.0) + jnp.maximum(-left, 0.0))
    )
    take_left = jnp.maximum(scale * (jnp.where(low, uy, before) + turned), 0.0)
    take_right = jnp.maximum(-scale * (turned + jnp.where(low, after, uy)), 0.0)
    same = jnp.where(low, take_left, take_right)
    other = jnp.where(low, take_right, take_left)
    return keep, jnp.maximum(lower, 0.0), jnp.maximum(-upper, 0.0), same, other


def values_at(state, weights, j, first_row, wanted):
    low = low_lanes()
    here = slice(first_row, first_row + 8)
    before = slice(first_row - 1, first_row + 7)
    after = slice(first_row + 1, first_row + 9)
    keep, take_before, take_after, same, other = weights
    values = []
    for q in wanted:
        mid = state[j, q, here, :]
        beside = jnp.where(low, state[j + 1, q, here, :], state[j - 1, q, here, :])
        value = (keep * mid + take_before * state[j, q, before, :]) + take_after * state[j, q, after, :]
        values.append(value + turn(same * mid + other * beside))
    return values


def pressure_of(props, values):
    terms = [value * (props[1, m] + (0.5 * props[1, m]) * value) for m, value in enumerate(values[:MAT])]
    return total(terms) + 0.4 * values[-1]


def remap_tiles(props, state, speed, press, fresh, places, wanted):
    weights, values = {}, {}
    for step in range(len(places) + 2):
        if step < len(places):
            weights[step] = weights_at(speed, *places[step])
        k = step - 1
        if 0 <= k < len(places):
            values[k] = values_at(state, weights.pop(k), *places[k], wanted)
        k = step - 2
        if k >= 0:
            found = values.pop(k)
            j, first_row = places[k]
            inside = slice(first_row - PAD, first_row - PAD + 8)
            lanes = column_lanes(j)
            for q, value in zip(wanted, found, strict=True):
                fresh[q, inside, lanes] = value
            if press is not None:
                press[j - 1, inside, :] = pressure_of(props, found)


def scalars(count):
    return [*range(MAT), count - 1]


def column_lanes(j):
    if isinstance(j, int):
        return slice((j - 1) * BLK, j * BLK)
    return pl.ds(pl.multiple_of((j - 1) * BLK, BLK), BLK)


def inner_kernel(props, state, fresh, press, speed):
    columns, tall = state.shape[0] - 2, state.shape[2]

    def speeds(step, carry):
        rows = range(PAD, tall - PAD, 8)
        places = [(1 + step * GROUP + k, row) for k in range(GROUP) for row in rows]
        store_speeds(props, state, speed, places, (0, 1))
        return carry

    lax.fori_loop(0, columns // GROUP, speeds, 0)

    def remap(step, carry):
        rows = range(PAD + 8, tall - PAD - 8, 8)
        places = [(2 + step * PAIR + k, row) for k in range(PAIR) for row in rows]
        remap_tiles(props, state, speed, press, fresh, places, scalars(state.shape[1]))
        return carry

    lax.fori_loop(0, (columns - 2) // PAIR, remap, 0)


def inner(props, state, width):
    columns, count, tall = state.shape[0] - 2, state.shape[1], state.shape[2]
    return pl.pallas_call(
        inner_kernel,
        name="inner",
        out_shape=(
            pltpu.VMEM((count, width, columns * BLK), F32),
            pltpu.VMEM((columns, width, BLK), F32),
            pltpu.VMEM((columns + 2, 3, tall, BLK), F32),
        ),
        in_specs=[SMEM, VMEM],
        out_specs=(VMEM, VMEM, VMEM),
        compiler_params=pltpu.CompilerParams(vmem_limit_bytes=4 * MIB),
        cost_estimate=pl.CostEstimate(flops=20 * state.size, bytes_accessed=2 * state.size * 4, transcendentals=0),
    )(props, state)


def outer_kernel(
    props, tile_slot, tile_cell, tile_count, edge_x1, edge_x2, edge_y1, edge_y2, weight, state_in, speed_in, press_in,
    fresh_in, state, speed, press, fresh, own, first, second, sums, *, size_x, size_y
):
    pos_x, pos_y = lax.axis_index("gx"), lax.axis_index("gy")
    n_tiles = weight.shape[0]
    columns, count, tall = state.shape[0] - 2, state.shape[1], state.shape[2]
    width = tall - 2 * PAD
    even_x, even_y = (pos_x & 1) == 0, (pos_y & 1) == 0
    line = state.reshape((columns + 2) * count * tall, BLK)
    above, below = tall - PAD, PAD - 1
    for edge, row, there in (
        (edge_x1, jnp.where(even_x, below, above), has_far(pos_x, size_x)),
        (edge_x2, jnp.where(even_x, above, below), True),
    ):
        for q in range(count):
            at = pl.ds(count * tall + q * tall + row, columns, stride=count * tall)
            line[at, :] = jnp.where(there, edge[q * columns : (q + 1) * columns, :].astype(F32), 0.0)
    low = low_lanes()
    for edge, column, there in (
        (edge_y1, jnp.where(even_y, 0, columns + 1), has_far(pos_y, size_y)),
        (edge_y2, jnp.where(even_y, columns + 1, 0), True),
    ):
        for q in range(count // 2):
            for i in range(width // ROWS):
                here = slice(PAD + i * ROWS, PAD + (i + 1) * ROWS)
                both = edge[q * width + i * ROWS : q * width + (i + 1) * ROWS, :].astype(F32)
                both = jnp.where(there, both, 0.0)
                turned = turn(both)
                state[column, q, here, :] = jnp.where(low, both, turned)
                state[column, q + count // 2, here, :] = jnp.where(low, turned, both)

    places = [(j, row) for j in range(1, columns + 1) for row in (0, tall - PAD)]
    store_speeds(props, state, speed, places, (0,))
    places = [(j, row) for j in (0, columns + 1) for row in range(PAD, tall - PAD, 8)]
    store_speeds(props, state, speed, places, (1,))

    def sides(step, carry):
        places = [(1 + step * 2 * PAIR + k, row) for k in range(2 * PAIR) for row in (PAD, tall - PAD - 8)]
        remap_tiles(props, state, speed, press, fresh, places, scalars(state.shape[1]))
        return carry

    lax.fori_loop(0, columns // (2 * PAIR), sides, 0)
    places = [(j, row) for j in (1, columns) for row in range(PAD + 8, tall - PAD - 8, 8)]
    remap_tiles(props, state, speed, press, fresh, places, scalars(state.shape[1]))

    sums[...] = jnp.zeros(sums.shape, F32)
    counted = tile_count[0]
    head = lax.broadcasted_iota(jnp.int32, (ROWS, BLK), 0) == 0

    def sample(step, carry):
        for k in range(UNROLL):
            t = step * UNROLL + k
            slot = local_slot(tile_slot[t], pos_x, pos_y, size_y)
            x, j = split_device(tile_cell[t], columns)
            probe = jnp.where(head, press[j, pl.ds(x, 1), :], 1.0).astype(BF16)
            both = jnp.dot(probe, weight[t], preferred_element_type=F32)[:8]
            sums[slot] = sums[slot] + jnp.where(t < counted, both, 0.0)
        return carry

    lax.fori_loop(0, n_tiles // UNROLL, sample, 0)
    table = sums.reshape(sums.shape[0] * 8, BLK)
    for k, out in enumerate((own, first, second)):
        top = table[pl.ds(k * 3 * CAP * 8, 3 * CAP, stride=8), :]
        under = table[pl.ds(k * 3 * CAP * 8 + 1, 3 * CAP, stride=8), :]
        out[...] = top / jnp.maximum(under, 1.0)


def outer(props, tile_slot, tile_cell, tile_count, edges, weight, state, speed, press, fresh, size_x, size_y):
    answer = pltpu.VMEM((3 * CAP, BLK), F32)
    outs = pl.pallas_call(
        functools.partial(outer_kernel, size_x=size_x, size_y=size_y),
        name="outer",
        out_shape=(
            pltpu.VMEM(state.shape, F32),
            pltpu.VMEM(speed.shape, F32),
            pltpu.VMEM(press.shape, F32),
            pltpu.VMEM(fresh.shape, F32),
            answer,
            answer,
            answer,
        ),
        in_specs=[SMEM] * 4 + [VMEM] * 9,
        out_specs=(VMEM,) * 7,
        input_output_aliases={9: 0, 10: 1, 11: 2, 12: 3},
        scratch_shapes=[pltpu.VMEM((9 * CAP, 8, BLK), F32)],
        compiler_params=pltpu.CompilerParams(vmem_limit_bytes=4 * MIB),
    )(props, tile_slot, tile_cell, tile_count, *edges, weight, state, speed, press, fresh)
    return outs[0], outs[1], outs[3], outs[4], outs[5], outs[6]


def late_kernel(state, speed, fresh_in, remapped, fresh, sem):
    columns, count, tall = state.shape[0] - 2, state.shape[1], state.shape[2]
    moving = range(MAT, count - 1)
    copies = [
        pltpu.make_async_copy(fresh.at[rows], remapped.at[rows], sem.at[k])
        for k, rows in enumerate((pl.ds(0, MAT), pl.ds(count - 1, 1), pl.ds(MAT, count - 1 - MAT)))
    ]
    copies[0].start()
    copies[1].start()

    def remap(step, carry):
        rows = range(PAD, tall - PAD, 8)
        places = [(1 + step * PAIR + k, row) for k in range(PAIR) for row in rows]
        remap_tiles(None, state, speed, None, fresh, places, moving)
        return carry

    lax.fori_loop(0, columns // PAIR, remap, 0)
    copies[2].start()
    for copy in copies:
        copy.wait()


def late(state, speed, fresh):
    return pl.pallas_call(
        late_kernel,
        name="late",
        out_shape=(jax.ShapeDtypeStruct(fresh.shape, F32), pltpu.VMEM(fresh.shape, F32)),
        in_specs=[VMEM] * 3,
        out_specs=(ANY, VMEM),
        input_output_aliases={2: 1},
        scratch_shapes=[pltpu.SemaphoreType.DMA((3,))],
        compiler_params=pltpu.CompilerParams(vmem_limit_bytes=4 * MIB),
        cost_estimate=pl.CostEstimate(flops=5 * state.size, bytes_accessed=2 * state.size * 4, transcendentals=0),
    )(state, speed, fresh)[0]


def pick_kernel(place, own, first, second, out, table, lines):
    for k, part in enumerate((own, first, second)):
        table[k * 3 * CAP : (k + 1) * 3 * CAP, :] = part[...]
    for b in range(out.shape[0]):
        lines[b : b + 1, :] = table[pl.ds(place[b], 1), :]
    out[...] = lines[...].astype(BF16)


def pick(place, own, first, second):
    n_blocks = place.shape[0]
    return pl.pallas_call(
        pick_kernel,
        name="pick",
        out_shape=jax.ShapeDtypeStruct((n_blocks, BLK), BF16),
        in_specs=[SMEM, VMEM, VMEM, VMEM],
        out_specs=VMEM,
        scratch_shapes=[pltpu.VMEM((9 * CAP, BLK), F32), pltpu.VMEM((n_blocks, BLK), F32)],
        compiler_params=pltpu.CompilerParams(vmem_limit_bytes=2 * MIB),
    )(place, own, first, second)


def per_device(
    elem_volume,
    elem_velocity,
    elem_energy,
    elem_mat,
    elem_dest,
    tile_slot,
    tile_cell,
    tile_weight,
    tile_count,
    cell_state,
    mat_props,
):
    size_x, size_y = lax.axis_size("gx"), lax.axis_size("gy")
    n_blocks = elem_dest.shape[0]
    shape = (n_blocks, BLK)
    own, first, second, place, mat_props, tile_slot, tile_cell = payload(
        elem_dest,
        mat_props,
        elem_volume.reshape(shape),
        elem_velocity,
        elem_energy.reshape(shape),
        elem_mat.reshape(shape),
        tile_slot,
        tile_cell,
        size_y,
    )
    weight = fetch(tile_weight)

    first = swap(first, "gx", 1)
    second = swap(second, "gx", 2)
    weight, own = lax.optimization_barrier((weight, own))
    state, turned = stage(cell_state, weight)

    def along_y(which):
        rows = slice(which * CAP, (which + 1) * CAP)
        return jnp.concatenate([own[rows], first[rows], second[rows]], axis=0)

    south = swap(along_y(1), "gy", 1)
    north = swap(along_y(2), "gy", 2)
    state, *edges = deposit(
        tile_slot, tile_cell, tile_count, (own, first, second, south, north), weight, state, size_y
    )
    edges = (
        swap(edges[0], "gx", 1),
        swap(edges[1], "gx", 2),
        swap(edges[2], "gy", 1, wrap=False),
        swap(edges[3], "gy", 2),
    )
    fresh, press, speed = inner(mat_props, state, cell_state.shape[1])
    state, speed, fresh, own, first, second = outer(
        mat_props, tile_slot, tile_cell, tile_count, edges, turned, state, speed, press, fresh, size_x, size_y
    )
    remapped = late(state, speed, fresh)
    first = swap(first, "gy", 1)
    second = swap(second, "gy", 2)

    def along_x(which):
        rows = slice(which * CAP, (which + 1) * CAP)
        return jnp.concatenate([own[rows], first[rows], second[rows]], axis=0)

    back = pick(place, along_x(0), swap(along_x(1), "gx", 1), swap(along_x(2), "gx", 2))
    return remapped, back.reshape(n_blocks * BLK)


def solution(mesh):
    placed = (
        P(("gx", "gy")),
        P(None, ("gx", "gy")),
        P(("gx", "gy")),
        P(("gx", "gy")),
        P(("gx", "gy")),
        P(("gx", "gy")),
        P(("gx", "gy")),
        P(("gx", "gy"), None, None),
        P(("gx", "gy")),
        P(None, "gx", "gy"),
        P(),
    )
    return jax.shard_map(
        per_device,
        mesh=mesh,
        in_specs=placed,
        out_specs=(P(None, "gx", "gy"), P(("gx", "gy"))),
        check_vma=False,
    )
```

```python
import functools

import jax
import jax.numpy as jnp
from jax import lax
from jax.experimental import pallas as pl
from jax.experimental.pallas import tpu as pltpu
from jax.sharding import PartitionSpec as P

MAT = 8
NZ = 64
BLK = 128
CAP = 2
HALF = BLK // 2
PAD = 8
AFTER = 16
ROOM = PAD + AFTER
ROWS = 16
PAIR = 2
TOGETHER = 4
PARTS = 4
TURN = 16
GROUP = 8
DELAY = 4
MIB = 2**20

time_step = 0.8
F32 = jnp.float32
BF16 = jnp.bfloat16

SMEM = pl.BlockSpec(memory_space=pltpu.SMEM)
VMEM = pl.BlockSpec(memory_space=pltpu.VMEM)
ANY = pl.BlockSpec(memory_space=pl.ANY)


def partner(index, size, which):
    if which == 2:
        return index ^ 1
    return (index + 1 if index % 2 else index - 1) % size


def swap(value, axis, which, wrap=True):
    size = lax.axis_size(axis)
    pairs = [(i, partner(i, size, which)) for i in range(size)]
    if not wrap:
        pairs = [(i, j if abs(i - j) == 1 else i) for i, j in pairs]
    return lax.ppermute(value, axis, pairs)


def has_far(index, size):
    return (index > 0) & (index < size - 1)


def code_of(index, mine):
    return jnp.where(index == mine, 0, jnp.where(index == (mine ^ 1), 2, 1))


def split_device(device, size):
    if size & (size - 1) == 0:
        return device >> (size.bit_length() - 1), device & (size - 1)
    return lax.div(device, size), lax.rem(device, size)


def in_hbm(value):
    return pltpu.with_memory_space_constraint(value, pltpu.HBM)


def payload_kernel(
    dest_hbm, props_hbm, volume_hbm, velocity_hbm, energy_hbm, mat_hbm, slot_hbm, cell_hbm,
    own, first, second, place, props, slot_out, cell_out, dest, volume, velocity, energy, mat, seen, packed, sem, *, size_y
):
    moves = (
        (dest_hbm, dest), (props_hbm, props), (mat_hbm, mat),
        (volume_hbm, volume), (velocity_hbm, velocity), (energy_hbm, energy),
        (slot_hbm, slot_out), (cell_hbm, cell_out),
    )
    copies = [pltpu.make_async_copy(src, dst, sem.at[k]) for k, (src, dst) in enumerate(moves)]
    for copy in copies:
        copy.start()
    for copy in copies:
        copy.wait()
    pos_x, pos_y = lax.axis_index("gx"), lax.axis_index("gy")
    n_blocks = volume.shape[0]
    kinds = mat[...]
    density = jnp.zeros(kinds.shape, F32)
    for m in range(MAT):
        density = jnp.where(kinds == m, props[0, m], density)
    mass = volume[...] * density
    heat = mass * energy[...]
    level = lax.broadcasted_iota(jnp.int32, (MAT, BLK), 0)
    for k in range(9):
        seen[k] = 0
    for b in range(n_blocks):
        at_x, at_y = split_device(dest[b], size_y)
        near = code_of(at_x, pos_x) * 3 + code_of(at_y, pos_y)
        rank = seen[near]
        seen[near] = rank + 1
        slot = near * CAP + rank
        place[b] = slot
        volumes = jnp.where(kinds[b : b + 1] == level, volume[b : b + 1, :], 0.0)
        momentum = mass[b : b + 1] * velocity[:, b * BLK : (b + 1) * BLK]
        rows = jnp.concatenate([volumes, momentum, heat[b : b + 1], jnp.zeros((4, BLK), F32)], axis=0)
        packed[slot] = rows.astype(BF16)
    for k, out in enumerate((own, first, second)):
        for s in range(3 * CAP):
            out[s] = packed[k * 3 * CAP + s]


def payload(dest, props, volume, velocity, energy, mat, tile_slot, tile_cell, size_y):
    n_blocks = volume.shape[0]
    parcel = pltpu.VMEM((3 * CAP, ROWS, BLK), BF16)
    return pl.pallas_call(
        functools.partial(payload_kernel, size_y=size_y),
        name="payload",
        out_shape=(
            parcel,
            parcel,
            parcel,
            pltpu.SMEM((n_blocks,), jnp.int32),
            pltpu.SMEM(props.shape, F32),
            pltpu.SMEM(tile_slot.shape, jnp.int32),
            pltpu.SMEM(tile_cell.shape, jnp.int32),
        ),
        in_specs=[ANY] * 8,
        out_specs=(VMEM, VMEM, VMEM, SMEM, SMEM, SMEM, SMEM),
        scratch_shapes=[
            pltpu.SMEM(dest.shape, jnp.int32),
            pltpu.VMEM(volume.shape, F32),
            pltpu.VMEM(velocity.shape, F32),
            pltpu.VMEM(energy.shape, F32),
            pltpu.VMEM(mat.shape, jnp.int32),
            pltpu.SMEM((9,), jnp.int32),
            pltpu.VMEM((9 * CAP, ROWS, BLK), BF16),
            pltpu.SemaphoreType.DMA((8,)),
        ],
        compiler_params=pltpu.CompilerParams(vmem_limit_bytes=4 * MIB),
    )(*(in_hbm(value) for value in (dest, props, volume, velocity, energy, mat, tile_slot, tile_cell)))


def stage_kernel(
    tile_slot, tile_cell, tile_count, cell, weight, state, turned, slots, spots, points, sem, *, size_y
):
    pos_x, pos_y = lax.axis_index("gx"), lax.axis_index("gy")
    columns, count, tall = state.shape[0] - 2, state.shape[1], state.shape[2]
    width = tall - ROOM
    copies = [
        pltpu.make_async_copy(
            cell.at[:, :, pl.ds(j * BLK, BLK)], state.at[j + 1, :, pl.ds(PAD, width)], sem.at[j]
        )
        for j in range(columns)
    ]
    for copy in copies:
        copy.start()

    def transpose(step, carry):
        for k in range(TURN):
            turned[step * TURN + k] = weight[step * TURN + k].T
        return carry

    lax.fori_loop(0, weight.shape[0] // TURN, transpose, 0)
    counted = tile_count[0]

    def index(step, carry):
        for k in range(TURN):
            t = step * TURN + k
            x, j = split_device(tile_cell[t], columns)
            slots[t] = jnp.where(t < counted, local_slot(tile_slot[t], pos_x, pos_y, size_y), 9 * CAP)
            spots[t] = (j + 1) * (count * tall) + x + PAD
            points[t] = j * width + x
        return carry

    lax.fori_loop(0, weight.shape[0] // TURN, index, 0)
    for copy in copies:
        copy.wait()


def stage(tile_slot, tile_cell, tile_count, cell, weight, size_y):
    count, width, lanes = cell.shape
    columns = lanes // BLK
    indices = pltpu.SMEM(tile_slot.shape, jnp.int32)
    return pl.pallas_call(
        functools.partial(stage_kernel, size_y=size_y),
        name="stage",
        out_shape=(
            pltpu.VMEM((columns + 2, count, width + ROOM, BLK), F32),
            pltpu.VMEM(weight.shape, weight.dtype),
            indices,
            indices,
            indices,
        ),
        in_specs=[SMEM, SMEM, SMEM, ANY, VMEM],
        out_specs=(VMEM, VMEM, SMEM, SMEM, SMEM),
        scratch_shapes=[pltpu.SemaphoreType.DMA((columns,))],
        compiler_params=pltpu.CompilerParams(vmem_limit_bytes=2 * MIB),
        cost_estimate=pl.CostEstimate(flops=0, bytes_accessed=2 * cell.size * 4, transcendentals=0),
    )(tile_slot, tile_cell, tile_count, in_hbm(cell), weight)


def fetch_kernel(source, target, sem):
    copy = pltpu.make_async_copy(source, target, sem)
    copy.start()
    copy.wait()


def fetch(value):
    return pl.pallas_call(
        fetch_kernel,
        name="fetch",
        out_shape=pltpu.VMEM(value.shape, value.dtype),
        in_specs=[ANY],
        out_specs=VMEM,
        scratch_shapes=[pltpu.SemaphoreType.DMA],
        compiler_params=pltpu.CompilerParams(vmem_limit_bytes=2 * MIB),
        cost_estimate=pl.CostEstimate(flops=0, bytes_accessed=2 * value.size * 2, transcendentals=0),
    )(in_hbm(value))


def local_slot(slot, pos_x, pos_y, size_y):
    at_x, at_y = split_device(slot >> 1, size_y)
    return code_of(at_y, pos_y) * (3 * CAP) + code_of(at_x, pos_x) * CAP + (slot & 1)


def low_lanes():
    return lax.broadcasted_iota(jnp.int32, (1, BLK), 1) < HALF


def turn(value):
    return pltpu.roll(value, HALF, value.ndim - 1)


def beside(weight, t):
    return jnp.concatenate([weight[t], weight[t + 1]], axis=1)


def add_at(buffer, places, index, values):
    held = [buffer[index(place)] for place in places]
    for k, place in enumerate(places):
        value = values[k]
        for earlier in range(k):
            value = value + jnp.where(places[earlier] == place, values[earlier], 0.0)
        buffer[index(place)] = held[k] + value


def deposit_kernel(
    slots, spots, own, first, second, south, north, weight, state_in,
    state, edge_x1, edge_x2, edge_y1, edge_y2, rows
):
    pos_x, pos_y = lax.axis_index("gx"), lax.axis_index("gy")
    n_tiles = weight.shape[0]
    columns, count, tall = state.shape[0] - 2, state.shape[1], state.shape[2]
    line = state.reshape((columns + 2) * count * tall, BLK)
    rows[9 * CAP] = jnp.zeros(rows.shape[1:], BF16)
    for k, part in enumerate((own, first, second)):
        for r in range(CAP):
            rows[k * CAP + r] = part[r]
    for k, part in enumerate((south, north)):
        for r in range(3 * CAP):
            rows[(k + 1) * 3 * CAP + r] = part[r]
    for first_tile in range(0, n_tiles, TOGETHER):
        tiles = range(first_tile, first_tile + TOGETHER)
        contribs = []
        for t in tiles[::2]:
            both = jnp.concatenate([rows[slots[t]], rows[slots[t + 1]]], axis=0)
            found = jnp.dot(both, beside(weight, t), preferred_element_type=F32)
            contribs += [found[:count, :BLK], found[ROWS : ROWS + count, BLK:]]
        add_at(line, [spots[t] for t in tiles], lambda place: (pl.ds(place, count, stride=tall), slice(None)), contribs)

    even_x, even_y = (pos_x & 1) == 0, (pos_y & 1) == 0
    width = tall - ROOM
    top, bottom = PAD + width - 1, PAD
    for edge, row in (
        (edge_x1, jnp.where(even_x, bottom, top)),
        (edge_x2, jnp.where(even_x, top, bottom)),
    ):
        for q in range(count):
            at = pl.ds(count * tall + q * tall + row, columns, stride=count * tall)
            edge[q * columns : (q + 1) * columns, :] = line[at, :].astype(BF16)
    low = low_lanes()
    for edge, upper in ((edge_y1, jnp.logical_not(even_y)), (edge_y2, even_y)):
        column = jnp.where(upper, columns, 1)
        for q in range(count // 2):
            for i in range(width // ROWS):
                here = slice(PAD + i * ROWS, PAD + (i + 1) * ROWS)
                a = state[column, q, here, :]
                b = state[column, q + count // 2, here, :]
                both = jnp.where(low, jnp.where(upper, turn(a), a), jnp.where(upper, b, turn(b)))
                edge[q * width + i * ROWS : q * width + (i + 1) * ROWS, :] = both.astype(BF16)


def deposit(slots, spots, parts, weight, state):
    columns, count, tall = state.shape[0] - 2, state.shape[1], state.shape[2]
    edge_x = pltpu.VMEM((count * columns, BLK), BF16)
    edge_y = pltpu.VMEM((count // 2 * (tall - ROOM), BLK), BF16)
    return pl.pallas_call(
        deposit_kernel,
        name="deposit",
        out_shape=(pltpu.VMEM(state.shape, F32), edge_x, edge_x, edge_y, edge_y),
        in_specs=[SMEM] * 2 + [VMEM] * 7,
        out_specs=(VMEM,) * 5,
        input_output_aliases={8: 0},
        scratch_shapes=[pltpu.VMEM((9 * CAP + 1, ROWS, BLK), BF16)],
        compiler_params=pltpu.CompilerParams(vmem_limit_bytes=4 * MIB),
    )(slots, spots, *parts, weight, state)


def total(terms):
    while len(terms) > 1:
        terms = [a + b for a, b in zip(terms[::2], terms[1::2], strict=True)]
    return terms[0]


def speeds_at(props, state, j, here, parts):
    share = 1.0 / (1.0 + total([props[0, m] * state[j, m, here, :] for m in range(MAT)]))
    found = []
    if 0 in parts:
        found.append((0, state[j, MAT, here, :] * share))
    if 1 in parts:
        along = state[j, MAT + 1, here, :] * share
        found += [(1, along), (2, turn(along))]
    return found


def store_speeds(props, state, speed, places, parts):
    waiting = []
    for step in range(len(places) + DELAY):
        if step < len(places):
            j, first_row = places[step]
            waiting.append(speeds_at(props, state, j, slice(first_row, first_row + 8), parts))
        if step >= DELAY:
            j, first_row = places[step - DELAY]
            for plane, value in waiting.pop(0):
                speed[j, plane, first_row : first_row + 8, :] = value


def weights_at(speed, j, first_row):
    low = low_lanes()
    here = slice(first_row, first_row + 8)
    scale = 0.5 * time_step
    ux = speed[j, 0, here, :]
    lower = scale * (speed[j, 0, slice(first_row - 1, first_row + 7), :] + ux)
    upper = scale * (ux + speed[j, 0, slice(first_row + 1, first_row + 9), :])
    uy, before, after = (speed[k, 1, here, :] for k in (j, j - 1, j + 1))
    turned, turned_before, turned_after = (speed[k, 2, here, :] for k in (j, j - 1, j + 1))
    left = scale * (jnp.where(low, turned_before, turned) + uy)
    right = scale * (uy + jnp.where(low, turned, turned_after))
    keep = 1.0 - (
        (jnp.maximum(upper, 0.0) + jnp.maximum(-lower, 0.0)) + (jnp.maximum(right, 0.0) + jnp.maximum(-left, 0.0))
    )
    take_left = jnp.maximum(scale * (jnp.where(low, uy, before) + turned), 0.0)
    take_right = jnp.maximum(-scale * (turned + jnp.where(low, after, uy)), 0.0)
    same = jnp.where(low, take_left, take_right)
    other = jnp.where(low, take_right, take_left)
    return keep, jnp.maximum(lower, 0.0), jnp.maximum(-upper, 0.0), same, other


def values_at(state, weights, j, first_row, wanted):
    low = low_lanes()
    here = slice(first_row, first_row + 8)
    before = slice(first_row - 1, first_row + 7)
    after = slice(first_row + 1, first_row + 9)
    keep, take_before, take_after, same, other = weights
    values = []
    for q in wanted:
        mid = state[j, q, here, :]
        beside = jnp.where(low, state[j + 1, q, here, :], state[j - 1, q, here, :])
        value = (keep * mid + take_before * state[j, q, before, :]) + take_after * state[j, q, after, :]
        values.append(value + turn(same * mid + other * beside))
    return values


def pressure_of(props, values):
    terms = [value * (props[1, m] + (0.5 * props[1, m]) * value) for m, value in enumerate(values[:MAT])]
    return total(terms) + 0.4 * values[-1]


def remap_tiles(props, state, speed, press, fresh, places, wanted):
    weights, values = {}, {}
    for step in range(len(places) + 2):
        if step < len(places):
            weights[step] = weights_at(speed, *places[step])
        k = step - 1
        if 0 <= k < len(places):
            values[k] = values_at(state, weights.pop(k), *places[k], wanted)
        k = step - 2
        if k >= 0:
            found = values.pop(k)
            j, first_row = places[k]
            inside = slice(first_row - PAD, first_row - PAD + 8)
            lanes = column_lanes(j)
            for q, value in zip(wanted, found, strict=True):
                fresh[q, inside, lanes] = value
            if press is not None:
                press[j - 1, inside, :] = pressure_of(props, found)


def scalars(count):
    return [*range(MAT), count - 1]


def column_lanes(j):
    if isinstance(j, int):
        return slice((j - 1) * BLK, j * BLK)
    return pl.ds(pl.multiple_of((j - 1) * BLK, BLK), BLK)


def inner_kernel(props, state, fresh, press, speed):
    columns, tall = state.shape[0] - 2, state.shape[2]

    def speeds(step, carry):
        rows = range(PAD, tall - AFTER, 8)
        places = [(1 + step * GROUP + k, row) for k in range(GROUP) for row in rows]
        store_speeds(props, state, speed, places, (0, 1))
        return carry

    lax.fori_loop(0, columns // GROUP, speeds, 0)

    def remap(step, carry):
        rows = range(PAD + 8, tall - AFTER - 8, 8)
        places = [(2 + step * PAIR + k, row) for k in range(PAIR) for row in rows]
        remap_tiles(props, state, speed, press, fresh, places, scalars(state.shape[1]))
        return carry

    lax.fori_loop(0, (columns - 2) // PAIR, remap, 0)


def inner(props, state, width):
    columns, count, tall = state.shape[0] - 2, state.shape[1], state.shape[2]
    return pl.pallas_call(
        inner_kernel,
        name="inner",
        out_shape=(
            pltpu.VMEM((count, width, columns * BLK), F32),
            pltpu.VMEM((columns, width, BLK), F32),
            pltpu.VMEM((columns + 2, 3, tall, BLK), F32),
        ),
        in_specs=[SMEM, VMEM],
        out_specs=(VMEM, VMEM, VMEM),
        compiler_params=pltpu.CompilerParams(vmem_limit_bytes=4 * MIB),
        cost_estimate=pl.CostEstimate(flops=20 * state.size, bytes_accessed=2 * state.size * 4, transcendentals=0),
    )(props, state)


def outer_kernel(
    props, slots, points, edge_x1, edge_x2, edge_y1, edge_y2, weight, state_in, speed_in, press_in,
    fresh_in, remapped, state, speed, press, fresh, own, first, second, sums, sem, *, size_x, size_y
):
    pos_x, pos_y = lax.axis_index("gx"), lax.axis_index("gy")
    n_tiles = weight.shape[0]
    columns, count, tall = state.shape[0] - 2, state.shape[1], state.shape[2]
    width = tall - ROOM
    copies = area_copies(fresh, remapped, sem, scalar_planes(count), [inner_area(fresh)])
    for copy in copies:
        copy.start()
    even_x, even_y = (pos_x & 1) == 0, (pos_y & 1) == 0
    line = state.reshape((columns + 2) * count * tall, BLK)
    above, below = PAD + width, PAD - 1
    for edge, row, there in (
        (edge_x1, jnp.where(even_x, below, above), has_far(pos_x, size_x)),
        (edge_x2, jnp.where(even_x, above, below), True),
    ):
        for q in range(count):
            at = pl.ds(count * tall + q * tall + row, columns, stride=count * tall)
            line[at, :] = jnp.where(there, edge[q * columns : (q + 1) * columns, :].astype(F32), 0.0)
    low = low_lanes()
    for edge, column, there in (
        (edge_y1, jnp.where(even_y, 0, columns + 1), has_far(pos_y, size_y)),
        (edge_y2, jnp.where(even_y, columns + 1, 0), True),
    ):
        for q in range(count // 2):
            for i in range(width // ROWS):
                here = slice(PAD + i * ROWS, PAD + (i + 1) * ROWS)
                both = edge[q * width + i * ROWS : q * width + (i + 1) * ROWS, :].astype(F32)
                both = jnp.where(there, both, 0.0)
                turned = turn(both)
                state[column, q, here, :] = jnp.where(low, both, turned)
                state[column, q + count // 2, here, :] = jnp.where(low, turned, both)

    places = [(j, row) for j in range(1, columns + 1) for row in (0, tall - AFTER)]
    store_speeds(props, state, speed, places, (0,))
    places = [(j, row) for j in (0, columns + 1) for row in range(PAD, tall - AFTER, 8)]
    store_speeds(props, state, speed, places, (1,))

    def sides(step, carry):
        places = [(1 + step * 2 * PAIR + k, row) for k in range(2 * PAIR) for row in (PAD, tall - AFTER - 8)]
        remap_tiles(props, state, speed, press, fresh, places, scalars(state.shape[1]))
        return carry

    lax.fori_loop(0, columns // (2 * PAIR), sides, 0)
    places = [(j, row) for j in (1, columns) for row in range(PAD + 8, tall - AFTER - 8, 8)]
    remap_tiles(props, state, speed, press, fresh, places, scalars(state.shape[1]))

    sums[...] = jnp.zeros(sums.shape, F32)
    line_of = lax.broadcasted_iota(jnp.int32, (ROWS, BLK), 0)
    field = press.reshape(columns * width, BLK)
    for first_tile in range(0, n_tiles, TOGETHER):
        tiles = range(first_tile, first_tile + TOGETHER)
        found = []
        for t in tiles[::2]:
            one, two = (field[pl.ds(points[k], 1), :] for k in (t, t + 1))
            probe = jnp.where(line_of == 0, one, jnp.where(line_of == 8, two, 1.0)).astype(BF16)
            both = jnp.dot(probe, beside(weight, t), preferred_element_type=F32)
            found += [both[:8, :BLK], both[8:, BLK:]]
        add_at(sums, [slots[t] for t in tiles], lambda place: place, found)
    table = sums.reshape(sums.shape[0] * 8, BLK)
    for k, out in enumerate((own, first, second)):
        top = table[pl.ds(k * 3 * CAP * 8, 3 * CAP, stride=8), :]
        under = table[pl.ds(k * 3 * CAP * 8 + 1, 3 * CAP, stride=8), :]
        out[...] = top / jnp.maximum(under, 1.0)
    for copy in copies:
        copy.wait()


def outer(props, slots, points, edges, weight, state, speed, press, fresh, size_x, size_y):
    answer = pltpu.VMEM((3 * CAP, BLK), F32)
    outs = pl.pallas_call(
        functools.partial(outer_kernel, size_x=size_x, size_y=size_y),
        name="outer",
        out_shape=(
            jax.ShapeDtypeStruct(fresh.shape, F32),
            pltpu.VMEM(state.shape, F32),
            pltpu.VMEM(speed.shape, F32),
            pltpu.VMEM(press.shape, F32),
            pltpu.VMEM(fresh.shape, F32),
            answer,
            answer,
            answer,
        ),
        in_specs=[SMEM] * 3 + [VMEM] * 9,
        out_specs=(ANY,) + (VMEM,) * 7,
        input_output_aliases={8: 1, 9: 2, 10: 3, 11: 4},
        scratch_shapes=[pltpu.VMEM((9 * CAP + 1, 8, BLK), F32), pltpu.SemaphoreType.DMA((2,))],
        compiler_params=pltpu.CompilerParams(vmem_limit_bytes=4 * MIB),
    )(props, slots, points, *edges, weight, state, speed, press, fresh)
    return outs[0], outs[1], outs[2], outs[4], outs[5], outs[6], outs[7]


def late_kernel(state, speed, fresh_in, remapped_in, remapped, fresh, sem, sem_moving):
    columns, count, tall = state.shape[0] - 2, state.shape[1], state.shape[2]
    width, lanes = fresh.shape[1], fresh.shape[2]
    rows = pl.ds(8, width - 16)
    areas = [
        (pl.ds(0, 8), pl.ds(0, lanes)),
        (pl.ds(width - 8, 8), pl.ds(0, lanes)),
        (rows, pl.ds(0, BLK)),
        (rows, pl.ds(lanes - BLK, BLK)),
    ]
    copies = area_copies(fresh, remapped, sem, scalar_planes(count), areas)
    for copy in copies:
        copy.start()
    for part in range(PARTS):
        held = range(1 + part * columns // PARTS, 1 + (part + 1) * columns // PARTS)
        places = [(j, row) for j in held for row in range(PAD, tall - AFTER, 8)]
        remap_tiles(None, state, speed, None, fresh, places, range(MAT, count - 1))
        area = (pl.ds(0, width), pl.ds((held[0] - 1) * BLK, len(held) * BLK))
        copies += area_copies(fresh, remapped, sem_moving.at[part], [pl.ds(MAT, count - 1 - MAT)], [area])
        copies[-1].start()
    for copy in copies:
        copy.wait()


def scalar_planes(count):
    return [pl.ds(0, MAT), pl.ds(count - 1, 1)]


def inner_area(fresh):
    return pl.ds(8, fresh.shape[1] - 16), pl.ds(BLK, fresh.shape[2] - 2 * BLK)


def area_copies(fresh, remapped, sem, planes, areas):
    boxes = [(plane, *area) for area in areas for plane in planes]
    return [pltpu.make_async_copy(fresh.at[box], remapped.at[box], sem.at[k]) for k, box in enumerate(boxes)]


def late(state, speed, fresh, remapped):
    return pl.pallas_call(
        late_kernel,
        name="late",
        out_shape=(jax.ShapeDtypeStruct(fresh.shape, F32), pltpu.VMEM(fresh.shape, F32)),
        in_specs=[VMEM] * 3 + [ANY],
        out_specs=(ANY, VMEM),
        input_output_aliases={2: 1, 3: 0},
        scratch_shapes=[pltpu.SemaphoreType.DMA((8,)), pltpu.SemaphoreType.DMA((PARTS, 1))],
        compiler_params=pltpu.CompilerParams(vmem_limit_bytes=4 * MIB),
        cost_estimate=pl.CostEstimate(flops=5 * state.size, bytes_accessed=2 * state.size * 4, transcendentals=0),
    )(state, speed, fresh, remapped)[0]


def pick_kernel(place, own, first, second, out, table, lines):
    for k, part in enumerate((own, first, second)):
        table[k * 3 * CAP : (k + 1) * 3 * CAP, :] = part[...]
    for b in range(out.shape[0]):
        lines[b : b + 1, :] = table[pl.ds(place[b], 1), :]
    out[...] = lines[...].astype(BF16)


def pick(place, own, first, second):
    n_blocks = place.shape[0]
    return pl.pallas_call(
        pick_kernel,
        name="pick",
        out_shape=jax.ShapeDtypeStruct((n_blocks, BLK), BF16),
        in_specs=[SMEM, VMEM, VMEM, VMEM],
        out_specs=VMEM,
        scratch_shapes=[pltpu.VMEM((9 * CAP, BLK), F32), pltpu.VMEM((n_blocks, BLK), F32)],
        compiler_params=pltpu.CompilerParams(vmem_limit_bytes=2 * MIB),
    )(place, own, first, second)


def per_device(
    elem_volume,
    elem_velocity,
    elem_energy,
    elem_mat,
    elem_dest,
    tile_slot,
    tile_cell,
    tile_weight,
    tile_count,
    cell_state,
    mat_props,
):
    size_x, size_y = lax.axis_size("gx"), lax.axis_size("gy")
    n_blocks = elem_dest.shape[0]
    shape = (n_blocks, BLK)
    own, first, second, place, mat_props, tile_slot, tile_cell = payload(
        elem_dest,
        mat_props,
        elem_volume.reshape(shape),
        elem_velocity,
        elem_energy.reshape(shape),
        elem_mat.reshape(shape),
        tile_slot,
        tile_cell,
        size_y,
    )
    weight = fetch(tile_weight)

    first = swap(first, "gx", 1)
    second = swap(second, "gx", 2)
    weight, own = lax.optimization_barrier((weight, own))
    state, turned, slots, spots, points = stage(
        tile_slot, tile_cell, tile_count, cell_state, weight, size_y
    )

    def along_y(which):
        rows = slice(which * CAP, (which + 1) * CAP)
        return jnp.concatenate([own[rows], first[rows], second[rows]], axis=0)

    south = swap(along_y(1), "gy", 1)
    north = swap(along_y(2), "gy", 2)
    state, *edges = deposit(
        slots, spots, (own, first, second, south, north), weight, state
    )
    edges = (
        swap(edges[0], "gx", 1),
        swap(edges[1], "gx", 2),
        swap(edges[2], "gy", 1, wrap=False),
        swap(edges[3], "gy", 2),
    )
    fresh, press, speed = inner(mat_props, state, cell_state.shape[1])
    remapped, state, speed, fresh, own, first, second = outer(
        mat_props, slots, points, edges, turned, state, speed, press, fresh, size_x, size_y
    )
    remapped = late(state, speed, fresh, remapped)
    first = swap(first, "gy", 1)
    second = swap(second, "gy", 2)

    def along_x(which):
        rows = slice(which * CAP, (which + 1) * CAP)
        return jnp.concatenate([own[rows], first[rows], second[rows]], axis=0)

    back = pick(place, along_x(0), swap(along_x(1), "gx", 1), swap(along_x(2), "gx", 2))
    return remapped, back.reshape(n_blocks * BLK)


def solution(mesh):
    placed = (
        P(("gx", "gy")),
        P(None, ("gx", "gy")),
        P(("gx", "gy")),
        P(("gx", "gy")),
        P(("gx", "gy")),
        P(("gx", "gy")),
        P(("gx", "gy")),
        P(("gx", "gy"), None, None),
        P(("gx", "gy")),
        P(None, "gx", "gy"),
        P(),
    )
    return jax.shard_map(
        per_device,
        mesh=mesh,
        in_specs=placed,
        out_specs=(P(None, "gx", "gy"), P(("gx", "gy"))),
        check_vma=False,
    )
```

```python
import functools

import jax
import jax.numpy as jnp
from jax import lax
from jax.experimental import pallas as pl
from jax.experimental.pallas import tpu as pltpu
from jax.sharding import PartitionSpec as P

MAT = 8
NZ = 64
BLK = 128
CAP = 2
HALF = BLK // 2
PAD = 8
AFTER = 16
ROOM = PAD + AFTER
ROWS = 16
PAIR = 2
TOGETHER = 4
PARTS = 4
TURN = 16
GROUP = 8
DELAY = 4
MIB = 2**20

time_step = 0.8
F32 = jnp.float32
BF16 = jnp.bfloat16

SMEM = pl.BlockSpec(memory_space=pltpu.SMEM)
VMEM = pl.BlockSpec(memory_space=pltpu.VMEM)
ANY = pl.BlockSpec(memory_space=pl.ANY)


def partner(index, size, which):
    if which == 2:
        return index ^ 1
    return (index + 1 if index % 2 else index - 1) % size


def swap(value, axis, which, wrap=True):
    size = lax.axis_size(axis)
    pairs = [(i, partner(i, size, which)) for i in range(size)]
    if not wrap:
        pairs = [(i, j if abs(i - j) == 1 else i) for i, j in pairs]
    return lax.ppermute(value, axis, pairs)


def has_far(index, size):
    return (index > 0) & (index < size - 1)


def code_of(index, mine):
    return jnp.where(index == mine, 0, jnp.where(index == (mine ^ 1), 2, 1))


def split_device(device, size):
    if size & (size - 1) == 0:
        return device >> (size.bit_length() - 1), device & (size - 1)
    return lax.div(device, size), lax.rem(device, size)


def in_hbm(value):
    return pltpu.with_memory_space_constraint(value, pltpu.HBM)


def payload_kernel(
    dest_hbm, props_hbm, volume_hbm, velocity_hbm, energy_hbm, mat_hbm, slot_hbm, cell_hbm,
    own, first, second, place, props, slot_out, cell_out, dest, volume, velocity, energy, mat, seen, packed, sem, *, size_y
):
    moves = (
        (dest_hbm, dest), (props_hbm, props), (mat_hbm, mat),
        (volume_hbm, volume), (velocity_hbm, velocity), (energy_hbm, energy),
        (slot_hbm, slot_out), (cell_hbm, cell_out),
    )
    copies = [pltpu.make_async_copy(src, dst, sem.at[k]) for k, (src, dst) in enumerate(moves)]
    for copy in copies:
        copy.start()
    for copy in copies:
        copy.wait()
    pos_x, pos_y = lax.axis_index("gx"), lax.axis_index("gy")
    n_blocks = volume.shape[0]
    kinds = mat[...]
    density = jnp.zeros(kinds.shape, F32)
    for m in range(MAT):
        density = jnp.where(kinds == m, props[0, m], density)
    mass = volume[...] * density
    heat = mass * energy[...]
    level = lax.broadcasted_iota(jnp.int32, (MAT, BLK), 0)
    for k in range(9):
        seen[k] = 0
    for b in range(n_blocks):
        at_x, at_y = split_device(dest[b], size_y)
        near = code_of(at_x, pos_x) * 3 + code_of(at_y, pos_y)
        rank = seen[near]
        seen[near] = rank + 1
        slot = near * CAP + rank
        place[b] = slot
        volumes = jnp.where(kinds[b : b + 1] == level, volume[b : b + 1, :], 0.0)
        momentum = mass[b : b + 1] * velocity[:, b * BLK : (b + 1) * BLK]
        rows = jnp.concatenate([volumes, momentum, heat[b : b + 1], jnp.zeros((4, BLK), F32)], axis=0)
        packed[slot] = rows.astype(BF16)
    for k, out in enumerate((own, first, second)):
        for s in range(3 * CAP):
            out[s] = packed[k * 3 * CAP + s]


def payload(dest, props, volume, velocity, energy, mat, tile_slot, tile_cell, size_y):
    n_blocks = volume.shape[0]
    parcel = pltpu.VMEM((3 * CAP, ROWS, BLK), BF16)
    return pl.pallas_call(
        functools.partial(payload_kernel, size_y=size_y),
        name="payload",
        out_shape=(
            parcel,
            parcel,
            parcel,
            pltpu.SMEM((n_blocks,), jnp.int32),
            pltpu.SMEM(props.shape, F32),
            pltpu.SMEM(tile_slot.shape, jnp.int32),
            pltpu.SMEM(tile_cell.shape, jnp.int32),
        ),
        in_specs=[ANY] * 8,
        out_specs=(VMEM, VMEM, VMEM, SMEM, SMEM, SMEM, SMEM),
        scratch_shapes=[
            pltpu.SMEM(dest.shape, jnp.int32),
            pltpu.VMEM(volume.shape, F32),
            pltpu.VMEM(velocity.shape, F32),
            pltpu.VMEM(energy.shape, F32),
            pltpu.VMEM(mat.shape, jnp.int32),
            pltpu.SMEM((9,), jnp.int32),
            pltpu.VMEM((9 * CAP, ROWS, BLK), BF16),
            pltpu.SemaphoreType.DMA((8,)),
        ],
        compiler_params=pltpu.CompilerParams(vmem_limit_bytes=4 * MIB),
    )(*(in_hbm(value) for value in (dest, props, volume, velocity, energy, mat, tile_slot, tile_cell)))


def stage_kernel(
    tile_slot, tile_cell, tile_count, cell, weight, state, turned, slots, spots, points, sem, *, size_y
):
    pos_x, pos_y = lax.axis_index("gx"), lax.axis_index("gy")
    columns, count, tall = state.shape[0] - 2, state.shape[1], state.shape[2]
    width = tall - ROOM
    copies = [
        pltpu.make_async_copy(
            cell.at[:, :, pl.ds(j * BLK, BLK)], state.at[j + 1, :, pl.ds(PAD, width)], sem.at[j]
        )
        for j in range(columns)
    ]
    for copy in copies:
        copy.start()

    counted = tile_count[0]

    def turn_and_index(step, carry):
        for k in range(TURN):
            t = step * TURN + k
            turned[t] = weight[t].T
            x, j = split_device(tile_cell[t], columns)
            slots[t] = jnp.where(t < counted, local_slot(tile_slot[t], pos_x, pos_y, size_y), 9 * CAP)
            spots[t] = (j + 1) * (count * tall) + x + PAD
            points[t] = j * width + x
        return carry

    lax.fori_loop(0, weight.shape[0] // TURN, turn_and_index, 0)
    for copy in copies:
        copy.wait()


def stage(tile_slot, tile_cell, tile_count, cell, weight, size_y):
    count, width, lanes = cell.shape
    columns = lanes // BLK
    indices = pltpu.SMEM(tile_slot.shape, jnp.int32)
    return pl.pallas_call(
        functools.partial(stage_kernel, size_y=size_y),
        name="stage",
        out_shape=(
            pltpu.VMEM((columns + 2, count, width + ROOM, BLK), F32),
            pltpu.VMEM(weight.shape, weight.dtype),
            indices,
            indices,
            indices,
        ),
        in_specs=[SMEM, SMEM, SMEM, ANY, VMEM],
        out_specs=(VMEM, VMEM, SMEM, SMEM, SMEM),
        scratch_shapes=[pltpu.SemaphoreType.DMA((columns,))],
        compiler_params=pltpu.CompilerParams(vmem_limit_bytes=2 * MIB),
        cost_estimate=pl.CostEstimate(flops=0, bytes_accessed=2 * cell.size * 4, transcendentals=0),
    )(tile_slot, tile_cell, tile_count, in_hbm(cell), weight)


def fetch_kernel(source, target, sem):
    copy = pltpu.make_async_copy(source, target, sem)
    copy.start()
    copy.wait()


def fetch(value):
    return pl.pallas_call(
        fetch_kernel,
        name="fetch",
        out_shape=pltpu.VMEM(value.shape, value.dtype),
        in_specs=[ANY],
        out_specs=VMEM,
        scratch_shapes=[pltpu.SemaphoreType.DMA],
        compiler_params=pltpu.CompilerParams(vmem_limit_bytes=2 * MIB),
        cost_estimate=pl.CostEstimate(flops=0, bytes_accessed=2 * value.size * 2, transcendentals=0),
    )(in_hbm(value))


def local_slot(slot, pos_x, pos_y, size_y):
    at_x, at_y = split_device(slot >> 1, size_y)
    return code_of(at_y, pos_y) * (3 * CAP) + code_of(at_x, pos_x) * CAP + (slot & 1)


def low_lanes():
    return lax.broadcasted_iota(jnp.int32, (1, BLK), 1) < HALF


def turn(value):
    return pltpu.roll(value, HALF, value.ndim - 1)


def beside(weight, t):
    return jnp.concatenate([weight[t], weight[t + 1]], axis=1)


def add_at(buffer, places, index, values):
    held = [buffer[index(place)] for place in places]
    for k, place in enumerate(places):
        value = values[k]
        for earlier in range(k):
            value = value + jnp.where(places[earlier] == place, values[earlier], 0.0)
        buffer[index(place)] = held[k] + value


def deposit_kernel(
    slots, spots, own, first, second, south, north, weight, state_in,
    state, edge_x1, edge_x2, edge_y1, edge_y2, rows
):
    pos_x, pos_y = lax.axis_index("gx"), lax.axis_index("gy")
    n_tiles = weight.shape[0]
    columns, count, tall = state.shape[0] - 2, state.shape[1], state.shape[2]
    line = state.reshape((columns + 2) * count * tall, BLK)
    rows[9 * CAP] = jnp.zeros(rows.shape[1:], BF16)
    for k, part in enumerate((own, first, second)):
        for r in range(CAP):
            rows[k * CAP + r] = part[r]
    for k, part in enumerate((south, north)):
        for r in range(3 * CAP):
            rows[(k + 1) * 3 * CAP + r] = part[r]
    for first_tile in range(0, n_tiles, TOGETHER):
        tiles = range(first_tile, first_tile + TOGETHER)
        contribs = []
        for t in tiles[::2]:
            both = jnp.concatenate([rows[slots[t]], rows[slots[t + 1]]], axis=0)
            found = jnp.dot(both, beside(weight, t), preferred_element_type=F32)
            contribs += [found[:count, :BLK], found[ROWS : ROWS + count, BLK:]]
        add_at(line, [spots[t] for t in tiles], lambda place: (pl.ds(place, count, stride=tall), slice(None)), contribs)

    even_x, even_y = (pos_x & 1) == 0, (pos_y & 1) == 0
    width = tall - ROOM
    top, bottom = PAD + width - 1, PAD
    for edge, row in (
        (edge_x1, jnp.where(even_x, bottom, top)),
        (edge_x2, jnp.where(even_x, top, bottom)),
    ):
        for q in range(count):
            at = pl.ds(count * tall + q * tall + row, columns, stride=count * tall)
            edge[q * columns : (q + 1) * columns, :] = line[at, :].astype(BF16)
    low = low_lanes()
    for edge, upper in ((edge_y1, jnp.logical_not(even_y)), (edge_y2, even_y)):
        column = jnp.where(upper, columns, 1)
        for q in range(count // 2):
            for i in range(width // ROWS):
                here = slice(PAD + i * ROWS, PAD + (i + 1) * ROWS)
                a = state[column, q, here, :]
                b = state[column, q + count // 2, here, :]
                both = jnp.where(low, jnp.where(upper, turn(a), a), jnp.where(upper, b, turn(b)))
                edge[q * width + i * ROWS : q * width + (i + 1) * ROWS, :] = both.astype(BF16)


def deposit(slots, spots, parts, weight, state):
    columns, count, tall = state.shape[0] - 2, state.shape[1], state.shape[2]
    edge_x = pltpu.VMEM((count * columns, BLK), BF16)
    edge_y = pltpu.VMEM((count // 2 * (tall - ROOM), BLK), BF16)
    return pl.pallas_call(
        deposit_kernel,
        name="deposit",
        out_shape=(pltpu.VMEM(state.shape, F32), edge_x, edge_x, edge_y, edge_y),
        in_specs=[SMEM] * 2 + [VMEM] * 7,
        out_specs=(VMEM,) * 5,
        input_output_aliases={8: 0},
        scratch_shapes=[pltpu.VMEM((9 * CAP + 1, ROWS, BLK), BF16)],
        compiler_params=pltpu.CompilerParams(vmem_limit_bytes=4 * MIB),
    )(slots, spots, *parts, weight, state)


def total(terms):
    while len(terms) > 1:
        terms = [a + b for a, b in zip(terms[::2], terms[1::2], strict=True)]
    return terms[0]


def speeds_at(props, state, j, here, parts):
    share = 1.0 / (1.0 + total([props[0, m] * state[j, m, here, :] for m in range(MAT)]))
    found = []
    if 0 in parts:
        found.append((0, state[j, MAT, here, :] * share))
    if 1 in parts:
        along = state[j, MAT + 1, here, :] * share
        found += [(1, along), (2, turn(along))]
    return found


def store_speeds(props, state, speed, places, parts):
    waiting = []
    for step in range(len(places) + DELAY):
        if step < len(places):
            j, first_row = places[step]
            waiting.append(speeds_at(props, state, j, slice(first_row, first_row + 8), parts))
        if step >= DELAY:
            j, first_row = places[step - DELAY]
            for plane, value in waiting.pop(0):
                speed[j, plane, first_row : first_row + 8, :] = value


def weights_at(speed, j, first_row):
    low = low_lanes()
    here = slice(first_row, first_row + 8)
    scale = 0.5 * time_step
    ux = speed[j, 0, here, :]
    lower = scale * (speed[j, 0, slice(first_row - 1, first_row + 7), :] + ux)
    upper = scale * (ux + speed[j, 0, slice(first_row + 1, first_row + 9), :])
    uy, before, after = (speed[k, 1, here, :] for k in (j, j - 1, j + 1))
    turned, turned_before, turned_after = (speed[k, 2, here, :] for k in (j, j - 1, j + 1))
    left = scale * (jnp.where(low, turned_before, turned) + uy)
    right = scale * (uy + jnp.where(low, turned, turned_after))
    keep = 1.0 - (
        (jnp.maximum(upper, 0.0) + jnp.maximum(-lower, 0.0)) + (jnp.maximum(right, 0.0) + jnp.maximum(-left, 0.0))
    )
    take_left = jnp.maximum(scale * (jnp.where(low, uy, before) + turned), 0.0)
    take_right = jnp.maximum(-scale * (turned + jnp.where(low, after, uy)), 0.0)
    same = jnp.where(low, take_left, take_right)
    other = jnp.where(low, take_right, take_left)
    return keep, jnp.maximum(lower, 0.0), jnp.maximum(-upper, 0.0), same, other


def values_at(state, weights, j, first_row, wanted):
    low = low_lanes()
    here = slice(first_row, first_row + 8)
    before = slice(first_row - 1, first_row + 7)
    after = slice(first_row + 1, first_row + 9)
    keep, take_before, take_after, same, other = weights
    values = []
    for q in wanted:
        mid = state[j, q, here, :]
        beside = jnp.where(low, state[j + 1, q, here, :], state[j - 1, q, here, :])
        value = (keep * mid + take_before * state[j, q, before, :]) + take_after * state[j, q, after, :]
        values.append(value + turn(same * mid + other * beside))
    return values


def pressure_of(props, values):
    terms = [value * (props[1, m] + (0.5 * props[1, m]) * value) for m, value in enumerate(values[:MAT])]
    return total(terms) + 0.4 * values[-1]


def remap_tiles(props, state, speed, press, fresh, places, wanted):
    weights, values = {}, {}
    for step in range(len(places) + 2):
        if step < len(places):
            weights[step] = weights_at(speed, *places[step])
        k = step - 1
        if 0 <= k < len(places):
            values[k] = values_at(state, weights.pop(k), *places[k], wanted)
        k = step - 2
        if k >= 0:
            found = values.pop(k)
            j, first_row = places[k]
            inside = slice(first_row - PAD, first_row - PAD + 8)
            lanes = column_lanes(j)
            for q, value in zip(wanted, found, strict=True):
                fresh[q, inside, lanes] = value
            if press is not None:
                press[j - 1, inside, :] = pressure_of(props, found)


def scalars(count):
    return [*range(MAT), count - 1]


def column_lanes(j):
    if isinstance(j, int):
        return slice((j - 1) * BLK, j * BLK)
    return pl.ds(pl.multiple_of((j - 1) * BLK, BLK), BLK)


def inner_kernel(props, state, fresh, press, speed):
    columns, tall = state.shape[0] - 2, state.shape[2]

    def speeds(step, carry):
        rows = range(PAD, tall - AFTER, 8)
        places = [(1 + step * GROUP + k, row) for k in range(GROUP) for row in rows]
        store_speeds(props, state, speed, places, (0, 1))
        return carry

    lax.fori_loop(0, columns // GROUP, speeds, 0)

    def remap(step, carry):
        rows = range(PAD + 8, tall - AFTER - 8, 8)
        places = [(2 + step * PAIR + k, row) for k in range(PAIR) for row in rows]
        remap_tiles(props, state, speed, press, fresh, places, scalars(state.shape[1]))
        return carry

    lax.fori_loop(0, (columns - 2) // PAIR, remap, 0)


def inner(props, state, width):
    columns, count, tall = state.shape[0] - 2, state.shape[1], state.shape[2]
    return pl.pallas_call(
        inner_kernel,
        name="inner",
        out_shape=(
            pltpu.VMEM((count, width, columns * BLK), F32),
            pltpu.VMEM((columns, width, BLK), F32),
            pltpu.VMEM((columns + 2, 3, tall, BLK), F32),
        ),
        in_specs=[SMEM, VMEM],
        out_specs=(VMEM, VMEM, VMEM),
        compiler_params=pltpu.CompilerParams(vmem_limit_bytes=4 * MIB),
        cost_estimate=pl.CostEstimate(flops=20 * state.size, bytes_accessed=2 * state.size * 4, transcendentals=0),
    )(props, state)


def outer_kernel(
    props, slots, points, edge_x1, edge_x2, edge_y2, edge_y1, weight, state_in, speed_in, press_in,
    fresh_in, remapped, state, speed, press, fresh, own, first, second, sums, sem, *, size_x, size_y
):
    pos_x, pos_y = lax.axis_index("gx"), lax.axis_index("gy")
    n_tiles = weight.shape[0]
    columns, count, tall = state.shape[0] - 2, state.shape[1], state.shape[2]
    width = tall - ROOM
    copies = area_copies(fresh, remapped, sem, scalar_planes(count), [inner_area(fresh)])
    for copy in copies:
        copy.start()
    even_x, even_y = (pos_x & 1) == 0, (pos_y & 1) == 0
    line = state.reshape((columns + 2) * count * tall, BLK)
    above, below = PAD + width, PAD - 1
    for edge, row, there in (
        (edge_x1, jnp.where(even_x, below, above), has_far(pos_x, size_x)),
        (edge_x2, jnp.where(even_x, above, below), True),
    ):
        for q in range(count):
            at = pl.ds(count * tall + q * tall + row, columns, stride=count * tall)
            line[at, :] = jnp.where(there, edge[q * columns : (q + 1) * columns, :].astype(F32), 0.0)
    low = low_lanes()
    for edge, column, there in (
        (edge_y1, jnp.where(even_y, 0, columns + 1), has_far(pos_y, size_y)),
        (edge_y2, jnp.where(even_y, columns + 1, 0), True),
    ):
        for q in range(count // 2):
            for i in range(width // ROWS):
                here = slice(PAD + i * ROWS, PAD + (i + 1) * ROWS)
                both = edge[q * width + i * ROWS : q * width + (i + 1) * ROWS, :].astype(F32)
                both = jnp.where(there, both, 0.0)
                turned = turn(both)
                state[column, q, here, :] = jnp.where(low, both, turned)
                state[column, q + count // 2, here, :] = jnp.where(low, turned, both)

    places = [(j, row) for j in range(1, columns + 1) for row in (0, tall - AFTER)]
    store_speeds(props, state, speed, places, (0,))
    places = [(j, row) for j in (0, columns + 1) for row in range(PAD, tall - AFTER, 8)]
    store_speeds(props, state, speed, places, (1,))

    def sides(step, carry):
        places = [(1 + step * 2 * PAIR + k, row) for k in range(2 * PAIR) for row in (PAD, tall - AFTER - 8)]
        remap_tiles(props, state, speed, press, fresh, places, scalars(state.shape[1]))
        return carry

    lax.fori_loop(0, columns // (2 * PAIR), sides, 0)
    places = [(j, row) for j in (1, columns) for row in range(PAD + 8, tall - AFTER - 8, 8)]
    remap_tiles(props, state, speed, press, fresh, places, scalars(state.shape[1]))

    sums[...] = jnp.zeros(sums.shape, F32)
    line_of = lax.broadcasted_iota(jnp.int32, (ROWS, BLK), 0)
    field = press.reshape(columns * width, BLK)
    for first_tile in range(0, n_tiles, TOGETHER):
        tiles = range(first_tile, first_tile + TOGETHER)
        found = []
        for t in tiles[::2]:
            one, two = (field[pl.ds(points[k], 1), :] for k in (t, t + 1))
            probe = jnp.where(line_of == 0, one, jnp.where(line_of == 8, two, 1.0)).astype(BF16)
            both = jnp.dot(probe, beside(weight, t), preferred_element_type=F32)
            found += [both[:8, :BLK], both[8:, BLK:]]
        add_at(sums, [slots[t] for t in tiles], lambda place: place, found)
    table = sums.reshape(sums.shape[0] * 8, BLK)
    for k, out in enumerate((own, first, second)):
        top = table[pl.ds(k * 3 * CAP * 8, 3 * CAP, stride=8), :]
        under = table[pl.ds(k * 3 * CAP * 8 + 1, 3 * CAP, stride=8), :]
        out[...] = top / jnp.maximum(under, 1.0)
    for copy in copies:
        copy.wait()


def outer(props, slots, points, edges, weight, state, speed, press, fresh, size_x, size_y):
    answer = pltpu.VMEM((3 * CAP, BLK), F32)
    outs = pl.pallas_call(
        functools.partial(outer_kernel, size_x=size_x, size_y=size_y),
        name="outer",
        out_shape=(
            jax.ShapeDtypeStruct(fresh.shape, F32),
            pltpu.VMEM(state.shape, F32),
            pltpu.VMEM(speed.shape, F32),
            pltpu.VMEM(press.shape, F32),
            pltpu.VMEM(fresh.shape, F32),
            answer,
            answer,
            answer,
        ),
        in_specs=[SMEM] * 3 + [VMEM] * 9,
        out_specs=(ANY,) + (VMEM,) * 7,
        input_output_aliases={8: 1, 9: 2, 10: 3, 11: 4},
        scratch_shapes=[pltpu.VMEM((9 * CAP + 1, 8, BLK), F32), pltpu.SemaphoreType.DMA((2,))],
        compiler_params=pltpu.CompilerParams(vmem_limit_bytes=4 * MIB),
    )(props, slots, points, *edges, weight, state, speed, press, fresh)
    return outs[0], outs[1], outs[2], outs[4], outs[5], outs[6], outs[7]


def late_kernel(state, speed, fresh_in, remapped_in, remapped, fresh, sem, sem_moving):
    columns, count, tall = state.shape[0] - 2, state.shape[1], state.shape[2]
    width, lanes = fresh.shape[1], fresh.shape[2]
    rows = pl.ds(8, width - 16)
    areas = [
        (pl.ds(0, 8), pl.ds(0, lanes)),
        (pl.ds(width - 8, 8), pl.ds(0, lanes)),
        (rows, pl.ds(0, BLK)),
        (rows, pl.ds(lanes - BLK, BLK)),
    ]
    copies = area_copies(fresh, remapped, sem, scalar_planes(count), areas)
    for copy in copies:
        copy.start()
    for part in range(PARTS):
        held = range(1 + part * columns // PARTS, 1 + (part + 1) * columns // PARTS)
        places = [(j, row) for j in held for row in range(PAD, tall - AFTER, 8)]
        remap_tiles(None, state, speed, None, fresh, places, range(MAT, count - 1))
        area = (pl.ds(0, width), pl.ds((held[0] - 1) * BLK, len(held) * BLK))
        copies += area_copies(fresh, remapped, sem_moving.at[part], [pl.ds(MAT, count - 1 - MAT)], [area])
        copies[-1].start()
    for copy in copies:
        copy.wait()


def scalar_planes(count):
    return [pl.ds(0, MAT), pl.ds(count - 1, 1)]


def inner_area(fresh):
    return pl.ds(8, fresh.shape[1] - 16), pl.ds(BLK, fresh.shape[2] - 2 * BLK)


def area_copies(fresh, remapped, sem, planes, areas):
    boxes = [(plane, *area) for area in areas for plane in planes]
    return [pltpu.make_async_copy(fresh.at[box], remapped.at[box], sem.at[k]) for k, box in enumerate(boxes)]


def late(state, speed, fresh, remapped):
    return pl.pallas_call(
        late_kernel,
        name="late",
        out_shape=(jax.ShapeDtypeStruct(fresh.shape, F32), pltpu.VMEM(fresh.shape, F32)),
        in_specs=[VMEM] * 3 + [ANY],
        out_specs=(ANY, VMEM),
        input_output_aliases={2: 1, 3: 0},
        scratch_shapes=[pltpu.SemaphoreType.DMA((8,)), pltpu.SemaphoreType.DMA((PARTS, 1))],
        compiler_params=pltpu.CompilerParams(vmem_limit_bytes=4 * MIB),
        cost_estimate=pl.CostEstimate(flops=5 * state.size, bytes_accessed=2 * state.size * 4, transcendentals=0),
    )(state, speed, fresh, remapped)[0]


def pick_kernel(place, own, first, second, out, table, lines):
    for k, part in enumerate((own, first, second)):
        table[k * 3 * CAP : (k + 1) * 3 * CAP, :] = part[...]
    for b in range(out.shape[0]):
        lines[b : b + 1, :] = table[pl.ds(place[b], 1), :]
    out[...] = lines[...].astype(BF16)


def pick(place, own, first, second):
    n_blocks = place.shape[0]
    return pl.pallas_call(
        pick_kernel,
        name="pick",
        out_shape=jax.ShapeDtypeStruct((n_blocks, BLK), BF16),
        in_specs=[SMEM, VMEM, VMEM, VMEM],
        out_specs=VMEM,
        scratch_shapes=[pltpu.VMEM((9 * CAP, BLK), F32), pltpu.VMEM((n_blocks, BLK), F32)],
        compiler_params=pltpu.CompilerParams(vmem_limit_bytes=2 * MIB),
    )(place, own, first, second)


def per_device(
    elem_volume,
    elem_velocity,
    elem_energy,
    elem_mat,
    elem_dest,
    tile_slot,
    tile_cell,
    tile_weight,
    tile_count,
    cell_state,
    mat_props,
):
    size_x, size_y = lax.axis_size("gx"), lax.axis_size("gy")
    n_blocks = elem_dest.shape[0]
    shape = (n_blocks, BLK)
    own, first, second, place, mat_props, tile_slot, tile_cell = payload(
        elem_dest,
        mat_props,
        elem_volume.reshape(shape),
        elem_velocity,
        elem_energy.reshape(shape),
        elem_mat.reshape(shape),
        tile_slot,
        tile_cell,
        size_y,
    )
    weight = fetch(tile_weight)

    first = swap(first, "gx", 1)
    second = swap(second, "gx", 2)
    weight, own = lax.optimization_barrier((weight, own))
    state, turned, slots, spots, points = stage(
        tile_slot, tile_cell, tile_count, cell_state, weight, size_y
    )

    def along_y(which):
        rows = slice(which * CAP, (which + 1) * CAP)
        return jnp.concatenate([own[rows], first[rows], second[rows]], axis=0)

    south = swap(along_y(1), "gy", 1)
    north = swap(along_y(2), "gy", 2)
    state, *edges = deposit(
        slots, spots, (own, first, second, south, north), weight, state
    )
    edges = (
        swap(edges[0], "gx", 1),
        swap(edges[1], "gx", 2),
        swap(edges[3], "gy", 2),
        swap(edges[2], "gy", 1, wrap=False),
    )
    fresh, press, speed = inner(mat_props, state, cell_state.shape[1])
    remapped, state, speed, fresh, own, first, second = outer(
        mat_props, slots, points, edges, turned, state, speed, press, fresh, size_x, size_y
    )
    remapped = late(state, speed, fresh, remapped)
    first = swap(first, "gy", 1)
    second = swap(second, "gy", 2)

    def along_x(which):
        rows = slice(which * CAP, (which + 1) * CAP)
        return jnp.concatenate([own[rows], first[rows], second[rows]], axis=0)

    back = pick(place, along_x(0), swap(along_x(1), "gx", 1), swap(along_x(2), "gx", 2))
    return remapped, back.reshape(n_blocks * BLK)


def solution(mesh):
    placed = (
        P(("gx", "gy")),
        P(None, ("gx", "gy")),
        P(("gx", "gy")),
        P(("gx", "gy")),
        P(("gx", "gy")),
        P(("gx", "gy")),
        P(("gx", "gy")),
        P(("gx", "gy"), None, None),
        P(("gx", "gy")),
        P(None, "gx", "gy"),
        P(),
    )
    return jax.shard_map(
        per_device,
        mesh=mesh,
        in_specs=placed,
        out_specs=(P(None, "gx", "gy"), P(("gx", "gy"))),
        check_vma=False,
    )
```

```python
import functools

import jax
import jax.numpy as jnp
from jax import lax
from jax.experimental import pallas as pl
from jax.experimental.pallas import tpu as pltpu
from jax.sharding import PartitionSpec as P

MAT = 8
NZ = 64
BLK = 128
CAP = 2
HALF = BLK // 2
PAD = 8
AFTER = 16
ROOM = PAD + AFTER
ROWS = 16
PAIR = 2
TOGETHER = 4
PARTS = 4
TURN = 16
GROUP = 8
DELAY = 4
MIB = 2**20

time_step = 0.8
F32 = jnp.float32
BF16 = jnp.bfloat16

SMEM = pl.BlockSpec(memory_space=pltpu.SMEM)
VMEM = pl.BlockSpec(memory_space=pltpu.VMEM)
ANY = pl.BlockSpec(memory_space=pl.ANY)


def partner(index, size, which):
    if which == 2:
        return index ^ 1
    return (index + 1 if index % 2 else index - 1) % size


def swap(value, axis, which, wrap=True):
    size = lax.axis_size(axis)
    pairs = [(i, partner(i, size, which)) for i in range(size)]
    if not wrap:
        pairs = [(i, j if abs(i - j) == 1 else i) for i, j in pairs]
    return lax.ppermute(value, axis, pairs)


def has_far(index, size):
    return (index > 0) & (index < size - 1)


def code_of(index, mine):
    return jnp.where(index == mine, 0, jnp.where(index == (mine ^ 1), 2, 1))


def split_device(device, size):
    if size & (size - 1) == 0:
        return device >> (size.bit_length() - 1), device & (size - 1)
    return lax.div(device, size), lax.rem(device, size)


def in_hbm(value):
    return pltpu.with_memory_space_constraint(value, pltpu.HBM)


def payload_kernel(
    dest_hbm, props_hbm, volume_hbm, velocity_hbm, energy_hbm, mat_hbm, slot_hbm, cell_hbm,
    own, first, second, place, props, slot_out, cell_out, dest, volume, velocity, energy, mat, seen, packed, sem, *, size_y
):
    moves = (
        (dest_hbm, dest), (props_hbm, props), (mat_hbm, mat),
        (volume_hbm, volume), (velocity_hbm, velocity), (energy_hbm, energy),
        (slot_hbm, slot_out), (cell_hbm, cell_out),
    )
    copies = [pltpu.make_async_copy(src, dst, sem.at[k]) for k, (src, dst) in enumerate(moves)]
    for copy in copies:
        copy.start()
    for copy in copies:
        copy.wait()
    pos_x, pos_y = lax.axis_index("gx"), lax.axis_index("gy")
    n_blocks = volume.shape[0]
    kinds = mat[...]
    density = jnp.zeros(kinds.shape, F32)
    for m in range(MAT):
        density = jnp.where(kinds == m, props[0, m], density)
    mass = volume[...] * density
    heat = mass * energy[...]
    level = lax.broadcasted_iota(jnp.int32, (MAT, BLK), 0)
    for k in range(9):
        seen[k] = 0
    for b in range(n_blocks):
        at_x, at_y = split_device(dest[b], size_y)
        near = code_of(at_x, pos_x) * 3 + code_of(at_y, pos_y)
        rank = seen[near]
        seen[near] = rank + 1
        slot = near * CAP + rank
        place[b] = slot
        volumes = jnp.where(kinds[b : b + 1] == level, volume[b : b + 1, :], 0.0)
        momentum = mass[b : b + 1] * velocity[:, b * BLK : (b + 1) * BLK]
        rows = jnp.concatenate([volumes, momentum, heat[b : b + 1], jnp.zeros((4, BLK), F32)], axis=0)
        packed[slot] = rows.astype(BF16)
    for k, out in enumerate((own, first, second)):
        for s in range(3 * CAP):
            out[s] = packed[k * 3 * CAP + s]


def payload(dest, props, volume, velocity, energy, mat, tile_slot, tile_cell, size_y):
    n_blocks = volume.shape[0]
    parcel = pltpu.VMEM((3 * CAP, ROWS, BLK), BF16)
    return pl.pallas_call(
        functools.partial(payload_kernel, size_y=size_y),
        name="payload",
        out_shape=(
            parcel,
            parcel,
            parcel,
            pltpu.SMEM((n_blocks,), jnp.int32),
            pltpu.SMEM(props.shape, F32),
            pltpu.SMEM(tile_slot.shape, jnp.int32),
            pltpu.SMEM(tile_cell.shape, jnp.int32),
        ),
        in_specs=[ANY] * 8,
        out_specs=(VMEM, VMEM, VMEM, SMEM, SMEM, SMEM, SMEM),
        scratch_shapes=[
            pltpu.SMEM(dest.shape, jnp.int32),
            pltpu.VMEM(volume.shape, F32),
            pltpu.VMEM(velocity.shape, F32),
            pltpu.VMEM(energy.shape, F32),
            pltpu.VMEM(mat.shape, jnp.int32),
            pltpu.SMEM((9,), jnp.int32),
            pltpu.VMEM((9 * CAP, ROWS, BLK), BF16),
            pltpu.SemaphoreType.DMA((8,)),
        ],
        compiler_params=pltpu.CompilerParams(vmem_limit_bytes=4 * MIB),
    )(*(in_hbm(value) for value in (dest, props, volume, velocity, energy, mat, tile_slot, tile_cell)))


def stage_kernel(
    tile_slot, tile_cell, tile_count, cell, weight, state, turned, slots, spots, points, sem, *, size_y
):
    pos_x, pos_y = lax.axis_index("gx"), lax.axis_index("gy")
    columns, count, tall = state.shape[0] - 2, state.shape[1], state.shape[2]
    width = tall - ROOM
    copies = [
        pltpu.make_async_copy(
            cell.at[:, :, pl.ds(j * BLK, BLK)], state.at[j + 1, :, pl.ds(PAD, width)], sem.at[j]
        )
        for j in range(columns)
    ]
    for copy in copies:
        copy.start()

    counted = tile_count[0]

    def turn_and_index(step, carry):
        for k in range(TURN):
            t = step * TURN + k
            turned[t] = weight[t].T
            x, j = split_device(tile_cell[t], columns)
            slots[t] = jnp.where(t < counted, local_slot(tile_slot[t], pos_x, pos_y, size_y), 9 * CAP)
            spots[t] = (j + 1) * (count * tall) + x + PAD
            points[t] = j * width + x
        return carry

    lax.fori_loop(0, weight.shape[0] // TURN, turn_and_index, 0)
    for copy in copies:
        copy.wait()


def stage(tile_slot, tile_cell, tile_count, cell, weight, size_y):
    count, width, lanes = cell.shape
    columns = lanes // BLK
    indices = pltpu.SMEM(tile_slot.shape, jnp.int32)
    return pl.pallas_call(
        functools.partial(stage_kernel, size_y=size_y),
        name="stage",
        out_shape=(
            pltpu.VMEM((columns + 2, count, width + ROOM, BLK), F32),
            pltpu.VMEM(weight.shape, weight.dtype),
            indices,
            indices,
            indices,
        ),
        in_specs=[SMEM, SMEM, SMEM, ANY, VMEM],
        out_specs=(VMEM, VMEM, SMEM, SMEM, SMEM),
        scratch_shapes=[pltpu.SemaphoreType.DMA((columns,))],
        compiler_params=pltpu.CompilerParams(vmem_limit_bytes=2 * MIB),
        cost_estimate=pl.CostEstimate(flops=0, bytes_accessed=2 * cell.size * 4, transcendentals=0),
    )(tile_slot, tile_cell, tile_count, in_hbm(cell), weight)


def fetch_kernel(source, target, sem):
    copy = pltpu.make_async_copy(source, target, sem)
    copy.start()
    copy.wait()


def fetch(value):
    return pl.pallas_call(
        fetch_kernel,
        name="fetch",
        out_shape=pltpu.VMEM(value.shape, value.dtype),
        in_specs=[ANY],
        out_specs=VMEM,
        scratch_shapes=[pltpu.SemaphoreType.DMA],
        compiler_params=pltpu.CompilerParams(vmem_limit_bytes=2 * MIB),
        cost_estimate=pl.CostEstimate(flops=0, bytes_accessed=2 * value.size * 2, transcendentals=0),
    )(in_hbm(value))


def local_slot(slot, pos_x, pos_y, size_y):
    at_x, at_y = split_device(slot >> 1, size_y)
    return code_of(at_y, pos_y) * (3 * CAP) + code_of(at_x, pos_x) * CAP + (slot & 1)


def low_lanes():
    return lax.broadcasted_iota(jnp.int32, (1, BLK), 1) < HALF


def turn(value):
    return pltpu.roll(value, HALF, value.ndim - 1)


def beside(weight, t):
    return jnp.concatenate([weight[t], weight[t + 1]], axis=1)


def add_at(buffer, places, index, values):
    held = [buffer[index(place)] for place in places]
    for k, place in enumerate(places):
        value = values[k]
        for earlier in range(k):
            value = value + jnp.where(places[earlier] == place, values[earlier], 0.0)
        buffer[index(place)] = held[k] + value


def deposit_kernel(
    slots, spots, own, first, second, north, south, weight, state_in,
    state, edge_x1, edge_x2, edge_y1, edge_y2, rows
):
    pos_x, pos_y = lax.axis_index("gx"), lax.axis_index("gy")
    n_tiles = weight.shape[0]
    columns, count, tall = state.shape[0] - 2, state.shape[1], state.shape[2]
    line = state.reshape((columns + 2) * count * tall, BLK)
    rows[9 * CAP] = jnp.zeros(rows.shape[1:], BF16)
    for k, part in enumerate((own, first, second)):
        for r in range(CAP):
            rows[k * CAP + r] = part[r]
    for k, part in enumerate((south, north)):
        for r in range(3 * CAP):
            rows[(k + 1) * 3 * CAP + r] = part[r]
    for first_tile in range(0, n_tiles, TOGETHER):
        tiles = range(first_tile, first_tile + TOGETHER)
        contribs = []
        for t in tiles[::2]:
            both = jnp.concatenate([rows[slots[t]], rows[slots[t + 1]]], axis=0)
            found = jnp.dot(both, beside(weight, t), preferred_element_type=F32)
            contribs += [found[:count, :BLK], found[ROWS : ROWS + count, BLK:]]
        add_at(line, [spots[t] for t in tiles], lambda place: (pl.ds(place, count, stride=tall), slice(None)), contribs)

    even_x, even_y = (pos_x & 1) == 0, (pos_y & 1) == 0
    width = tall - ROOM
    top, bottom = PAD + width - 1, PAD
    for edge, row in (
        (edge_x1, jnp.where(even_x, bottom, top)),
        (edge_x2, jnp.where(even_x, top, bottom)),
    ):
        for q in range(count):
            at = pl.ds(count * tall + q * tall + row, columns, stride=count * tall)
            edge[q * columns : (q + 1) * columns, :] = line[at, :].astype(BF16)
    low = low_lanes()
    for edge, upper in ((edge_y1, jnp.logical_not(even_y)), (edge_y2, even_y)):
        column = jnp.where(upper, columns, 1)
        for q in range(count // 2):
            for i in range(width // ROWS):
                here = slice(PAD + i * ROWS, PAD + (i + 1) * ROWS)
                a = state[column, q, here, :]
                b = state[column, q + count // 2, here, :]
                both = jnp.where(low, jnp.where(upper, turn(a), a), jnp.where(upper, b, turn(b)))
                edge[q * width + i * ROWS : q * width + (i + 1) * ROWS, :] = both.astype(BF16)


def deposit(slots, spots, parts, weight, state):
    columns, count, tall = state.shape[0] - 2, state.shape[1], state.shape[2]
    edge_x = pltpu.VMEM((count * columns, BLK), BF16)
    edge_y = pltpu.VMEM((count // 2 * (tall - ROOM), BLK), BF16)
    return pl.pallas_call(
        deposit_kernel,
        name="deposit",
        out_shape=(pltpu.VMEM(state.shape, F32), edge_x, edge_x, edge_y, edge_y),
        in_specs=[SMEM] * 2 + [VMEM] * 7,
        out_specs=(VMEM,) * 5,
        input_output_aliases={8: 0},
        scratch_shapes=[pltpu.VMEM((9 * CAP + 1, ROWS, BLK), BF16)],
        compiler_params=pltpu.CompilerParams(vmem_limit_bytes=4 * MIB),
    )(slots, spots, *parts, weight, state)


def total(terms):
    while len(terms) > 1:
        terms = [a + b for a, b in zip(terms[::2], terms[1::2], strict=True)]
    return terms[0]


def speeds_at(props, state, j, here, parts):
    share = 1.0 / (1.0 + total([props[0, m] * state[j, m, here, :] for m in range(MAT)]))
    found = []
    if 0 in parts:
        found.append((0, state[j, MAT, here, :] * share))
    if 1 in parts:
        along = state[j, MAT + 1, here, :] * share
        found += [(1, along), (2, turn(along))]
    return found


def store_speeds(props, state, speed, places, parts):
    waiting = []
    for step in range(len(places) + DELAY):
        if step < len(places):
            j, first_row = places[step]
            waiting.append(speeds_at(props, state, j, slice(first_row, first_row + 8), parts))
        if step >= DELAY:
            j, first_row = places[step - DELAY]
            for plane, value in waiting.pop(0):
                speed[j, plane, first_row : first_row + 8, :] = value


def weights_at(speed, j, first_row):
    low = low_lanes()
    here = slice(first_row, first_row + 8)
    scale = 0.5 * time_step
    ux = speed[j, 0, here, :]
    lower = scale * (speed[j, 0, slice(first_row - 1, first_row + 7), :] + ux)
    upper = scale * (ux + speed[j, 0, slice(first_row + 1, first_row + 9), :])
    uy, before, after = (speed[k, 1, here, :] for k in (j, j - 1, j + 1))
    turned, turned_before, turned_after = (speed[k, 2, here, :] for k in (j, j - 1, j + 1))
    left = scale * (jnp.where(low, turned_before, turned) + uy)
    right = scale * (uy + jnp.where(low, turned, turned_after))
    keep = 1.0 - (
        (jnp.maximum(upper, 0.0) + jnp.maximum(-lower, 0.0)) + (jnp.maximum(right, 0.0) + jnp.maximum(-left, 0.0))
    )
    take_left = jnp.maximum(scale * (jnp.where(low, uy, before) + turned), 0.0)
    take_right = jnp.maximum(-scale * (turned + jnp.where(low, after, uy)), 0.0)
    same = jnp.where(low, take_left, take_right)
    other = jnp.where(low, take_right, take_left)
    return keep, jnp.maximum(lower, 0.0), jnp.maximum(-upper, 0.0), same, other


def values_at(state, weights, j, first_row, wanted):
    low = low_lanes()
    here = slice(first_row, first_row + 8)
    before = slice(first_row - 1, first_row + 7)
    after = slice(first_row + 1, first_row + 9)
    keep, take_before, take_after, same, other = weights
    values = []
    for q in wanted:
        mid = state[j, q, here, :]
        beside = jnp.where(low, state[j + 1, q, here, :], state[j - 1, q, here, :])
        value = (keep * mid + take_before * state[j, q, before, :]) + take_after * state[j, q, after, :]
        values.append(value + turn(same * mid + other * beside))
    return values


def pressure_of(props, values):
    terms = [value * (props[1, m] + (0.5 * props[1, m]) * value) for m, value in enumerate(values[:MAT])]
    return total(terms) + 0.4 * values[-1]


def remap_tiles(props, state, speed, press, fresh, places, wanted):
    weights, values = {}, {}
    for step in range(len(places) + 2):
        if step < len(places):
            weights[step] = weights_at(speed, *places[step])
        k = step - 1
        if 0 <= k < len(places):
            values[k] = values_at(state, weights.pop(k), *places[k], wanted)
        k = step - 2
        if k >= 0:
            found = values.pop(k)
            j, first_row = places[k]
            inside = slice(first_row - PAD, first_row - PAD + 8)
            lanes = column_lanes(j)
            for q, value in zip(wanted, found, strict=True):
                fresh[q, inside, lanes] = value
            if press is not None:
                press[j - 1, inside, :] = pressure_of(props, found)


def scalars(count):
    return [*range(MAT), count - 1]


def column_lanes(j):
    if isinstance(j, int):
        return slice((j - 1) * BLK, j * BLK)
    return pl.ds(pl.multiple_of((j - 1) * BLK, BLK), BLK)


def inner_kernel(props, state, fresh, press, speed):
    columns, tall = state.shape[0] - 2, state.shape[2]

    def speeds(step, carry):
        rows = range(PAD, tall - AFTER, 8)
        places = [(1 + step * GROUP + k, row) for k in range(GROUP) for row in rows]
        store_speeds(props, state, speed, places, (0, 1))
        return carry

    lax.fori_loop(0, columns // GROUP, speeds, 0)

    def remap(step, carry):
        rows = range(PAD + 8, tall - AFTER - 8, 8)
        places = [(2 + step * PAIR + k, row) for k in range(PAIR) for row in rows]
        remap_tiles(props, state, speed, press, fresh, places, scalars(state.shape[1]))
        return carry

    lax.fori_loop(0, (columns - 2) // PAIR, remap, 0)


def inner(props, state, width):
    columns, count, tall = state.shape[0] - 2, state.shape[1], state.shape[2]
    return pl.pallas_call(
        inner_kernel,
        name="inner",
        out_shape=(
            pltpu.VMEM((count, width, columns * BLK), F32),
            pltpu.VMEM((columns, width, BLK), F32),
            pltpu.VMEM((columns + 2, 3, tall, BLK), F32),
        ),
        in_specs=[SMEM, VMEM],
        out_specs=(VMEM, VMEM, VMEM),
        compiler_params=pltpu.CompilerParams(vmem_limit_bytes=4 * MIB),
        cost_estimate=pl.CostEstimate(flops=20 * state.size, bytes_accessed=2 * state.size * 4, transcendentals=0),
    )(props, state)


def outer_kernel(
    props, slots, points, edge_x1, edge_x2, edge_y2, edge_y1, weight, state_in, speed_in, press_in,
    fresh_in, remapped, state, speed, press, fresh, own, first, second, sums, sem, *, size_x, size_y
):
    pos_x, pos_y = lax.axis_index("gx"), lax.axis_index("gy")
    n_tiles = weight.shape[0]
    columns, count, tall = state.shape[0] - 2, state.shape[1], state.shape[2]
    width = tall - ROOM
    copies = area_copies(fresh, remapped, sem, scalar_planes(count), [inner_area(fresh)])
    for copy in copies:
        copy.start()
    even_x, even_y = (pos_x & 1) == 0, (pos_y & 1) == 0
    line = state.reshape((columns + 2) * count * tall, BLK)
    above, below = PAD + width, PAD - 1
    for edge, row, there in (
        (edge_x1, jnp.where(even_x, below, above), has_far(pos_x, size_x)),
        (edge_x2, jnp.where(even_x, above, below), True),
    ):
        for q in range(count):
            at = pl.ds(count * tall + q * tall + row, columns, stride=count * tall)
            line[at, :] = jnp.where(there, edge[q * columns : (q + 1) * columns, :].astype(F32), 0.0)
    low = low_lanes()
    for edge, column, there in (
        (edge_y1, jnp.where(even_y, 0, columns + 1), has_far(pos_y, size_y)),
        (edge_y2, jnp.where(even_y, columns + 1, 0), True),
    ):
        for q in range(count // 2):
            for i in range(width // ROWS):
                here = slice(PAD + i * ROWS, PAD + (i + 1) * ROWS)
                both = edge[q * width + i * ROWS : q * width + (i + 1) * ROWS, :].astype(F32)
                both = jnp.where(there, both, 0.0)
                turned = turn(both)
                state[column, q, here, :] = jnp.where(low, both, turned)
                state[column, q + count // 2, here, :] = jnp.where(low, turned, both)

    places = [(j, row) for j in range(1, columns + 1) for row in (0, tall - AFTER)]
    store_speeds(props, state, speed, places, (0,))
    places = [(j, row) for j in (0, columns + 1) for row in range(PAD, tall - AFTER, 8)]
    store_speeds(props, state, speed, places, (1,))

    def sides(step, carry):
        places = [(1 + step * 2 * PAIR + k, row) for k in range(2 * PAIR) for row in (PAD, tall - AFTER - 8)]
        remap_tiles(props, state, speed, press, fresh, places, scalars(state.shape[1]))
        return carry

    lax.fori_loop(0, columns // (2 * PAIR), sides, 0)
    places = [(j, row) for j in (1, columns) for row in range(PAD + 8, tall - AFTER - 8, 8)]
    remap_tiles(props, state, speed, press, fresh, places, scalars(state.shape[1]))

    sums[...] = jnp.zeros(sums.shape, F32)
    line_of = lax.broadcasted_iota(jnp.int32, (ROWS, BLK), 0)
    field = press.reshape(columns * width, BLK)
    for first_tile in range(0, n_tiles, TOGETHER):
        tiles = range(first_tile, first_tile + TOGETHER)
        found = []
        for t in tiles[::2]:
            one, two = (field[pl.ds(points[k], 1), :] for k in (t, t + 1))
            probe = jnp.where(line_of == 0, one, jnp.where(line_of == 8, two, 1.0)).astype(BF16)
            both = jnp.dot(probe, beside(weight, t), preferred_element_type=F32)
            found += [both[:8, :BLK], both[8:, BLK:]]
        add_at(sums, [slots[t] for t in tiles], lambda place: place, found)
    table = sums.reshape(sums.shape[0] * 8, BLK)
    for k, out in enumerate((own, first, second)):
        top = table[pl.ds(k * 3 * CAP * 8, 3 * CAP, stride=8), :]
        under = table[pl.ds(k * 3 * CAP * 8 + 1, 3 * CAP, stride=8), :]
        out[...] = top / jnp.maximum(under, 1.0)
    for copy in copies:
        copy.wait()


def outer(props, slots, points, edges, weight, state, speed, press, fresh, size_x, size_y):
    answer = pltpu.VMEM((3 * CAP, BLK), F32)
    outs = pl.pallas_call(
        functools.partial(outer_kernel, size_x=size_x, size_y=size_y),
        name="outer",
        out_shape=(
            jax.ShapeDtypeStruct(fresh.shape, F32),
            pltpu.VMEM(state.shape, F32),
            pltpu.VMEM(speed.shape, F32),
            pltpu.VMEM(press.shape, F32),
            pltpu.VMEM(fresh.shape, F32),
            answer,
            answer,
            answer,
        ),
        in_specs=[SMEM] * 3 + [VMEM] * 9,
        out_specs=(ANY,) + (VMEM,) * 7,
        input_output_aliases={8: 1, 9: 2, 10: 3, 11: 4},
        scratch_shapes=[pltpu.VMEM((9 * CAP + 1, 8, BLK), F32), pltpu.SemaphoreType.DMA((2,))],
        compiler_params=pltpu.CompilerParams(vmem_limit_bytes=4 * MIB),
    )(props, slots, points, *edges, weight, state, speed, press, fresh)
    return outs[0], outs[1], outs[2], outs[4], outs[5], outs[6], outs[7]


def late_kernel(state, speed, fresh_in, remapped_in, remapped, fresh, sem, sem_moving):
    columns, count, tall = state.shape[0] - 2, state.shape[1], state.shape[2]
    width, lanes = fresh.shape[1], fresh.shape[2]
    rows = pl.ds(8, width - 16)
    areas = [
        (pl.ds(0, 8), pl.ds(0, lanes)),
        (pl.ds(width - 8, 8), pl.ds(0, lanes)),
        (rows, pl.ds(0, BLK)),
        (rows, pl.ds(lanes - BLK, BLK)),
    ]
    copies = area_copies(fresh, remapped, sem, scalar_planes(count), areas)
    for copy in copies:
        copy.start()
    for part in range(PARTS):
        held = range(1 + part * columns // PARTS, 1 + (part + 1) * columns // PARTS)
        places = [(j, row) for j in held for row in range(PAD, tall - AFTER, 8)]
        remap_tiles(None, state, speed, None, fresh, places, range(MAT, count - 1))
        area = (pl.ds(0, width), pl.ds((held[0] - 1) * BLK, len(held) * BLK))
        copies += area_copies(fresh, remapped, sem_moving.at[part], [pl.ds(MAT, count - 1 - MAT)], [area])
        copies[-1].start()
    for copy in copies:
        copy.wait()


def scalar_planes(count):
    return [pl.ds(0, MAT), pl.ds(count - 1, 1)]


def inner_area(fresh):
    return pl.ds(8, fresh.shape[1] - 16), pl.ds(BLK, fresh.shape[2] - 2 * BLK)


def area_copies(fresh, remapped, sem, planes, areas):
    boxes = [(plane, *area) for area in areas for plane in planes]
    return [pltpu.make_async_copy(fresh.at[box], remapped.at[box], sem.at[k]) for k, box in enumerate(boxes)]


def late(state, speed, fresh, remapped):
    return pl.pallas_call(
        late_kernel,
        name="late",
        out_shape=(jax.ShapeDtypeStruct(fresh.shape, F32), pltpu.VMEM(fresh.shape, F32)),
        in_specs=[VMEM] * 3 + [ANY],
        out_specs=(ANY, VMEM),
        input_output_aliases={2: 1, 3: 0},
        scratch_shapes=[pltpu.SemaphoreType.DMA((8,)), pltpu.SemaphoreType.DMA((PARTS, 1))],
        compiler_params=pltpu.CompilerParams(vmem_limit_bytes=4 * MIB),
        cost_estimate=pl.CostEstimate(flops=5 * state.size, bytes_accessed=2 * state.size * 4, transcendentals=0),
    )(state, speed, fresh, remapped)[0]


def pick_kernel(place, own, first, second, out, table, lines):
    for k, part in enumerate((own, first, second)):
        table[k * 3 * CAP : (k + 1) * 3 * CAP, :] = part[...]
    for b in range(out.shape[0]):
        lines[b : b + 1, :] = table[pl.ds(place[b], 1), :]
    out[...] = lines[...].astype(BF16)


def pick(place, own, first, second):
    n_blocks = place.shape[0]
    return pl.pallas_call(
        pick_kernel,
        name="pick",
        out_shape=jax.ShapeDtypeStruct((n_blocks, BLK), BF16),
        in_specs=[SMEM, VMEM, VMEM, VMEM],
        out_specs=VMEM,
        scratch_shapes=[pltpu.VMEM((9 * CAP, BLK), F32), pltpu.VMEM((n_blocks, BLK), F32)],
        compiler_params=pltpu.CompilerParams(vmem_limit_bytes=2 * MIB),
    )(place, own, first, second)


def per_device(
    elem_volume,
    elem_velocity,
    elem_energy,
    elem_mat,
    elem_dest,
    tile_slot,
    tile_cell,
    tile_weight,
    tile_count,
    cell_state,
    mat_props,
):
    size_x, size_y = lax.axis_size("gx"), lax.axis_size("gy")
    n_blocks = elem_dest.shape[0]
    shape = (n_blocks, BLK)
    own, first, second, place, mat_props, tile_slot, tile_cell = payload(
        elem_dest,
        mat_props,
        elem_volume.reshape(shape),
        elem_velocity,
        elem_energy.reshape(shape),
        elem_mat.reshape(shape),
        tile_slot,
        tile_cell,
        size_y,
    )
    weight = fetch(tile_weight)

    first = swap(first, "gx", 1)
    second = swap(second, "gx", 2)
    weight, own = lax.optimization_barrier((weight, own))
    state, turned, slots, spots, points = stage(
        tile_slot, tile_cell, tile_count, cell_state, weight, size_y
    )

    def along_y(which):
        rows = slice(which * CAP, (which + 1) * CAP)
        return jnp.concatenate([own[rows], first[rows], second[rows]], axis=0)

    south = swap(along_y(1), "gy", 1)
    north = swap(along_y(2), "gy", 2)
    state, *edges = deposit(
        slots, spots, (own, first, second, north, south), weight, state
    )
    edges = (
        swap(edges[0], "gx", 1),
        swap(edges[1], "gx", 2),
        swap(edges[3], "gy", 2),
        swap(edges[2], "gy", 1, wrap=False),
    )
    fresh, press, speed = inner(mat_props, state, cell_state.shape[1])
    remapped, state, speed, fresh, own, first, second = outer(
        mat_props, slots, points, edges, turned, state, speed, press, fresh, size_x, size_y
    )
    remapped = late(state, speed, fresh, remapped)
    first = swap(first, "gy", 1)
    second = swap(second, "gy", 2)

    def along_x(which):
        rows = slice(which * CAP, (which + 1) * CAP)
        return jnp.concatenate([own[rows], first[rows], second[rows]], axis=0)

    back = pick(place, along_x(0), swap(along_x(1), "gx", 1), swap(along_x(2), "gx", 2))
    return remapped, back.reshape(n_blocks * BLK)


def solution(mesh):
    placed = (
        P(("gx", "gy")),
        P(None, ("gx", "gy")),
        P(("gx", "gy")),
        P(("gx", "gy")),
        P(("gx", "gy")),
        P(("gx", "gy")),
        P(("gx", "gy")),
        P(("gx", "gy"), None, None),
        P(("gx", "gy")),
        P(None, "gx", "gy"),
        P(),
    )
    return jax.shard_map(
        per_device,
        mesh=mesh,
        in_specs=placed,
        out_specs=(P(None, "gx", "gy"), P(("gx", "gy"))),
        check_vma=False,
    )
```

```python
import functools

import jax
import jax.numpy as jnp
from jax import lax
from jax.experimental import pallas as pl
from jax.experimental.pallas import tpu as pltpu
from jax.sharding import PartitionSpec as P

MAT = 8
NZ = 64
BLK = 128
CAP = 2
HALF = BLK // 2
PAD = 8
AFTER = 16
ROOM = PAD + AFTER
ROWS = 16
PAIR = 7
TOGETHER = 4
PARTS = 4
TURN = 16
GROUP = 16
DELAY = 4
MIB = 2**20

time_step = 0.8
F32 = jnp.float32
BF16 = jnp.bfloat16

SMEM = pl.BlockSpec(memory_space=pltpu.SMEM)
VMEM = pl.BlockSpec(memory_space=pltpu.VMEM)
ANY = pl.BlockSpec(memory_space=pl.ANY)


def partner(index, size, which):
    if which == 2:
        return index ^ 1
    return (index + 1 if index % 2 else index - 1) % size


def swap(value, axis, which, wrap=True):
    size = lax.axis_size(axis)
    pairs = [(i, partner(i, size, which)) for i in range(size)]
    if not wrap:
        pairs = [(i, j if abs(i - j) == 1 else i) for i, j in pairs]
    return lax.ppermute(value, axis, pairs)


def has_far(index, size):
    return (index > 0) & (index < size - 1)


def code_of(index, mine):
    return jnp.where(index == mine, 0, jnp.where(index == (mine ^ 1), 2, 1))


def split_device(device, size):
    if size & (size - 1) == 0:
        return device >> (size.bit_length() - 1), device & (size - 1)
    return lax.div(device, size), lax.rem(device, size)


def in_hbm(value):
    return pltpu.with_memory_space_constraint(value, pltpu.HBM)


def payload_kernel(
    dest_hbm, props_hbm, volume_hbm, velocity_hbm, energy_hbm, mat_hbm, slot_hbm, cell_hbm,
    own, first, second, place, props, slot_out, cell_out, dest, volume, velocity, energy, mat, seen, packed, sem, *, size_y
):
    moves = (
        (dest_hbm, dest), (props_hbm, props), (mat_hbm, mat),
        (volume_hbm, volume), (velocity_hbm, velocity), (energy_hbm, energy),
        (slot_hbm, slot_out), (cell_hbm, cell_out),
    )
    copies = [pltpu.make_async_copy(src, dst, sem.at[k]) for k, (src, dst) in enumerate(moves)]
    for copy in copies:
        copy.start()
    for copy in copies:
        copy.wait()
    pos_x, pos_y = lax.axis_index("gx"), lax.axis_index("gy")
    n_blocks = volume.shape[0]
    kinds = mat[...]
    density = jnp.zeros(kinds.shape, F32)
    for m in range(MAT):
        density = jnp.where(kinds == m, props[0, m], density)
    mass = volume[...] * density
    heat = mass * energy[...]
    level = lax.broadcasted_iota(jnp.int32, (MAT, BLK), 0)
    for k in range(9):
        seen[k] = 0
    for b in range(n_blocks):
        at_x, at_y = split_device(dest[b], size_y)
        near = code_of(at_x, pos_x) * 3 + code_of(at_y, pos_y)
        rank = seen[near]
        seen[near] = rank + 1
        slot = near * CAP + rank
        place[b] = slot
        volumes = jnp.where(kinds[b : b + 1] == level, volume[b : b + 1, :], 0.0)
        momentum = mass[b : b + 1] * velocity[:, b * BLK : (b + 1) * BLK]
        rows = jnp.concatenate([volumes, momentum, heat[b : b + 1], jnp.zeros((4, BLK), F32)], axis=0)
        packed[slot] = rows.astype(BF16)
    for k, out in enumerate((own, first, second)):
        for s in range(3 * CAP):
            out[s] = packed[k * 3 * CAP + s]


def payload(dest, props, volume, velocity, energy, mat, tile_slot, tile_cell, size_y):
    n_blocks = volume.shape[0]
    parcel = pltpu.VMEM((3 * CAP, ROWS, BLK), BF16)
    return pl.pallas_call(
        functools.partial(payload_kernel, size_y=size_y),
        name="payload",
        out_shape=(
            parcel,
            parcel,
            parcel,
            pltpu.SMEM((n_blocks,), jnp.int32),
            pltpu.SMEM(props.shape, F32),
            pltpu.SMEM(tile_slot.shape, jnp.int32),
            pltpu.SMEM(tile_cell.shape, jnp.int32),
        ),
        in_specs=[ANY] * 8,
        out_specs=(VMEM, VMEM, VMEM, SMEM, SMEM, SMEM, SMEM),
        scratch_shapes=[
            pltpu.SMEM(dest.shape, jnp.int32),
            pltpu.VMEM(volume.shape, F32),
            pltpu.VMEM(velocity.shape, F32),
            pltpu.VMEM(energy.shape, F32),
            pltpu.VMEM(mat.shape, jnp.int32),
            pltpu.SMEM((9,), jnp.int32),
            pltpu.VMEM((9 * CAP, ROWS, BLK), BF16),
            pltpu.SemaphoreType.DMA((8,)),
        ],
        compiler_params=pltpu.CompilerParams(vmem_limit_bytes=4 * MIB),
    )(*(in_hbm(value) for value in (dest, props, volume, velocity, energy, mat, tile_slot, tile_cell)))


def stage_kernel(
    tile_slot, tile_cell, tile_count, cell, weight, state, turned, slots, spots, points, sem, *, size_y
):
    pos_x, pos_y = lax.axis_index("gx"), lax.axis_index("gy")
    columns, count, tall = state.shape[0] - 2, state.shape[1], state.shape[2]
    width = tall - ROOM
    copies = [
        pltpu.make_async_copy(
            cell.at[:, :, pl.ds(j * BLK, BLK)], state.at[j + 1, :, pl.ds(PAD, width)], sem.at[j]
        )
        for j in range(columns)
    ]
    for copy in copies:
        copy.start()

    counted = tile_count[0]

    def turn_and_index(step, carry):
        for k in range(TURN):
            t = step * TURN + k
            turned[t] = weight[t].T
            x, j = split_device(tile_cell[t], columns)
            slots[t] = jnp.where(t < counted, local_slot(tile_slot[t], pos_x, pos_y, size_y), 9 * CAP)
            spots[t] = (j + 1) * (count * tall) + x + PAD
            points[t] = j * width + x
        return carry

    lax.fori_loop(0, weight.shape[0] // TURN, turn_and_index, 0)
    for copy in copies:
        copy.wait()


def stage(tile_slot, tile_cell, tile_count, cell, weight, size_y):
    count, width, lanes = cell.shape
    columns = lanes // BLK
    indices = pltpu.SMEM(tile_slot.shape, jnp.int32)
    return pl.pallas_call(
        functools.partial(stage_kernel, size_y=size_y),
        name="stage",
        out_shape=(
            pltpu.VMEM((columns + 2, count, width + ROOM, BLK), F32),
            pltpu.VMEM(weight.shape, weight.dtype),
            indices,
            indices,
            indices,
        ),
        in_specs=[SMEM, SMEM, SMEM, ANY, VMEM],
        out_specs=(VMEM, VMEM, SMEM, SMEM, SMEM),
        scratch_shapes=[pltpu.SemaphoreType.DMA((columns,))],
        compiler_params=pltpu.CompilerParams(vmem_limit_bytes=2 * MIB),
        cost_estimate=pl.CostEstimate(flops=0, bytes_accessed=2 * cell.size * 4, transcendentals=0),
    )(tile_slot, tile_cell, tile_count, in_hbm(cell), weight)


def fetch_kernel(source, target, sem):
    copy = pltpu.make_async_copy(source, target, sem)
    copy.start()
    copy.wait()


def fetch(value):
    return pl.pallas_call(
        fetch_kernel,
        name="fetch",
        out_shape=pltpu.VMEM(value.shape, value.dtype),
        in_specs=[ANY],
        out_specs=VMEM,
        scratch_shapes=[pltpu.SemaphoreType.DMA],
        compiler_params=pltpu.CompilerParams(vmem_limit_bytes=2 * MIB),
        cost_estimate=pl.CostEstimate(flops=0, bytes_accessed=2 * value.size * 2, transcendentals=0),
    )(in_hbm(value))


def local_slot(slot, pos_x, pos_y, size_y):
    at_x, at_y = split_device(slot >> 1, size_y)
    return code_of(at_y, pos_y) * (3 * CAP) + code_of(at_x, pos_x) * CAP + (slot & 1)


def low_lanes():
    return lax.broadcasted_iota(jnp.int32, (1, BLK), 1) < HALF


def turn(value):
    return pltpu.roll(value, HALF, value.ndim - 1)


def beside(weight, t):
    return jnp.concatenate([weight[t], weight[t + 1]], axis=1)


def add_at(buffer, places, index, values):
    held = [buffer[index(place)] for place in places]
    for k, place in enumerate(places):
        value = values[k]
        for earlier in range(k):
            value = value + jnp.where(places[earlier] == place, values[earlier], 0.0)
        buffer[index(place)] = held[k] + value


def deposit_kernel(
    slots, spots, own, first, second, south, north, weight, state_in,
    state, edge_x1, edge_x2, edge_y1, edge_y2, rows
):
    pos_x, pos_y = lax.axis_index("gx"), lax.axis_index("gy")
    n_tiles = weight.shape[0]
    columns, count, tall = state.shape[0] - 2, state.shape[1], state.shape[2]
    line = state.reshape((columns + 2) * count * tall, BLK)
    rows[9 * CAP] = jnp.zeros(rows.shape[1:], BF16)
    for k, part in enumerate((own, first, second)):
        for r in range(CAP):
            rows[k * CAP + r] = part[r]
    for k, part in enumerate((south, north)):
        for r in range(3 * CAP):
            rows[(k + 1) * 3 * CAP + r] = part[r]
    for first_tile in range(0, n_tiles, 2):
        tiles = range(first_tile, first_tile + 2)
        contribs = []
        for t in tiles[::2]:
            both = jnp.concatenate([rows[slots[t]], rows[slots[t + 1]]], axis=0)
            found = jnp.dot(both, beside(weight, t), preferred_element_type=F32)
            contribs += [found[:count, :BLK], found[ROWS : ROWS + count, BLK:]]
        add_at(line, [spots[t] for t in tiles], lambda place: (pl.ds(place, count, stride=tall), slice(None)), contribs)

    even_x, even_y = (pos_x & 1) == 0, (pos_y & 1) == 0
    width = tall - ROOM
    top, bottom = PAD + width - 1, PAD
    for edge, row in (
        (edge_x1, jnp.where(even_x, bottom, top)),
        (edge_x2, jnp.where(even_x, top, bottom)),
    ):
        for q in range(count):
            at = pl.ds(count * tall + q * tall + row, columns, stride=count * tall)
            edge[q * columns : (q + 1) * columns, :] = line[at, :].astype(BF16)
    low = low_lanes()
    for edge, upper in ((edge_y1, jnp.logical_not(even_y)), (edge_y2, even_y)):
        column = jnp.where(upper, columns, 1)
        for q in range(count // 2):
            for i in range(width // ROWS):
                here = slice(PAD + i * ROWS, PAD + (i + 1) * ROWS)
                a = state[column, q, here, :]
                b = state[column, q + count // 2, here, :]
                both = jnp.where(low, jnp.where(upper, turn(a), a), jnp.where(upper, b, turn(b)))
                edge[q * width + i * ROWS : q * width + (i + 1) * ROWS, :] = both.astype(BF16)


def deposit(slots, spots, parts, weight, state):
    columns, count, tall = state.shape[0] - 2, state.shape[1], state.shape[2]
    edge_x = pltpu.VMEM((count * columns, BLK), BF16)
    edge_y = pltpu.VMEM((count // 2 * (tall - ROOM), BLK), BF16)
    return pl.pallas_call(
        deposit_kernel,
        name="deposit",
        out_shape=(pltpu.VMEM(state.shape, F32), edge_x, edge_x, edge_y, edge_y),
        in_specs=[SMEM] * 2 + [VMEM] * 7,
        out_specs=(VMEM,) * 5,
        input_output_aliases={8: 0},
        scratch_shapes=[pltpu.VMEM((9 * CAP + 1, ROWS, BLK), BF16)],
        compiler_params=pltpu.CompilerParams(vmem_limit_bytes=4 * MIB),
    )(slots, spots, *parts, weight, state)


def total(terms):
    while len(terms) > 1:
        terms = [a + b for a, b in zip(terms[::2], terms[1::2], strict=True)]
    return terms[0]


def speeds_at(props, state, j, here, parts):
    share = 1.0 / (1.0 + total([props[0, m] * state[j, m, here, :] for m in range(MAT)]))
    found = []
    if 0 in parts:
        found.append((0, state[j, MAT, here, :] * share))
    if 1 in parts:
        along = state[j, MAT + 1, here, :] * share
        found += [(1, along), (2, turn(along))]
    return found


def store_speeds(props, state, speed, places, parts):
    waiting = []
    for step in range(len(places) + DELAY):
        if step < len(places):
            j, first_row = places[step]
            waiting.append(speeds_at(props, state, j, slice(first_row, first_row + 8), parts))
        if step >= DELAY:
            j, first_row = places[step - DELAY]
            for plane, value in waiting.pop(0):
                speed[j, plane, first_row : first_row + 8, :] = value


def weights_at(speed, j, first_row):
    low = low_lanes()
    here = slice(first_row, first_row + 8)
    scale = 0.5 * time_step
    ux = speed[j, 0, here, :]
    lower = scale * (speed[j, 0, slice(first_row - 1, first_row + 7), :] + ux)
    upper = scale * (ux + speed[j, 0, slice(first_row + 1, first_row + 9), :])
    uy, before, after = (speed[k, 1, here, :] for k in (j, j - 1, j + 1))
    turned, turned_before, turned_after = (speed[k, 2, here, :] for k in (j, j - 1, j + 1))
    left = scale * (jnp.where(low, turned_before, turned) + uy)
    right = scale * (uy + jnp.where(low, turned, turned_after))
    keep = 1.0 - (
        (jnp.maximum(upper, 0.0) + jnp.maximum(-lower, 0.0)) + (jnp.maximum(right, 0.0) + jnp.maximum(-left, 0.0))
    )
    take_left = jnp.maximum(scale * (jnp.where(low, uy, before) + turned), 0.0)
    take_right = jnp.maximum(-scale * (turned + jnp.where(low, after, uy)), 0.0)
    same = jnp.where(low, take_left, take_right)
    other = jnp.where(low, take_right, take_left)
    return keep, jnp.maximum(lower, 0.0), jnp.maximum(-upper, 0.0), same, other


def values_at(state, weights, j, first_row, wanted):
    low = low_lanes()
    here = slice(first_row, first_row + 8)
    before = slice(first_row - 1, first_row + 7)
    after = slice(first_row + 1, first_row + 9)
    keep, take_before, take_after, same, other = weights
    values = []
    for q in wanted:
        mid = state[j, q, here, :]
        beside = jnp.where(low, state[j + 1, q, here, :], state[j - 1, q, here, :])
        value = (keep * mid + take_before * state[j, q, before, :]) + take_after * state[j, q, after, :]
        values.append(value + turn(same * mid + other * beside))
    return values


def pressure_of(props, values):
    terms = [value * (props[1, m] + (0.5 * props[1, m]) * value) for m, value in enumerate(values[:MAT])]
    return total(terms) + 0.4 * values[-1]


def remap_tiles(props, state, speed, press, fresh, places, wanted):
    weights, values = {}, {}
    for step in range(len(places) + 2):
        if step < len(places):
            weights[step] = weights_at(speed, *places[step])
        k = step - 1
        if 0 <= k < len(places):
            values[k] = values_at(state, weights.pop(k), *places[k], wanted)
        k = step - 2
        if k >= 0:
            found = values.pop(k)
            j, first_row = places[k]
            inside = slice(first_row - PAD, first_row - PAD + 8)
            lanes = column_lanes(j)
            for q, value in zip(wanted, found, strict=True):
                fresh[q, inside, lanes] = value
            if press is not None:
                press[j - 1, inside, :] = pressure_of(props, found)


def scalars(count):
    return [*range(MAT), count - 1]


def column_lanes(j):
    if isinstance(j, int):
        return slice((j - 1) * BLK, j * BLK)
    return pl.ds(pl.multiple_of((j - 1) * BLK, BLK), BLK)


def share(columns, most):
    return max(k for k in range(1, most + 1) if columns % k == 0)


def inner_kernel(props, state, fresh, press, speed):
    columns, tall = state.shape[0] - 2, state.shape[2]

    group = share(columns, GROUP)

    def speeds(step, carry):
        rows = range(PAD, tall - AFTER, 8)
        places = [(1 + step * group + k, row) for k in range(group) for row in rows]
        store_speeds(props, state, speed, places, (0, 1))
        return carry

    lax.fori_loop(0, columns // group, speeds, 0)
    pair = share(columns - 2, PAIR)

    def remap(step, carry):
        rows = range(PAD + 8, tall - AFTER - 8, 8)
        places = [(2 + step * pair + k, row) for k in range(pair) for row in rows]
        remap_tiles(props, state, speed, press, fresh, places, scalars(state.shape[1]))
        return carry

    lax.fori_loop(0, (columns - 2) // pair, remap, 0)


def inner(props, state, width):
    columns, count, tall = state.shape[0] - 2, state.shape[1], state.shape[2]
    return pl.pallas_call(
        inner_kernel,
        name="inner",
        out_shape=(
            pltpu.VMEM((count, width, columns * BLK), F32),
            pltpu.VMEM((columns, width, BLK), F32),
            pltpu.VMEM((columns + 2, 3, tall, BLK), F32),
        ),
        in_specs=[SMEM, VMEM],
        out_specs=(VMEM, VMEM, VMEM),
        compiler_params=pltpu.CompilerParams(vmem_limit_bytes=4 * MIB),
        cost_estimate=pl.CostEstimate(flops=20 * state.size, bytes_accessed=2 * state.size * 4, transcendentals=0),
    )(props, state)


def outer_kernel(
    props, slots, points, edge_x1, edge_x2, edge_y2, edge_y1, weight, state_in, speed_in, press_in,
    fresh_in, remapped, state, speed, press, fresh, own, first, second, sums, sem, *, size_x, size_y
):
    pos_x, pos_y = lax.axis_index("gx"), lax.axis_index("gy")
    n_tiles = weight.shape[0]
    columns, count, tall = state.shape[0] - 2, state.shape[1], state.shape[2]
    width = tall - ROOM
    copies = area_copies(fresh, remapped, sem, scalar_planes(count), [inner_area(fresh)])
    for copy in copies:
        copy.start()
    even_x, even_y = (pos_x & 1) == 0, (pos_y & 1) == 0
    line = state.reshape((columns + 2) * count * tall, BLK)
    above, below = PAD + width, PAD - 1
    for edge, row, there in (
        (edge_x1, jnp.where(even_x, below, above), has_far(pos_x, size_x)),
        (edge_x2, jnp.where(even_x, above, below), True),
    ):
        for q in range(count):
            at = pl.ds(count * tall + q * tall + row, columns, stride=count * tall)
            line[at, :] = jnp.where(there, edge[q * columns : (q + 1) * columns, :].astype(F32), 0.0)
    low = low_lanes()
    for edge, column, there in (
        (edge_y1, jnp.where(even_y, 0, columns + 1), has_far(pos_y, size_y)),
        (edge_y2, jnp.where(even_y, columns + 1, 0), True),
    ):
        for q in range(count // 2):
            for i in range(width // ROWS):
                here = slice(PAD + i * ROWS, PAD + (i + 1) * ROWS)
                both = edge[q * width + i * ROWS : q * width + (i + 1) * ROWS, :].astype(F32)
                both = jnp.where(there, both, 0.0)
                turned = turn(both)
                state[column, q, here, :] = jnp.where(low, both, turned)
                state[column, q + count // 2, here, :] = jnp.where(low, turned, both)

    places = [(j, row) for j in range(1, columns + 1) for row in (0, tall - AFTER)]
    store_speeds(props, state, speed, places, (0,))
    places = [(j, row) for j in (0, columns + 1) for row in range(PAD, tall - AFTER, 8)]
    store_speeds(props, state, speed, places, (1,))

    group = share(columns, GROUP)

    def sides(step, carry):
        places = [(1 + step * group + k, row) for k in range(group) for row in (PAD, tall - AFTER - 8)]
        remap_tiles(props, state, speed, press, fresh, places, scalars(state.shape[1]))
        return carry

    lax.fori_loop(0, columns // group, sides, 0)
    places = [(j, row) for j in (1, columns) for row in range(PAD + 8, tall - AFTER - 8, 8)]
    remap_tiles(props, state, speed, press, fresh, places, scalars(state.shape[1]))

    sums[...] = jnp.zeros(sums.shape, F32)
    line_of = lax.broadcasted_iota(jnp.int32, (ROWS, BLK), 0)
    field = press.reshape(columns * width, BLK)
    for first_tile in range(0, n_tiles, TOGETHER):
        tiles = range(first_tile, first_tile + TOGETHER)
        found = []
        for t in tiles[::2]:
            one, two = (field[pl.ds(points[k], 1), :] for k in (t, t + 1))
            probe = jnp.where(line_of == 0, one, jnp.where(line_of == 8, two, 1.0)).astype(BF16)
            both = jnp.dot(probe, beside(weight, t), preferred_element_type=F32)
            found += [both[:8, :BLK], both[8:, BLK:]]
        add_at(sums, [slots[t] for t in tiles], lambda place: place, found)
    table = sums.reshape(sums.shape[0] * 8, BLK)
    for k, out in enumerate((own, first, second)):
        top = table[pl.ds(k * 3 * CAP * 8, 3 * CAP, stride=8), :]
        under = table[pl.ds(k * 3 * CAP * 8 + 1, 3 * CAP, stride=8), :]
        out[...] = top / jnp.maximum(under, 1.0)
    for copy in copies:
        copy.wait()


def outer(props, slots, points, edges, weight, state, speed, press, fresh, size_x, size_y):
    answer = pltpu.VMEM((3 * CAP, BLK), F32)
    outs = pl.pallas_call(
        functools.partial(outer_kernel, size_x=size_x, size_y=size_y),
        name="outer",
        out_shape=(
            jax.ShapeDtypeStruct(fresh.shape, F32),
            pltpu.VMEM(state.shape, F32),
            pltpu.VMEM(speed.shape, F32),
            pltpu.VMEM(press.shape, F32),
            pltpu.VMEM(fresh.shape, F32),
            answer,
            answer,
            answer,
        ),
        in_specs=[SMEM] * 3 + [VMEM] * 9,
        out_specs=(ANY,) + (VMEM,) * 7,
        input_output_aliases={8: 1, 9: 2, 10: 3, 11: 4},
        scratch_shapes=[pltpu.VMEM((9 * CAP + 1, 8, BLK), F32), pltpu.SemaphoreType.DMA((2,))],
        compiler_params=pltpu.CompilerParams(vmem_limit_bytes=4 * MIB),
    )(props, slots, points, *edges, weight, state, speed, press, fresh)
    return outs[0], outs[1], outs[2], outs[4], outs[5], outs[6], outs[7]


def late_kernel(state, speed, fresh_in, remapped_in, remapped, fresh, sem, sem_moving):
    columns, count, tall = state.shape[0] - 2, state.shape[1], state.shape[2]
    width, lanes = fresh.shape[1], fresh.shape[2]
    rows = pl.ds(8, width - 16)
    areas = [
        (pl.ds(0, 8), pl.ds(0, lanes)),
        (pl.ds(width - 8, 8), pl.ds(0, lanes)),
        (rows, pl.ds(0, BLK)),
        (rows, pl.ds(lanes - BLK, BLK)),
    ]
    copies = area_copies(fresh, remapped, sem, scalar_planes(count), areas)
    for copy in copies:
        copy.start()
    for part in range(PARTS):
        held = range(1 + part * columns // PARTS, 1 + (part + 1) * columns // PARTS)
        places = [(j, row) for j in held for row in range(PAD, tall - AFTER, 8)]
        remap_tiles(None, state, speed, None, fresh, places, range(MAT, count - 1))
        area = (pl.ds(0, width), pl.ds((held[0] - 1) * BLK, len(held) * BLK))
        copies += area_copies(fresh, remapped, sem_moving.at[part], [pl.ds(MAT, count - 1 - MAT)], [area])
        copies[-1].start()
    for copy in copies:
        copy.wait()


def scalar_planes(count):
    return [pl.ds(0, MAT), pl.ds(count - 1, 1)]


def inner_area(fresh):
    return pl.ds(8, fresh.shape[1] - 16), pl.ds(BLK, fresh.shape[2] - 2 * BLK)


def area_copies(fresh, remapped, sem, planes, areas):
    boxes = [(plane, *area) for area in areas for plane in planes]
    return [pltpu.make_async_copy(fresh.at[box], remapped.at[box], sem.at[k]) for k, box in enumerate(boxes)]


def late(state, speed, fresh, remapped):
    return pl.pallas_call(
        late_kernel,
        name="late",
        out_shape=(jax.ShapeDtypeStruct(fresh.shape, F32), pltpu.VMEM(fresh.shape, F32)),
        in_specs=[VMEM] * 3 + [ANY],
        out_specs=(ANY, VMEM),
        input_output_aliases={2: 1, 3: 0},
        scratch_shapes=[pltpu.SemaphoreType.DMA((8,)), pltpu.SemaphoreType.DMA((PARTS, 1))],
        compiler_params=pltpu.CompilerParams(vmem_limit_bytes=4 * MIB),
        cost_estimate=pl.CostEstimate(flops=5 * state.size, bytes_accessed=2 * state.size * 4, transcendentals=0),
    )(state, speed, fresh, remapped)[0]


def pick_kernel(place, own, first, second, out, table, lines):
    for k, part in enumerate((own, first, second)):
        for spot, code in enumerate((0, 2, 1)):
            row = (k * 3 + code) * CAP
            table[row : row + CAP, :] = part[spot * CAP : (spot + 1) * CAP, :]
    for b in range(out.shape[0]):
        lines[b : b + 1, :] = table[pl.ds(place[b], 1), :]
    out[...] = lines[...].astype(BF16)


def pick(place, own, first, second):
    n_blocks = place.shape[0]
    return pl.pallas_call(
        pick_kernel,
        name="pick",
        out_shape=jax.ShapeDtypeStruct((n_blocks, BLK), BF16),
        in_specs=[SMEM, VMEM, VMEM, VMEM],
        out_specs=VMEM,
        scratch_shapes=[pltpu.VMEM((9 * CAP, BLK), F32), pltpu.VMEM((n_blocks, BLK), F32)],
        compiler_params=pltpu.CompilerParams(vmem_limit_bytes=2 * MIB),
    )(place, own, first, second)


def per_device(
    elem_volume,
    elem_velocity,
    elem_energy,
    elem_mat,
    elem_dest,
    tile_slot,
    tile_cell,
    tile_weight,
    tile_count,
    cell_state,
    mat_props,
):
    size_x, size_y = lax.axis_size("gx"), lax.axis_size("gy")
    n_blocks = elem_dest.shape[0]
    shape = (n_blocks, BLK)
    own, first, second, place, mat_props, tile_slot, tile_cell = payload(
        elem_dest,
        mat_props,
        elem_volume.reshape(shape),
        elem_velocity,
        elem_energy.reshape(shape),
        elem_mat.reshape(shape),
        tile_slot,
        tile_cell,
        size_y,
    )
    weight = fetch(tile_weight)

    first = swap(first, "gx", 1)
    second = swap(second, "gx", 2)
    weight, own = lax.optimization_barrier((weight, own))
    state, turned, slots, spots, points = stage(
        tile_slot, tile_cell, tile_count, cell_state, weight, size_y
    )

    def along_y(which):
        rows = slice(which * CAP, (which + 1) * CAP)
        return jnp.concatenate([own[rows], first[rows], second[rows]], axis=0)

    south = swap(along_y(1), "gy", 1)
    north = swap(along_y(2), "gy", 2)
    state, *edges = deposit(
        slots, spots, (own, first, second, south, north), weight, state
    )
    edges = (
        swap(edges[0], "gx", 1),
        swap(edges[1], "gx", 2),
        swap(edges[3], "gy", 2),
        swap(edges[2], "gy", 1, wrap=False),
    )
    fresh, press, speed = inner(mat_props, state, cell_state.shape[1])
    remapped, state, speed, fresh, own, first, second = outer(
        mat_props, slots, points, edges, turned, state, speed, press, fresh, size_x, size_y
    )
    remapped = late(state, speed, fresh, remapped)
    first = swap(first, "gy", 1)
    second = swap(second, "gy", 2)

    def along_x(which):
        rows = slice(which * CAP, (which + 1) * CAP)
        return jnp.concatenate([own[rows], second[rows], first[rows]], axis=0)

    back = pick(place, along_x(0), swap(along_x(1), "gx", 1), swap(along_x(2), "gx", 2))
    return remapped, back.reshape(n_blocks * BLK)


def solution(mesh):
    placed = (
        P(("gx", "gy")),
        P(None, ("gx", "gy")),
        P(("gx", "gy")),
        P(("gx", "gy")),
        P(("gx", "gy")),
        P(("gx", "gy")),
        P(("gx", "gy")),
        P(("gx", "gy"), None, None),
        P(("gx", "gy")),
        P(None, "gx", "gy"),
        P(),
    )
    return jax.shard_map(
        per_device,
        mesh=mesh,
        in_specs=placed,
        out_specs=(P(None, "gx", "gy"), P(("gx", "gy"))),
        check_vma=False,
    )
```

```python
import functools

import jax
import jax.numpy as jnp
from jax import lax
from jax.experimental import pallas as pl
from jax.experimental.pallas import tpu as pltpu
from jax.sharding import PartitionSpec as P

MAT = 8
NZ = 64
BLK = 128
CAP = 2
HALF = BLK // 2
PAD = 8
AFTER = 16
ROOM = PAD + AFTER
ROWS = 16
PAIR = 7
TOGETHER = 4
PARTS = 4
TURN = 16
GROUP = 16
DELAY = 4
MIB = 2**20

time_step = 0.8
F32 = jnp.float32
BF16 = jnp.bfloat16

SMEM = pl.BlockSpec(memory_space=pltpu.SMEM)
VMEM = pl.BlockSpec(memory_space=pltpu.VMEM)
ANY = pl.BlockSpec(memory_space=pl.ANY)


def partner(index, size, which):
    if which == 2:
        return index ^ 1
    return (index + 1 if index % 2 else index - 1) % size


def swap(value, axis, which, wrap=True):
    size = lax.axis_size(axis)
    pairs = [(i, partner(i, size, which)) for i in range(size)]
    if not wrap:
        pairs = [(i, j if abs(i - j) == 1 else i) for i, j in pairs]
    return lax.ppermute(value, axis, pairs)


def has_far(index, size):
    return (index > 0) & (index < size - 1)


def code_of(index, mine):
    return jnp.where(index == mine, 0, jnp.where(index == (mine ^ 1), 2, 1))


def split_device(device, size):
    if size & (size - 1) == 0:
        return device >> (size.bit_length() - 1), device & (size - 1)
    return lax.div(device, size), lax.rem(device, size)


def in_hbm(value):
    return pltpu.with_memory_space_constraint(value, pltpu.HBM)


def payload_kernel(
    dest_hbm, props_hbm, volume_hbm, velocity_hbm, energy_hbm, mat_hbm, slot_hbm, cell_hbm,
    own, first, second, place, props, slot_out, cell_out, dest, volume, velocity, energy, mat, seen, packed, sem, *, size_y
):
    moves = (
        (dest_hbm, dest), (props_hbm, props), (mat_hbm, mat),
        (volume_hbm, volume), (velocity_hbm, velocity), (energy_hbm, energy),
        (slot_hbm, slot_out), (cell_hbm, cell_out),
    )
    copies = [pltpu.make_async_copy(src, dst, sem.at[k]) for k, (src, dst) in enumerate(moves)]
    for copy in copies:
        copy.start()
    for copy in copies:
        copy.wait()
    pos_x, pos_y = lax.axis_index("gx"), lax.axis_index("gy")
    n_blocks = volume.shape[0]
    kinds = mat[...]
    density = jnp.zeros(kinds.shape, F32)
    for m in range(MAT):
        density = jnp.where(kinds == m, props[0, m], density)
    mass = volume[...] * density
    heat = mass * energy[...]
    level = lax.broadcasted_iota(jnp.int32, (MAT, BLK), 0)
    for k in range(9):
        seen[k] = 0
    for b in range(n_blocks):
        at_x, at_y = split_device(dest[b], size_y)
        near = code_of(at_x, pos_x) * 3 + code_of(at_y, pos_y)
        rank = seen[near]
        seen[near] = rank + 1
        slot = near * CAP + rank
        place[b] = slot
        volumes = jnp.where(kinds[b : b + 1] == level, volume[b : b + 1, :], 0.0)
        momentum = mass[b : b + 1] * velocity[:, b * BLK : (b + 1) * BLK]
        rows = jnp.concatenate([volumes, momentum, heat[b : b + 1], jnp.zeros((4, BLK), F32)], axis=0)
        packed[slot] = rows.astype(BF16)
    for k, out in enumerate((own, first, second)):
        for s in range(3 * CAP):
            out[s] = packed[k * 3 * CAP + s]


def payload(dest, props, volume, velocity, energy, mat, tile_slot, tile_cell, size_y):
    n_blocks = volume.shape[0]
    parcel = pltpu.VMEM((3 * CAP, ROWS, BLK), BF16)
    return pl.pallas_call(
        functools.partial(payload_kernel, size_y=size_y),
        name="payload",
        out_shape=(
            parcel,
            parcel,
            parcel,
            pltpu.SMEM((n_blocks,), jnp.int32),
            pltpu.SMEM(props.shape, F32),
            pltpu.SMEM(tile_slot.shape, jnp.int32),
            pltpu.SMEM(tile_cell.shape, jnp.int32),
        ),
        in_specs=[ANY] * 8,
        out_specs=(VMEM, VMEM, VMEM, SMEM, SMEM, SMEM, SMEM),
        scratch_shapes=[
            pltpu.SMEM(dest.shape, jnp.int32),
            pltpu.VMEM(volume.shape, F32),
            pltpu.VMEM(velocity.shape, F32),
            pltpu.VMEM(energy.shape, F32),
            pltpu.VMEM(mat.shape, jnp.int32),
            pltpu.SMEM((9,), jnp.int32),
            pltpu.VMEM((9 * CAP, ROWS, BLK), BF16),
            pltpu.SemaphoreType.DMA((8,)),
        ],
        compiler_params=pltpu.CompilerParams(vmem_limit_bytes=4 * MIB),
    )(*(in_hbm(value) for value in (dest, props, volume, velocity, energy, mat, tile_slot, tile_cell)))


def stage_kernel(
    tile_slot, tile_cell, tile_count, cell, weight, state, turned, slots, spots, points, sem, *, size_y
):
    pos_x, pos_y = lax.axis_index("gx"), lax.axis_index("gy")
    columns, count, tall = state.shape[0] - 2, state.shape[1], state.shape[2]
    width = tall - ROOM
    copies = [
        pltpu.make_async_copy(
            cell.at[:, :, pl.ds(j * BLK, BLK)], state.at[j + 1, :, pl.ds(PAD, width)], sem.at[j]
        )
        for j in range(columns)
    ]
    for copy in copies:
        copy.start()

    counted = tile_count[0]

    def turn_and_index(step, carry):
        for k in range(TURN):
            t = step * TURN + k
            turned[t] = weight[t].T
            x, j = split_device(tile_cell[t], columns)
            slots[t] = jnp.where(t < counted, local_slot(tile_slot[t], pos_x, pos_y, size_y), 9 * CAP)
            spots[t] = (j + 1) * (count * tall) + x + PAD
            points[t] = j * width + x
        return carry

    lax.fori_loop(0, weight.shape[0] // TURN, turn_and_index, 0)
    for copy in copies:
        copy.wait()


def stage(tile_slot, tile_cell, tile_count, cell, weight, size_y):
    count, width, lanes = cell.shape
    columns = lanes // BLK
    indices = pltpu.SMEM(tile_slot.shape, jnp.int32)
    return pl.pallas_call(
        functools.partial(stage_kernel, size_y=size_y),
        name="stage",
        out_shape=(
            pltpu.VMEM((columns + 2, count, width + ROOM, BLK), F32),
            pltpu.VMEM(weight.shape, weight.dtype),
            indices,
            indices,
            indices,
        ),
        in_specs=[SMEM, SMEM, SMEM, ANY, VMEM],
        out_specs=(VMEM, VMEM, SMEM, SMEM, SMEM),
        scratch_shapes=[pltpu.SemaphoreType.DMA((columns,))],
        compiler_params=pltpu.CompilerParams(vmem_limit_bytes=2 * MIB),
        cost_estimate=pl.CostEstimate(flops=0, bytes_accessed=2 * cell.size * 4, transcendentals=0),
    )(tile_slot, tile_cell, tile_count, in_hbm(cell), weight)


def fetch_kernel(source, target, sem):
    copy = pltpu.make_async_copy(source, target, sem)
    copy.start()
    copy.wait()


def fetch(value):
    return pl.pallas_call(
        fetch_kernel,
        name="fetch",
        out_shape=pltpu.VMEM(value.shape, value.dtype),
        in_specs=[ANY],
        out_specs=VMEM,
        scratch_shapes=[pltpu.SemaphoreType.DMA],
        compiler_params=pltpu.CompilerParams(vmem_limit_bytes=2 * MIB),
        cost_estimate=pl.CostEstimate(flops=0, bytes_accessed=2 * value.size * 2, transcendentals=0),
    )(in_hbm(value))


def local_slot(slot, pos_x, pos_y, size_y):
    at_x, at_y = split_device(slot >> 1, size_y)
    return code_of(at_y, pos_y) * (3 * CAP) + code_of(at_x, pos_x) * CAP + (slot & 1)


def low_lanes():
    return lax.broadcasted_iota(jnp.int32, (1, BLK), 1) < HALF


def turn(value):
    return pltpu.roll(value, HALF, value.ndim - 1)


def beside(weight, t):
    return jnp.concatenate([weight[t], weight[t + 1]], axis=1)


def add_at(buffer, places, index, values):
    held = [buffer[index(place)] for place in places]
    for k, place in enumerate(places):
        value = values[k]
        for earlier in range(k):
            value = value + jnp.where(places[earlier] == place, values[earlier], 0.0)
        buffer[index(place)] = held[k] + value


def deposit_kernel(
    slots, spots, own, first, second, south, north, weight, state_in,
    state, edge_x1, edge_x2, edge_y1, edge_y2, rows
):
    pos_x, pos_y = lax.axis_index("gx"), lax.axis_index("gy")
    n_tiles = weight.shape[0]
    columns, count, tall = state.shape[0] - 2, state.shape[1], state.shape[2]
    line = state.reshape((columns + 2) * count * tall, BLK)
    rows[9 * CAP] = jnp.zeros(rows.shape[1:], BF16)
    for k, part in enumerate((own, first, second)):
        for r in range(CAP):
            rows[k * CAP + r] = part[r]
    for k, part in enumerate((south, north)):
        for r in range(3 * CAP):
            rows[(k + 1) * 3 * CAP + r] = part[r]
    for first_tile in range(0, n_tiles, 2):
        tiles = range(first_tile, first_tile + 2)
        contribs = []
        for t in tiles[::2]:
            both = jnp.concatenate([rows[slots[t]], rows[slots[t + 1]]], axis=0)
            found = jnp.dot(both, beside(weight, t), preferred_element_type=F32)
            contribs += [found[:count, :BLK], found[ROWS : ROWS + count, BLK:]]
        add_at(line, [spots[t] for t in tiles], lambda place: (pl.ds(place, count, stride=tall), slice(None)), contribs)

    even_x, even_y = (pos_x & 1) == 0, (pos_y & 1) == 0
    width = tall - ROOM
    top, bottom = PAD + width - 1, PAD
    for edge, row in (
        (edge_x1, jnp.where(even_x, bottom, top)),
        (edge_x2, jnp.where(even_x, top, bottom)),
    ):
        for q in range(count):
            at = pl.ds(count * tall + q * tall + row, columns, stride=count * tall)
            edge[q * columns : (q + 1) * columns, :] = line[at, :].astype(BF16)
    low = low_lanes()
    for edge, upper in ((edge_y1, jnp.logical_not(even_y)), (edge_y2, even_y)):
        column = jnp.where(upper, columns, 1)
        for q in range(count // 2):
            for i in range(width // ROWS):
                here = slice(PAD + i * ROWS, PAD + (i + 1) * ROWS)
                a = state[column, q, here, :]
                b = state[column, q + count // 2, here, :]
                both = jnp.where(low, jnp.where(upper, turn(a), a), jnp.where(upper, b, turn(b)))
                edge[q * width + i * ROWS : q * width + (i + 1) * ROWS, :] = both.astype(BF16)


def deposit(slots, spots, parts, weight, state):
    columns, count, tall = state.shape[0] - 2, state.shape[1], state.shape[2]
    edge_x = pltpu.VMEM((count * columns, BLK), BF16)
    edge_y = pltpu.VMEM((count // 2 * (tall - ROOM), BLK), BF16)
    return pl.pallas_call(
        deposit_kernel,
        name="deposit",
        out_shape=(pltpu.VMEM(state.shape, F32), edge_x, edge_x, edge_y, edge_y),
        in_specs=[SMEM] * 2 + [VMEM] * 7,
        out_specs=(VMEM,) * 5,
        input_output_aliases={8: 0},
        scratch_shapes=[pltpu.VMEM((9 * CAP + 1, ROWS, BLK), BF16)],
        compiler_params=pltpu.CompilerParams(vmem_limit_bytes=4 * MIB),
    )(slots, spots, *parts, weight, state)


def total(terms):
    while len(terms) > 1:
        terms = [a + b for a, b in zip(terms[::2], terms[1::2], strict=True)]
    return terms[0]


def speeds_at(props, state, j, here, parts):
    share = 1.0 / (1.0 + total([props[0, m] * state[j, m, here, :] for m in range(MAT)]))
    found = []
    if 0 in parts:
        found.append((0, state[j, MAT, here, :] * share))
    if 1 in parts:
        along = state[j, MAT + 1, here, :] * share
        found += [(1, along), (2, turn(along))]
    return found


def store_speeds(props, state, speed, places, parts):
    waiting = []
    for step in range(len(places) + DELAY):
        if step < len(places):
            j, first_row = places[step]
            waiting.append(speeds_at(props, state, j, slice(first_row, first_row + 8), parts))
        if step >= DELAY:
            j, first_row = places[step - DELAY]
            for plane, value in waiting.pop(0):
                speed[j, plane, first_row : first_row + 8, :] = value


def weights_at(speed, j, first_row):
    low = low_lanes()
    here = slice(first_row, first_row + 8)
    scale = 0.5 * time_step
    ux = speed[j, 0, here, :]
    lower = scale * (speed[j, 0, slice(first_row - 1, first_row + 7), :] + ux)
    upper = scale * (ux + speed[j, 0, slice(first_row + 1, first_row + 9), :])
    uy, before, after = (speed[k, 1, here, :] for k in (j, j - 1, j + 1))
    turned, turned_before, turned_after = (speed[k, 2, here, :] for k in (j, j - 1, j + 1))
    left = scale * (jnp.where(low, turned_before, turned) + uy)
    right = scale * (uy + jnp.where(low, turned, turned_after))
    keep = 1.0 - (
        (jnp.maximum(upper, 0.0) + jnp.maximum(-lower, 0.0)) + (jnp.maximum(right, 0.0) + jnp.maximum(-left, 0.0))
    )
    take_left = jnp.maximum(scale * (jnp.where(low, uy, before) + turned), 0.0)
    take_right = jnp.maximum(-scale * (turned + jnp.where(low, after, uy)), 0.0)
    same = jnp.where(low, take_left, take_right)
    other = jnp.where(low, take_right, take_left)
    return keep, jnp.maximum(lower, 0.0), jnp.maximum(-upper, 0.0), same, other


def values_at(state, weights, j, first_row, wanted):
    low = low_lanes()
    here = slice(first_row, first_row + 8)
    before = slice(first_row - 1, first_row + 7)
    after = slice(first_row + 1, first_row + 9)
    keep, take_before, take_after, same, other = weights
    values = []
    for q in wanted:
        mid = state[j, q, here, :]
        beside = jnp.where(low, state[j + 1, q, here, :], state[j - 1, q, here, :])
        value = (keep * mid + take_before * state[j, q, before, :]) + take_after * state[j, q, after, :]
        values.append(value + turn(same * mid + other * beside))
    return values


def pressure_of(props, values):
    terms = [value * (props[1, m] + (0.5 * props[1, m]) * value) for m, value in enumerate(values[:MAT])]
    return total(terms) + 0.4 * values[-1]


def remap_tiles(props, state, speed, press, fresh, places, wanted):
    weights, values = {}, {}
    for step in range(len(places) + 2):
        if step < len(places):
            weights[step] = weights_at(speed, *places[step])
        k = step - 1
        if 0 <= k < len(places):
            values[k] = values_at(state, weights.pop(k), *places[k], wanted)
        k = step - 2
        if k >= 0:
            found = values.pop(k)
            j, first_row = places[k]
            inside = slice(first_row - PAD, first_row - PAD + 8)
            lanes = column_lanes(j)
            for q, value in zip(wanted, found, strict=True):
                fresh[q, inside, lanes] = value
            if press is not None:
                press[j - 1, inside, :] = pressure_of(props, found)


def scalars(count):
    return [*range(MAT), count - 1]


def column_lanes(j):
    if isinstance(j, int):
        return slice((j - 1) * BLK, j * BLK)
    return pl.ds(pl.multiple_of((j - 1) * BLK, BLK), BLK)


def share(columns, most):
    return max(k for k in range(1, most + 1) if columns % k == 0)


def inner_kernel(props, state, fresh, press, speed):
    columns, tall = state.shape[0] - 2, state.shape[2]

    group = share(columns, GROUP)

    def speeds(step, carry):
        rows = range(PAD, tall - AFTER, 8)
        places = [(1 + step * group + k, row) for k in range(group) for row in rows]
        store_speeds(props, state, speed, places, (0, 1))
        return carry

    lax.fori_loop(0, columns // group, speeds, 0)
    pair = share(columns - 2, PAIR)

    def remap(step, carry):
        rows = range(PAD + 8, tall - AFTER - 8, 8)
        places = [(2 + step * pair + k, row) for k in range(pair) for row in rows]
        remap_tiles(props, state, speed, press, fresh, places, scalars(state.shape[1]))
        return carry

    lax.fori_loop(0, (columns - 2) // pair, remap, 0)


def inner(props, state, width):
    columns, count, tall = state.shape[0] - 2, state.shape[1], state.shape[2]
    return pl.pallas_call(
        inner_kernel,
        name="inner",
        out_shape=(
            pltpu.VMEM((count, width, columns * BLK), F32),
            pltpu.VMEM((columns, width, BLK), F32),
            pltpu.VMEM((columns + 2, 3, tall, BLK), F32),
        ),
        in_specs=[SMEM, VMEM],
        out_specs=(VMEM, VMEM, VMEM),
        compiler_params=pltpu.CompilerParams(vmem_limit_bytes=4 * MIB),
        cost_estimate=pl.CostEstimate(flops=20 * state.size, bytes_accessed=2 * state.size * 4, transcendentals=0),
    )(props, state)


def outer_kernel(
    props, slots, points, edge_x1, edge_x2, edge_y2, edge_y1, weight, state_in, speed_in, press_in,
    fresh_in, remapped, state, speed, press, fresh, own, first, second, sums, sem, *, size_x, size_y
):
    pos_x, pos_y = lax.axis_index("gx"), lax.axis_index("gy")
    n_tiles = weight.shape[0]
    columns, count, tall = state.shape[0] - 2, state.shape[1], state.shape[2]
    width = tall - ROOM
    copies = area_copies(fresh, remapped, sem, scalar_planes(count), [inner_area(fresh)])
    for copy in copies:
        copy.start()
    even_x, even_y = (pos_x & 1) == 0, (pos_y & 1) == 0
    line = state.reshape((columns + 2) * count * tall, BLK)
    above, below = PAD + width, PAD - 1
    for edge, row, there in (
        (edge_x1, jnp.where(even_x, below, above), has_far(pos_x, size_x)),
        (edge_x2, jnp.where(even_x, above, below), True),
    ):
        for q in range(count):
            at = pl.ds(count * tall + q * tall + row, columns, stride=count * tall)
            line[at, :] = jnp.where(there, edge[q * columns : (q + 1) * columns, :].astype(F32), 0.0)
    low = low_lanes()
    for edge, column, there in (
        (edge_y1, jnp.where(even_y, 0, columns + 1), has_far(pos_y, size_y)),
        (edge_y2, jnp.where(even_y, columns + 1, 0), True),
    ):
        for q in range(count // 2):
            for i in range(width // ROWS):
                here = slice(PAD + i * ROWS, PAD + (i + 1) * ROWS)
                both = edge[q * width + i * ROWS : q * width + (i + 1) * ROWS, :].astype(F32)
                both = jnp.where(there, both, 0.0)
                turned = turn(both)
                state[column, q, here, :] = jnp.where(low, both, turned)
                state[column, q + count // 2, here, :] = jnp.where(low, turned, both)

    places = [(j, row) for j in range(1, columns + 1) for row in (0, tall - AFTER)]
    store_speeds(props, state, speed, places, (0,))
    places = [(j, row) for j in (0, columns + 1) for row in range(PAD, tall - AFTER, 8)]
    store_speeds(props, state, speed, places, (1,))

    group = share(columns, GROUP)

    def sides(step, carry):
        places = [(1 + step * group + k, row) for k in range(group) for row in (PAD, tall - AFTER - 8)]
        remap_tiles(props, state, speed, press, fresh, places, scalars(state.shape[1]))
        return carry

    lax.fori_loop(0, columns // group, sides, 0)
    places = [(j, row) for j in (1, columns) for row in range(PAD + 8, tall - AFTER - 8, 8)]
    remap_tiles(props, state, speed, press, fresh, places, scalars(state.shape[1]))

    sums[...] = jnp.zeros(sums.shape, F32)
    line_of = lax.broadcasted_iota(jnp.int32, (ROWS, BLK), 0)
    field = press.reshape(columns * width, BLK)
    for first_tile in range(0, n_tiles, TOGETHER):
        tiles = range(first_tile, first_tile + TOGETHER)
        found = []
        for t in tiles[::2]:
            one, two = (field[pl.ds(points[k], 1), :] for k in (t, t + 1))
            probe = jnp.where(line_of == 0, one, jnp.where(line_of == 8, two, 1.0)).astype(BF16)
            both = jnp.dot(probe, beside(weight, t), preferred_element_type=F32)
            found += [both[:8, :BLK], both[8:, BLK:]]
        add_at(sums, [slots[t] for t in tiles], lambda place: place, found)
    table = sums.reshape(sums.shape[0] * 8, BLK)
    for k, out in enumerate((own, first, second)):
        top = table[pl.ds(k * 3 * CAP * 8, 3 * CAP, stride=8), :]
        under = table[pl.ds(k * 3 * CAP * 8 + 1, 3 * CAP, stride=8), :]
        out[...] = top / jnp.maximum(under, 1.0)
    for copy in copies:
        copy.wait()


def outer(props, slots, points, edges, weight, state, speed, press, fresh, size_x, size_y):
    answer = pltpu.VMEM((3 * CAP, BLK), F32)
    outs = pl.pallas_call(
        functools.partial(outer_kernel, size_x=size_x, size_y=size_y),
        name="outer",
        out_shape=(
            jax.ShapeDtypeStruct(fresh.shape, F32),
            pltpu.VMEM(state.shape, F32),
            pltpu.VMEM(speed.shape, F32),
            pltpu.VMEM(press.shape, F32),
            pltpu.VMEM(fresh.shape, F32),
            answer,
            answer,
            answer,
        ),
        in_specs=[SMEM] * 3 + [VMEM] * 9,
        out_specs=(ANY,) + (VMEM,) * 7,
        input_output_aliases={8: 1, 9: 2, 10: 3, 11: 4},
        scratch_shapes=[pltpu.VMEM((9 * CAP + 1, 8, BLK), F32), pltpu.SemaphoreType.DMA((2,))],
        compiler_params=pltpu.CompilerParams(vmem_limit_bytes=4 * MIB),
    )(props, slots, points, *edges, weight, state, speed, press, fresh)
    return outs[0], outs[1], outs[2], outs[4], outs[5], outs[6], outs[7]


def late_kernel(state, speed, fresh_in, remapped_in, remapped, fresh, sem, sem_moving):
    columns, count, tall = state.shape[0] - 2, state.shape[1], state.shape[2]
    width, lanes = fresh.shape[1], fresh.shape[2]
    rows = pl.ds(8, width - 16)
    areas = [
        (pl.ds(0, 8), pl.ds(0, lanes)),
        (pl.ds(width - 8, 8), pl.ds(0, lanes)),
        (rows, pl.ds(0, BLK)),
        (rows, pl.ds(lanes - BLK, BLK)),
    ]
    copies = area_copies(fresh, remapped, sem, scalar_planes(count), areas)
    for copy in copies:
        copy.start()
    for part in range(PARTS):
        held = range(1 + part * columns // PARTS, 1 + (part + 1) * columns // PARTS)
        places = [(j, row) for j in held for row in range(PAD, tall - AFTER, 8)]
        remap_tiles(None, state, speed, None, fresh, places, range(MAT, count - 1))
        area = (pl.ds(0, width), pl.ds((held[0] - 1) * BLK, len(held) * BLK))
        copies += area_copies(fresh, remapped, sem_moving.at[part], [pl.ds(MAT, count - 1 - MAT)], [area])
        copies[-1].start()
    for copy in copies:
        copy.wait()


def scalar_planes(count):
    return [pl.ds(0, MAT), pl.ds(count - 1, 1)]


def inner_area(fresh):
    return pl.ds(8, fresh.shape[1] - 16), pl.ds(BLK, fresh.shape[2] - 2 * BLK)


def area_copies(fresh, remapped, sem, planes, areas):
    boxes = [(plane, *area) for area in areas for plane in planes]
    return [pltpu.make_async_copy(fresh.at[box], remapped.at[box], sem.at[k]) for k, box in enumerate(boxes)]


def late(state, speed, fresh, remapped):
    return pl.pallas_call(
        late_kernel,
        name="late",
        out_shape=(jax.ShapeDtypeStruct(fresh.shape, F32), pltpu.VMEM(fresh.shape, F32)),
        in_specs=[VMEM] * 3 + [ANY],
        out_specs=(ANY, VMEM),
        input_output_aliases={2: 1, 3: 0},
        scratch_shapes=[pltpu.SemaphoreType.DMA((8,)), pltpu.SemaphoreType.DMA((PARTS, 1))],
        compiler_params=pltpu.CompilerParams(vmem_limit_bytes=4 * MIB),
        cost_estimate=pl.CostEstimate(flops=5 * state.size, bytes_accessed=2 * state.size * 4, transcendentals=0),
    )(state, speed, fresh, remapped)[0]


def pick_kernel(place, own, first, second, out, table, lines):
    for k, part in enumerate((own, first, second)):
        table[k * 3 * CAP : (k + 1) * 3 * CAP, :] = part[...]
    for b in range(out.shape[0]):
        lines[b : b + 1, :] = table[pl.ds(place[b], 1), :]
    out[...] = lines[...].astype(BF16)


def pick(place, own, first, second):
    n_blocks = place.shape[0]
    return pl.pallas_call(
        pick_kernel,
        name="pick",
        out_shape=jax.ShapeDtypeStruct((n_blocks, BLK), BF16),
        in_specs=[SMEM, VMEM, VMEM, VMEM],
        out_specs=VMEM,
        scratch_shapes=[pltpu.VMEM((9 * CAP, BLK), F32), pltpu.VMEM((n_blocks, BLK), F32)],
        compiler_params=pltpu.CompilerParams(vmem_limit_bytes=2 * MIB),
    )(place, own, first, second)


def per_device(
    elem_volume,
    elem_velocity,
    elem_energy,
    elem_mat,
    elem_dest,
    tile_slot,
    tile_cell,
    tile_weight,
    tile_count,
    cell_state,
    mat_props,
):
    size_x, size_y = lax.axis_size("gx"), lax.axis_size("gy")
    n_blocks = elem_dest.shape[0]
    shape = (n_blocks, BLK)
    own, first, second, place, mat_props, tile_slot, tile_cell = payload(
        elem_dest,
        mat_props,
        elem_volume.reshape(shape),
        elem_velocity,
        elem_energy.reshape(shape),
        elem_mat.reshape(shape),
        tile_slot,
        tile_cell,
        size_y,
    )
    weight = fetch(tile_weight)

    first = swap(first, "gx", 1)
    second = swap(second, "gx", 2)
    weight, own = lax.optimization_barrier((weight, own))
    state, turned, slots, spots, points = stage(
        tile_slot, tile_cell, tile_count, cell_state, weight, size_y
    )

    def along_y(which):
        rows = slice(which * CAP, (which + 1) * CAP)
        return jnp.concatenate([own[rows], first[rows], second[rows]], axis=0)

    south = swap(along_y(1), "gy", 1)
    north = swap(along_y(2), "gy", 2)
    state, *edges = deposit(
        slots, spots, (own, first, second, south, north), weight, state
    )
    edges = (
        swap(edges[0], "gx", 1),
        swap(edges[1], "gx", 2),
        swap(edges[3], "gy", 2),
        swap(edges[2], "gy", 1, wrap=False),
    )
    fresh, press, speed = inner(mat_props, state, cell_state.shape[1])
    remapped, state, speed, fresh, own, first, second = outer(
        mat_props, slots, points, edges, turned, state, speed, press, fresh, size_x, size_y
    )
    remapped = late(state, speed, fresh, remapped)
    first = swap(first, "gy", 1)
    second = swap(second, "gy", 2)

    def along_x(which):
        rows = slice(which * CAP, (which + 1) * CAP)
        return jnp.concatenate([own[rows], first[rows], second[rows]], axis=0)

    back = pick(place, along_x(0), swap(along_x(1), "gx", 1), swap(along_x(2), "gx", 2))
    return remapped, back.reshape(n_blocks * BLK)


def solution(mesh):
    placed = (
        P(("gx", "gy")),
        P(None, ("gx", "gy")),
        P(("gx", "gy")),
        P(("gx", "gy")),
        P(("gx", "gy")),
        P(("gx", "gy")),
        P(("gx", "gy")),
        P(("gx", "gy"), None, None),
        P(("gx", "gy")),
        P(None, "gx", "gy"),
        P(),
    )
    return jax.shard_map(
        per_device,
        mesh=mesh,
        in_specs=placed,
        out_specs=(P(None, "gx", "gy"), P(("gx", "gy"))),
        check_vma=False,
    )
```
